128 devices in a mesh: dp: 16 (over z, x), mp: 8 (over y, core).
Axes of the slice: x: 4, y: 4, z: 4, core: 2. Of those that a mesh axis runs over, the one named last changes fastest.
Arguments:
- gradient: bfloat16 [16, 2560, 10240], P('dp', 'mp')
- error: bfloat16 [16, 2560, 10240], P('dp', 'mp'), may hold values from -3 to 3
- q_start: bfloat16 [64, 10240], replicated, may hold values from -6 to 6
Outputs:
- new_error: bfloat16 [16, 2560, 10240], P('dp', 'mp')
- p_hat: float32 [64, 2560], P(None, 'mp')
- q_new: float32 [64, 10240], replicated
The draws below stay inside these ranges and needn't reach their ends.
All inputs are finite; a program needn't handle non-finite values.
Results may differ from the reference program's by a relative error of at most 0.012.
Values sent between devices are 32-bit elements; how exact they have to be, the bound alone decides.
No kernel may reach another device: no remote copies, remote signals or barrier semaphores. Data moves between devices by JAX's collectives and lax.ppermute only.
A program may use at most 64 MiB of HBM per device.

```python
import math
import jax
import jax.numpy as jnp
from jax import lax

D = 2560
FF = 10240
R = 64
REPLICAS = 16


def draw_gradient(key, part):
    key = jax.random.fold_in(key, 11)
    key_rows, key_cols, key_noise = jax.random.split(key, 3)
    low = math.log(0.3)
    high = math.log(3.0)
    row_scale = jnp.exp(jax.random.uniform(key_rows, (REPLICAS, D, 1), jnp.float32, low, high))
    col_scale = jnp.exp(jax.random.uniform(key_cols, (1, 1, FF), jnp.float32, low, high))
    base = jax.random.normal(key_noise, (REPLICAS, D, FF), jnp.float32)
    return (base * row_scale * col_scale).astype(jnp.bfloat16)


def level_of(key, extent, cuts, smallest, high):
    def one(position, parts):
        steps = jax.random.uniform(jax.random.fold_in(jax.random.fold_in(key, 6), position), (parts,), jnp.float32, smallest / len(cuts), high / len(cuts))
        return jnp.repeat(jnp.exp(steps), extent[position] // parts).reshape((-1,) + (1,) * (len(extent) - position - 1))

    loudness = one(*cuts[0])
    for cut in cuts[1:]:
        loudness = loudness * one(*cut)
    return loudness


def scatter_about(stream_key, extent, spread, reach, cuts=(), dtype=jnp.bfloat16):
    array = jax.random.normal(stream_key, extent, jnp.float32) * spread
    if len(cuts) > 0:
        array = level_of(stream_key, extent, cuts, -0.22, 0.18) * array
    return jnp.clip(array, min=-reach, max=reach).astype(dtype)


def setup_inputs(seed: int = 0) -> dict:
    splits = jax.random.split(jax.random.key(seed), 4)
    return {
        "gradient": draw_gradient(jax.random.fold_in(splits[3], 71), 0),
        "error": scatter_about(splits[1], (REPLICAS, D, FF), 0.5, 3.0, ((0, 16), (1, 8))),
        "q_start": scatter_about(splits[2], (R, FF), 1.0, 6.0),
    }


def reference(gradient, error, q_start):

    def merge_one(pair):
        return (pair[0].astype(jnp.float32) + pair[1].astype(jnp.float32)).astype(jnp.bfloat16)
    merged = lax.map(merge_one, (gradient, error))

    def left_term(block):
        return lax.dot_general(q_start.astype(jnp.float32), block.astype(jnp.float32), (((1,), (1,)), ((), ())), preferred_element_type=jnp.float32)
    p_mean = jnp.sum(lax.map(left_term, merged), axis=0) / REPLICAS
    gram = jnp.dot(p_mean, p_mean.T, precision=lax.Precision.HIGHEST)
    lower = jnp.linalg.cholesky(gram)
    p_hat = lax.linalg.triangular_solve(lower, p_mean, left_side=True, lower=True)
    p_low = p_hat.astype(jnp.bfloat16)

    def right_term(block):
        return jnp.dot(p_low.astype(jnp.float32), block.astype(jnp.float32), preferred_element_type=jnp.float32)
    q_new = jnp.sum(lax.map(right_term, merged), axis=0) / REPLICAS
    q_low = q_new.astype(jnp.bfloat16)

    def residual_one(block):
        decoded = lax.dot_general(p_low.astype(jnp.float32), q_low.astype(jnp.float32), (((0,), (0,)), ((), ())), preferred_element_type=jnp.float32)
        return (block.astype(jnp.float32) - decoded).astype(jnp.bfloat16)
    new_error = lax.map(residual_one, merged)
    return (new_error, p_hat, q_new)
```

```python
import jax
import jax.numpy as jnp
from jax import lax
from jax.sharding import Mesh, PartitionSpec as P

DP = ("z", "x")
HIGHEST = lax.Precision.HIGHEST


def shifts(value, axis):
    n = lax.axis_size(axis)
    return [
        lax.ppermute(value, axis, [(i, (i + k) % n) for i in range(n)]) for k in range(1, n)
    ]


def swap(value):
    return lax.ppermute(value, "c", [(0, 1), (1, 0)])


def body(gradient, error, q_start):
    merged = (gradient[0].astype(jnp.float32) + error[0].astype(jnp.float32)).astype(jnp.bfloat16)
    rank, columns = q_start.shape
    replicas = lax.axis_size(DP)
    half = columns // 2
    core = lax.axis_index("c")
    rows = 8
    groups = rank // rows
    cuts = replicas // groups

    p = lax.dot_general(
        q_start, merged, (((1,), (1,)), ((), ())), preferred_element_type=jnp.float32
    )
    p = p + sum(shifts(p, "x"))
    p = (p + sum(shifts(p, "z"))) / replicas

    peak = jnp.max(jnp.abs(p))
    peak = jnp.where(peak > 0, peak, 1.0)
    own_gram = jnp.dot(p, p.T, precision=HIGHEST)
    packed = jnp.concatenate([own_gram, jnp.full_like(own_gram, peak)], axis=1)
    other = swap(packed)
    other_peak = other[0, rank]
    pair_peak = jnp.maximum(peak, other_peak)
    packed = jnp.concatenate(
        [own_gram + other[:, :rank], jnp.full_like(own_gram, pair_peak)], axis=1
    )
    across = shifts(packed, "y")
    gram = packed[:, :rank] + sum(a[:, :rank] for a in across)
    peaks = [a[0, rank] for a in across]
    top = pair_peak
    for a in peaks:
        top = jnp.maximum(top, a)
    lower = jnp.linalg.cholesky(gram)
    inverse = lax.linalg.triangular_solve(
        lower, jnp.eye(rank, dtype=jnp.float32), left_side=True, lower=True
    )
    p_hat = jnp.dot(inverse, p, precision=HIGHEST)

    scaled = p / peak
    sent = lax.dynamic_slice_in_dim(merged, (1 - core) * half, half, axis=1)
    kept = lax.dynamic_slice_in_dim(merged, core * half, half, axis=1)
    right_sent = jnp.dot(scaled, sent.astype(jnp.float32), precision=HIGHEST)
    received = swap(right_sent)
    right_kept = jnp.dot(scaled, kept.astype(jnp.float32), precision=HIGHEST)
    right = right_kept * (peak / pair_peak) + received * (other_peak / pair_peak)
    right = right.reshape(groups, rows, cuts, half // cuts).transpose(0, 2, 1, 3)
    right = lax.all_to_all(right.reshape(replicas, rows, half // cuts), DP, 0, 0)
    right = jnp.sum(right, axis=0)
    total = right * (pair_peak / top)
    for a, b in zip(shifts(right, "y"), peaks):
        total = total + a * (b / top)
    total = lax.all_to_all(jnp.broadcast_to(total[None], (replicas,) + total.shape), DP, 0, 0)
    mine = total.reshape(groups, cuts, rows, half // cuts).transpose(0, 2, 1, 3).reshape(rank, half)
    theirs = swap(mine)
    solve = inverse * (top / replicas)
    q_mine = jnp.dot(solve, mine, precision=HIGHEST)
    q_theirs = jnp.dot(solve, theirs, precision=HIGHEST)
    q_new = jnp.where(
        core == 0,
        jnp.concatenate([q_mine, q_theirs], axis=1),
        jnp.concatenate([q_theirs, q_mine], axis=1),
    )
    decoded = lax.dot_general(
        p_hat.astype(jnp.bfloat16),
        q_new.astype(jnp.bfloat16),
        (((0,), (0,)), ((), ())),
        preferred_element_type=jnp.float32,
    )
    new_error = (merged.astype(jnp.float32) - decoded).astype(jnp.bfloat16)
    return (new_error[None], p_hat, q_new)


def solution(mesh):
    fine = Mesh(mesh.devices.reshape(4, 4, 4, 2), ("z", "x", "y", "c"))
    return jax.shard_map(
        body,
        mesh=fine,
        in_specs=(P(DP, ("y", "c"), None), P(DP, ("y", "c"), None), P()),
        out_specs=(P(DP, ("y", "c"), None), P(None, ("y", "c")), P()),
        check_vma=False,
    )
```

```python
import functools

import jax
import jax.numpy as jnp
from jax import lax
from jax.experimental import pallas as pl
from jax.experimental.pallas import tpu as pltpu
from jax.sharding import Mesh, PartitionSpec as P

DP = ("z", "x")
AXES = ("z", "x", "y", "c")
SIZES = (4, 4, 4, 2)
HIGHEST = lax.Precision.HIGHEST
F32 = jnp.float32
BF16 = jnp.bfloat16
MIB = 1 << 20
ROWS = 8
ANY = pl.BlockSpec(memory_space=pl.ANY)
WHOLE = pl.BlockSpec(memory_space=pltpu.VMEM)
SCALAR = pl.BlockSpec(memory_space=pltpu.SMEM)


def params(mib):
    return pltpu.CompilerParams(vmem_limit_bytes=mib * MIB)


def cost(flops, nbytes):
    return pl.CostEstimate(flops=flops, bytes_accessed=nbytes, transcendentals=0)


def index(z, x, y, c):
    return ((z * SIZES[1] + x) * SIZES[2] + y) * SIZES[3] + c


def everyone():
    return [
        (z, x, y, c)
        for z in range(SIZES[0])
        for x in range(SIZES[1])
        for y in range(SIZES[2])
        for c in range(SIZES[3])
    ]


def ring_x_or_z(value, phase):
    out = []
    for k in (1, 3, 2):
        pairs = []
        for z, x, y, c in everyone():
            to = (z, (x + k) % SIZES[1], y, c) if c == phase else ((z + k) % SIZES[0], x, y, c)
            pairs.append((index(z, x, y, c), index(*to)))
        out.append(lax.ppermute(value, AXES, pairs))
    return out


def ring_y(value):
    n = SIZES[2]
    return [lax.ppermute(value, "y", [(i, (i + k) % n) for i in range(n)]) for k in (1, 3, 2)]


def swap(value):
    return lax.ppermute(value, "c", [(0, 1), (1, 0)])


def merge_kernel(width, g_ref, e_ref, q_ref, m_ref, p_ref, acc):
    rows, columns = g_ref.shape
    rank = q_ref.shape[0]
    acc[...] = jnp.zeros_like(acc)

    def step(g, e, q):
        at = pl.multiple_of(pl.program_id(0) * width, width)
        m = (g[...].astype(F32) + e[...].astype(F32)).astype(BF16)
        m_ref[:, pl.ds(at, width)] = m
        acc[...] += lax.dot_general(
            m, q[...], (((1,), (1,)), ((), ())), preferred_element_type=F32
        )

    def spec(n):
        return pl.BlockSpec((n, width), lambda i: (0, i))

    pltpu.emit_pipeline(
        step, grid=(columns // width,), in_specs=[spec(rows), spec(rows), spec(rank)]
    )(g_ref, e_ref, q_ref)
    p_ref[...] = acc[...].T


def merge(gradient, error, q_start):
    rows, columns = gradient.shape
    rank = q_start.shape[0]
    gradient, error, q_start = (
        pltpu.with_memory_space_constraint(a, pltpu.HBM) for a in (gradient, error, q_start)
    )
    return pl.pallas_call(
        functools.partial(merge_kernel, 1024),
        out_shape=[pltpu.VMEM((rows, columns), BF16), pltpu.VMEM((rank, rows), F32)],
        in_specs=[ANY, ANY, ANY],
        out_specs=[WHOLE, WHOLE],
        scratch_shapes=[pltpu.VMEM((rows, rank), F32)],
        compiler_params=params(20),
        cost_estimate=cost(2 * rank * rows * columns, 4 * rows * columns),
        name="merge",
    )(gradient, error, q_start)


def right_tiles(half, pieces, m_ref, out_ref, width):
    rank = pieces.shape[0] // 3
    cut = out_ref.shape[2]
    steps = cut // width
    cuts = m_ref.shape[1] // 2 // cut

    def step(i, carry):
        j, k = i // steps, i % steps
        at = pl.multiple_of(half * (cuts * cut) + i * width, width)
        t = jnp.dot(pieces, m_ref[:, pl.ds(at, width)], preferred_element_type=F32)
        t = t[:rank] + (t[rank : 2 * rank] + t[2 * rank :])
        to = pl.ds(pl.multiple_of(k * width, width), width)
        for g in range(rank // ROWS):
            out_ref[g * cuts + j, :, to] = t[g * ROWS : (g + 1) * ROWS]
        return carry

    lax.fori_loop(0, cuts * steps, step, 0)


def first_right_kernel(replicas, half_ref, a_ref, b_ref, c_ref, d_ref, m_ref, out_ref, ext_ref, p_ref, pieces_ref):
    p = (a_ref[...] + b_ref[...] + (c_ref[...] + d_ref[...])) * (1.0 / replicas)
    p_ref[...] = p
    rank = p.shape[0]
    peak = jnp.max(jnp.abs(p), axis=(0, 1), keepdims=True)
    peak = jnp.where(peak > 0, peak, 1.0)
    gram = lax.dot_general(
        p, p, (((1,), (1,)), ((), ())), precision=HIGHEST, preferred_element_type=F32
    )
    ext = jnp.concatenate(
        [gram[g * ROWS : (g + 1) * ROWS] for g in range(rank // ROWS)]
        + [jnp.broadcast_to(peak, (ROWS, 128))],
        axis=1,
    )
    ext_ref[...] = ext
    out_ref[out_ref.shape[0] - 1, :, : ext.shape[1]] = ext
    n = p / peak
    high = n.astype(BF16)
    n = n - high.astype(F32)
    middle = n.astype(BF16)
    low = (n - middle.astype(F32)).astype(BF16)
    pieces = jnp.concatenate([high, middle, low], axis=0)
    pieces_ref[...] = pieces
    right_tiles(half_ref[0], pieces, m_ref, out_ref, 512)


def second_right_kernel(half_ref, pieces_ref, m_ref, out_ref):
    right_tiles(half_ref[0], pieces_ref[...], m_ref, out_ref, 512)


def first_right(half, parts, merged, replicas, cut):
    rank, rows = parts[0].shape
    width = rank * ROWS + 128
    return pl.pallas_call(
        functools.partial(first_right_kernel, replicas),
        out_shape=[
            jax.ShapeDtypeStruct((replicas + 1, ROWS, cut), F32),
            pltpu.VMEM((ROWS, width), F32),
            pltpu.VMEM((rank, rows), F32),
            pltpu.VMEM((3 * rank, rows), BF16),
        ],
        in_specs=[SCALAR] + [WHOLE] * 5,
        out_specs=[WHOLE] * 4,
        compiler_params=params(12),
        cost_estimate=cost(3 * rank * rows * cut * replicas // ROWS, 4 * rank * cut * 2),
        name="first_right",
    )(half, *parts, merged)


def second_right(half, pieces, merged, replicas, cut):
    return pl.pallas_call(
        second_right_kernel,
        out_shape=pltpu.VMEM((replicas, ROWS, cut), F32),
        in_specs=[SCALAR, WHOLE, WHOLE],
        out_specs=WHOLE,
        compiler_params=params(12),
        cost_estimate=cost(pieces.shape[0] * pieces.shape[1] * cut * 4, replicas * ROWS * cut * 4),
        name="second_right",
    )(half, pieces, merged)


def pair_kernel(kept_ref, got_ref, ext_ref, out_ref, pair_ref):
    width = ext_ref.shape[1]
    last = got_ref.shape[0] - 1
    mine, other = ext_ref[...], got_ref[last, :, :width]
    own, its = mine[:1, width - 1 :], other[:1, width - 1 :]
    top = jnp.maximum(own, its)
    lane = lax.broadcasted_iota(jnp.int32, mine.shape, 1)
    pair_ref[...] = jnp.where(lane < width - 128, mine + other, top)
    for i in range(last):
        out_ref[i] = kept_ref[i] * (own / top) + got_ref[i] * (its / top)


def pair(kept, got, ext):
    return pl.pallas_call(
        pair_kernel,
        out_shape=[jax.ShapeDtypeStruct(kept.shape, F32), pltpu.VMEM(ext.shape, F32)],
        in_specs=[WHOLE] * 3,
        out_specs=[WHOLE] * 2,
        compiler_params=params(8),
        name="pair",
    )(kept, got, ext)


def gather_kernel(parts_ref, ext_ref, out_ref):
    total = parts_ref[0]
    for i in range(1, parts_ref.shape[0]):
        total = total + parts_ref[i]
    cut = total.shape[1]
    out_ref[:, :cut] = total
    out_ref[:, cut:] = ext_ref[...]


def add_parts(parts, ext):
    n, rows, cut = parts.shape
    return pl.pallas_call(
        gather_kernel,
        out_shape=jax.ShapeDtypeStruct((rows, cut + ext.shape[1]), F32),
        in_specs=[WHOLE] * 2,
        out_specs=WHOLE,
        compiler_params=params(8),
        name="add_parts",
    )(parts, ext)


def across_kernel(a_ref, b_ref, c_ref, d_ref, out_ref, ext_ref):
    copies, _, cut = out_ref.shape
    width = ext_ref.shape[1]
    refs = (a_ref, b_ref, c_ref, d_ref)
    peaks = [r[:1, cut + width - 1 :] for r in refs]
    top = jnp.maximum(jnp.maximum(peaks[0], peaks[1]), jnp.maximum(peaks[2], peaks[3]))
    total = sum(r[:, :cut] * (k / top) for r, k in zip(refs, peaks))
    for i in range(copies):
        out_ref[i] = total
    ext = (a_ref[:, cut:] + b_ref[:, cut:]) + (c_ref[:, cut:] + d_ref[:, cut:])
    lane = lax.broadcasted_iota(jnp.int32, ext.shape, 1)
    ext_ref[...] = jnp.where(lane < width - 128, ext, top)


def across(parts, replicas, cut):
    rows, width = parts[0].shape
    return pl.pallas_call(
        across_kernel,
        out_shape=[
            jax.ShapeDtypeStruct((replicas, rows, cut), F32),
            pltpu.VMEM((rows, width - cut), F32),
        ],
        in_specs=[WHOLE] * 4,
        out_specs=[WHOLE] * 2,
        compiler_params=params(8),
        name="across",
    )(*parts)


def result_kernel(width, half_ref, t_ref, m_ref, solve_ref, p_ref, *refs):
    error_ref, q_ref = refs[-2:]
    rank = solve_ref.shape[0]
    groups = rank // ROWS
    cut = t_ref.shape[2]
    cuts = t_ref.shape[0] // groups
    steps = cuts * (cut // width)
    base = half_ref[0] * steps
    left = p_ref[...].T.astype(BF16)
    solve = solve_ref[...]

    def step(e, q):
        i = pl.program_id(0)
        j, k = i // (cut // width), i % (cut // width)
        at = pl.ds(pl.multiple_of(k * width, width), width)
        t = jnp.concatenate([t_ref[g * cuts + j, :, at] for g in range(groups)], axis=0)
        new = jnp.dot(solve, t, precision=HIGHEST, preferred_element_type=F32)
        q[...] = new
        decoded = jnp.dot(left, new.astype(BF16), preferred_element_type=F32)
        m = m_ref[:, pl.ds(pl.multiple_of((base + i) * width, width), width)]
        e[...] = (m.astype(F32) - decoded).astype(BF16)

    pltpu.emit_pipeline(
        step,
        grid=(steps,),
        out_specs=[
            pl.BlockSpec((m_ref.shape[0], width), lambda i: (0, base + i)),
            pl.BlockSpec((rank, width), lambda i: (0, base + i)),
        ],
    )(error_ref, q_ref)


def result(half, totals, merged, solve, p_hat, before):
    rank = solve.shape[0]
    rows, columns = merged.shape
    held = [] if before is None else list(before)
    return pl.pallas_call(
        functools.partial(result_kernel, 1280),
        out_shape=[pltpu.HBM((rows, columns), BF16), pltpu.HBM((rank, columns), F32)],
        in_specs=[SCALAR] + [WHOLE] * 4 + [ANY] * len(held),
        out_specs=[ANY, ANY],
        input_output_aliases={5 + i: i for i in range(len(held))},
        compiler_params=params(16),
        cost_estimate=cost(rank * rows * columns, rows * columns + 2 * rank * columns),
        name="result",
    )(half, totals, merged, solve, p_hat, *held)


def body(gradient, error, q_start):
    rank, columns = q_start.shape
    replicas = SIZES[0] * SIZES[1]
    cut = columns * rank // (2 * replicas * ROWS)
    core = lax.axis_index("c").reshape(1)

    merged, p = merge(gradient[0], error[0], q_start)
    a, b, c = ring_x_or_z(p, 0)
    p = (p + a) + (b + c)
    sent, ext, p_mean, pieces = first_right(
        1 - core, (p, *ring_x_or_z(p, 1)), merged, replicas, cut
    )
    got = swap(sent)
    kept = second_right(core, pieces, merged, replicas, cut)
    parts, ext = pair(kept, got, ext)
    parts = lax.all_to_all(parts, DP, 0, 0)
    parts = add_parts(parts, ext)
    totals, ext = across((parts, *ring_y(parts)), replicas, cut)
    totals = lax.all_to_all(totals, DP, 0, 0)

    gram = ext[:, : rank * ROWS].reshape(ROWS, rank // ROWS, rank)
    gram = gram.transpose(1, 0, 2).reshape(rank, rank)
    lower = jnp.linalg.cholesky(gram)
    inverse = lax.linalg.triangular_solve(
        lower, jnp.eye(rank, dtype=F32), left_side=True, lower=True
    )
    p_hat = jnp.dot(inverse, p_mean, precision=HIGHEST)
    solve = inverse * (ext[:1, rank * ROWS : rank * ROWS + 1] / replicas)

    others = swap(totals)
    first = result(core, totals, merged, solve, p_hat, None)
    new_error, q_new = result(1 - core, others, merged, solve, p_hat, first)
    return (new_error[None], p_hat, q_new)


def solution(mesh):
    fine = Mesh(mesh.devices.reshape(SIZES), AXES)
    return jax.shard_map(
        body,
        mesh=fine,
        in_specs=(P(DP, ("y", "c"), None), P(DP, ("y", "c"), None), P()),
        out_specs=(P(DP, ("y", "c"), None), P(None, ("y", "c")), P()),
        check_vma=False,
    )
```

```python
import functools

import jax
import jax.numpy as jnp
from jax import lax
from jax.experimental import pallas as pl
from jax.experimental.pallas import tpu as pltpu
from jax.sharding import Mesh, PartitionSpec as P

DP = ("z", "x")
AXES = ("z", "x", "y", "c")
SIZES = (4, 4, 4, 2)
HIGHEST = lax.Precision.HIGHEST
F32 = jnp.float32
BF16 = jnp.bfloat16
MIB = 1 << 20
ROWS = 8
ANY = pl.BlockSpec(memory_space=pl.ANY)
WHOLE = pl.BlockSpec(memory_space=pltpu.VMEM)
SCALAR = pl.BlockSpec(memory_space=pltpu.SMEM)


def params(mib):
    return pltpu.CompilerParams(vmem_limit_bytes=mib * MIB)


def cost(flops, nbytes):
    return pl.CostEstimate(flops=flops, bytes_accessed=nbytes, transcendentals=0)


def index(z, x, y, c):
    return ((z * SIZES[1] + x) * SIZES[2] + y) * SIZES[3] + c


def everyone():
    return [
        (z, x, y, c)
        for z in range(SIZES[0])
        for x in range(SIZES[1])
        for y in range(SIZES[2])
        for c in range(SIZES[3])
    ]


def ring_x_or_z(value, phase):
    out = []
    for k in (1, 3, 2):
        pairs = []
        for z, x, y, c in everyone():
            to = (z, (x + k) % SIZES[1], y, c) if c == phase else ((z + k) % SIZES[0], x, y, c)
            pairs.append((index(z, x, y, c), index(*to)))
        out.append(lax.ppermute(value, AXES, pairs))
    return out


def ring_y(value):
    n = SIZES[2]
    return [lax.ppermute(value, "y", [(i, (i + k) % n) for i in range(n)]) for k in (1, 3, 2)]


def swap(value):
    return lax.ppermute(value, "c", [(0, 1), (1, 0)])


def merge_kernel(width, core_ref, g_hbm, e_hbm, q_hbm, m_ref, p_ref, g_ref, e_ref, q_ref, sems):
    rows, columns = g_ref.shape
    rank = q_ref.shape[0]
    steps = columns // width
    del core_ref

    def copies(i):
        at = pl.ds(i * width, width)
        return [
            pltpu.make_async_copy(src.at[:, at], dst.at[:, at], sems.at[n, i])
            for n, (src, dst) in enumerate(((g_hbm, g_ref), (e_hbm, e_ref), (q_hbm, q_ref)))
        ]

    for i in range(steps):
        for c in copies(i):
            c.start()
    acc = jnp.zeros((rows, rank), F32)
    for i in range(steps):
        for c in copies(i):
            c.wait()
        at = pl.ds(i * width, width)
        m = (g_ref[:, at].astype(F32) + e_ref[:, at].astype(F32)).astype(BF16)
        m_ref[:, at] = m
        acc = acc + lax.dot_general(
            m, q_ref[:, at], (((1,), (1,)), ((), ())), preferred_element_type=F32
        )
    p_ref[...] = pack(acc.T)


def pack(p):
    rank, rows = p.shape
    full = rows // 128
    half = rank // 2
    parts = [p[:, i * 128 : (i + 1) * 128] for i in range(full)]
    rest = p[:, full * 128 :]
    return jnp.concatenate(parts + [jnp.concatenate([rest[:half], rest[half:]], axis=1)], axis=0)


def unpack(packed, rank):
    full = packed.shape[0] // rank
    last = packed[full * rank :]
    rest = jnp.concatenate([last[:, :64], last[:, 64:]], axis=0)
    return jnp.concatenate(
        [packed[i * rank : (i + 1) * rank] for i in range(full)] + [rest], axis=1
    )


def merge(core, gradient, error, q_start):
    rows, columns = gradient.shape
    rank = q_start.shape[0]
    width = 1024
    gradient, error, q_start = (
        pltpu.with_memory_space_constraint(a, pltpu.HBM) for a in (gradient, error, q_start)
    )
    return pl.pallas_call(
        functools.partial(merge_kernel, width),
        out_shape=[pltpu.VMEM((rows, columns), BF16), pltpu.VMEM((rank * rows // 128, 128), F32)],
        in_specs=[SCALAR, ANY, ANY, ANY],
        out_specs=[WHOLE, WHOLE],
        scratch_shapes=[
            pltpu.VMEM((rows, columns), BF16),
            pltpu.VMEM((rows, columns), BF16),
            pltpu.VMEM((rank, columns), BF16),
            pltpu.SemaphoreType.DMA((3, columns // width)),
        ],
        compiler_params=params(24),
        cost_estimate=cost(2 * rank * rows * columns, 4 * rows * columns),
        name="merge",
    )(core, gradient, error, q_start)


def right_tiles(half, pieces, m_ref, out_ref, width):
    rank = pieces.shape[0] // 3
    groups = rank // ROWS
    tiles = width // 128
    cut = out_ref.shape[1] // ROWS * 128
    steps = cut // width
    cuts = m_ref.shape[1] // 2 // cut

    def step(i, carry):
        j, k = i // steps, i % steps
        at = pl.multiple_of(half * (cuts * cut) + i * width, width)
        t = jnp.dot(pieces, m_ref[:, pl.ds(at, width)], preferred_element_type=F32)
        t = t[:rank] + (t[rank : 2 * rank] + t[2 * rank :])
        for g in range(groups):
            for n in range(tiles):
                to = pl.ds(pl.multiple_of((k * tiles + n) * ROWS, ROWS), ROWS)
                out_ref[g * cuts + j, to, :] = t[g * ROWS : (g + 1) * ROWS, n * 128 : (n + 1) * 128]
        return carry

    lax.fori_loop(0, cuts * steps, step, 0)


def split(n):
    high = n.astype(BF16)
    n = n - high.astype(F32)
    middle = n.astype(BF16)
    return high, middle, (n - middle.astype(F32)).astype(BF16)


def first_right_kernel(replicas, rank, core_ref, a_ref, b_ref, c_ref, d_ref, m_ref, out_ref, ext_ref, p_ref, pieces_ref):
    p = (a_ref[...] + b_ref[...] + (c_ref[...] + d_ref[...])) * (1.0 / replicas)
    peak = jnp.max(jnp.abs(p), axis=(0, 1), keepdims=True)
    peak = jnp.where(peak > 0, peak, 1.0)
    p = unpack(p, rank)
    p_ref[...] = p
    gram = lax.dot_general(
        p, p, (((1,), (1,)), ((), ())), precision=HIGHEST, preferred_element_type=F32
    )
    two = 2 * ROWS
    ext = jnp.concatenate(
        [
            jnp.concatenate([gram[i : i + ROWS], gram[i + ROWS : i + two]], axis=1)
            for i in range(0, rank, two)
        ]
        + [jnp.broadcast_to(peak, (ROWS, 128))],
        axis=0,
    )
    ext_ref[...] = ext
    out_ref[out_ref.shape[0] - 1, : ext.shape[0], :] = ext
    pieces = jnp.concatenate(split(p / peak), axis=0)
    pieces_ref[...] = pieces
    right_tiles(1 - core_ref[0], pieces, m_ref, out_ref, 512)


def second_right_kernel(core_ref, pieces_ref, m_ref, out_ref):
    right_tiles(core_ref[0], pieces_ref[...], m_ref, out_ref, 512)


def first_right(core, parts, merged, rank, replicas, size):
    rows = merged.shape[0]
    return pl.pallas_call(
        functools.partial(first_right_kernel, replicas, rank),
        out_shape=[
            jax.ShapeDtypeStruct((replicas + 1, size, 128), F32),
            pltpu.VMEM((rank * rank // 128 + ROWS, 128), F32),
            pltpu.VMEM((rank, rows), F32),
            pltpu.VMEM((3 * rank, rows), BF16),
        ],
        in_specs=[SCALAR] + [WHOLE] * 5,
        out_specs=[WHOLE] * 4,
        compiler_params=params(12),
        cost_estimate=cost(6 * rows * replicas * size * 128, 8 * replicas * size * 128),
        name="first_right",
    )(core, *parts, merged)


def second_right(core, pieces, merged, replicas, size):
    return pl.pallas_call(
        second_right_kernel,
        out_shape=pltpu.VMEM((replicas, size, 128), F32),
        in_specs=[SCALAR, WHOLE, WHOLE],
        out_specs=WHOLE,
        compiler_params=params(12),
        cost_estimate=cost(6 * pieces.shape[1] * replicas * size * 128, 8 * replicas * size * 128),
        name="second_right",
    )(core, pieces, merged)


def pair_kernel(kept_ref, got_ref, ext_ref, out_ref, pair_ref):
    grams = ext_ref.shape[0] - ROWS
    last = got_ref.shape[0] - 1
    own, its = ext_ref[grams : grams + 1, :1], got_ref[last, grams : grams + 1, :1]
    top = jnp.maximum(own, its)
    pair_ref[:grams] = ext_ref[:grams] + got_ref[last, :grams]
    pair_ref[grams:] = jnp.broadcast_to(top, (ROWS, 128))
    own, its = own / top, its / top
    for i in range(last):
        out_ref[i] = kept_ref[i] * own + got_ref[i] * its


def pair(kept, got, ext):
    return pl.pallas_call(
        pair_kernel,
        out_shape=[jax.ShapeDtypeStruct(kept.shape, F32), pltpu.VMEM(ext.shape, F32)],
        in_specs=[WHOLE] * 3,
        out_specs=[WHOLE] * 2,
        compiler_params=params(8),
        name="pair",
    )(kept, got, ext)


def add_parts_kernel(parts_ref, ext_ref, out_ref):
    total = parts_ref[0]
    for i in range(1, parts_ref.shape[0]):
        total = total + parts_ref[i]
    out_ref[: total.shape[0]] = total
    out_ref[total.shape[0] :] = ext_ref[...]


def add_parts(parts, ext):
    _, size, lanes = parts.shape
    return pl.pallas_call(
        add_parts_kernel,
        out_shape=jax.ShapeDtypeStruct((size + ext.shape[0], lanes), F32),
        in_specs=[WHOLE] * 2,
        out_specs=WHOLE,
        compiler_params=params(8),
        name="add_parts",
    )(parts, ext)


def across_kernel(a_ref, b_ref, c_ref, d_ref, out_ref, ext_ref):
    copies, size, _ = out_ref.shape
    grams = ext_ref.shape[0] - ROWS
    refs = (a_ref, b_ref, c_ref, d_ref)
    peaks = [r[size + grams : size + grams + 1, :1] for r in refs]
    top = jnp.maximum(jnp.maximum(peaks[0], peaks[1]), jnp.maximum(peaks[2], peaks[3]))
    weights = [k / top for k in peaks]
    for n in range(0, size, ROWS):
        at = slice(n, n + ROWS)
        total = (a_ref[at] * weights[0] + b_ref[at] * weights[1]) + (
            c_ref[at] * weights[2] + d_ref[at] * weights[3]
        )
        for i in range(copies):
            out_ref[i, at, :] = total
    at = slice(size, size + grams)
    ext_ref[:grams] = (a_ref[at] + b_ref[at]) + (c_ref[at] + d_ref[at])
    ext_ref[grams:] = jnp.broadcast_to(top, (ROWS, 128))


def across(parts, replicas, size):
    rows, lanes = parts[0].shape
    return pl.pallas_call(
        across_kernel,
        out_shape=[
            jax.ShapeDtypeStruct((replicas, size, lanes), F32),
            pltpu.VMEM((rows - size, lanes), F32),
        ],
        in_specs=[WHOLE] * 4,
        out_specs=[WHOLE] * 2,
        compiler_params=params(8),
        name="across",
    )(*parts)


def factor_kernel(replicas, ext_ref, p_ref, solve_ref, hat_ref):
    rank = p_ref.shape[0]
    groups = rank // ROWS
    sub = lax.broadcasted_iota(jnp.int32, (ROWS, 2 * rank), 0)
    lane = lax.broadcasted_iota(jnp.int32, (ROWS, 2 * rank), 1)
    blocks = []
    for g in range(groups):
        tile = ext_ref[g // 2 * ROWS : (g // 2 + 1) * ROWS, (g % 2) * rank : (g % 2 + 1) * rank]
        unit = jnp.where(lane[:, :rank] == sub[:, :rank] + g * ROWS, 1.0, 0.0)
        blocks.append(jnp.concatenate([tile, unit], axis=1))
    for j in range(rank):
        own, at = j // ROWS, j % ROWS
        row = blocks[own][at : at + 1]
        row = row / row[:, j : j + 1]
        for g in range(own, groups):
            column = blocks[g][:, j : j + 1]
            if g == own:
                column = jnp.where(sub[:, :1] > at, column, 0.0)
            blocks[g] = blocks[g] - column * row
    inverse = []
    for g in range(groups):
        diagonal = jnp.sum(
            jnp.where(lane == sub + g * ROWS, blocks[g], 0.0), axis=1, keepdims=True
        )
        inverse.append(blocks[g][:, rank:] / jnp.sqrt(diagonal))
    inverse = jnp.concatenate(inverse, axis=0)
    grams = ext_ref.shape[0] - ROWS
    solve_ref[...] = inverse * (ext_ref[grams : grams + 1, :1] * (1.0 / replicas))
    hat_ref[...] = jnp.dot(inverse, p_ref[...], precision=HIGHEST, preferred_element_type=F32)


def factor(ext, p_mean, replicas):
    rank, rows = p_mean.shape
    return pl.pallas_call(
        functools.partial(factor_kernel, replicas),
        out_shape=[
            jax.ShapeDtypeStruct((rank, rank), F32),
            jax.ShapeDtypeStruct((rank, rows), F32),
        ],
        in_specs=[WHOLE] * 2,
        out_specs=[WHOLE] * 2,
        compiler_params=params(8),
        cost_estimate=cost(1 << 32, 1 << 20),
        name="factor",
    )(ext, p_mean)


def result_kernel(own, width, core_ref, t_ref, m_ref, solve_ref, p_ref, *refs):
    error_hbm, q_hbm, error_ref, q_ref, sems = refs[-5:]
    rank = solve_ref.shape[0]
    groups = rank // ROWS
    tiles = width // 128
    cuts = t_ref.shape[0] // groups
    steps = t_ref.shape[1] // ROWS * 128 // width
    half = cuts * steps * width
    base = pl.multiple_of((core_ref[0] if own else 1 - core_ref[0]) * half, half)
    left = p_ref[...].T.astype(BF16)
    s1, s2, s3 = split(solve_ref[...])
    solve = jnp.concatenate([s1, s1, s2, s2, s1, s3], axis=1)

    def out(at, size):
        to = pl.ds(pl.multiple_of(base + at, width), size)
        here = pl.ds(at, size)
        return (
            pltpu.make_async_copy(error_ref.at[:, here], error_hbm.at[:, to], sems.at[0]),
            pltpu.make_async_copy(q_ref.at[:, here], q_hbm.at[:, to], sems.at[1]),
        )

    def step(i, carry):
        j, k = i // steps, i % steps
        t = jnp.concatenate(
            [
                jnp.concatenate(
                    [
                        t_ref[g * cuts + j, pl.ds(pl.multiple_of((k * tiles + n) * ROWS, ROWS), ROWS), :]
                        for n in range(tiles)
                    ],
                    axis=1,
                )
                for g in range(groups)
            ],
            axis=0,
        )
        t1, t2, t3 = split(t)
        t = jnp.concatenate([t1, t2, t1, t2, t3, t1], axis=0)
        new = jnp.dot(solve, t, preferred_element_type=F32)
        at = pl.multiple_of(i * width, width)
        here = pl.ds(at, width)
        q_ref[:, here] = new
        decoded = jnp.dot(left, new.astype(BF16), preferred_element_type=F32)
        m = m_ref[:, pl.ds(pl.multiple_of(base + at, width), width)]
        error_ref[:, here] = (m.astype(F32) - decoded).astype(BF16)
        for c in out(at, width):
            c.start()
        return carry

    lax.fori_loop(0, cuts * steps, step, 0)
    for c in out(0, half):
        c.wait()


def result(core, own, totals, merged, solve, p_hat, before):
    rank = solve.shape[0]
    rows, columns = merged.shape
    held = [] if before is None else list(before)
    return pl.pallas_call(
        functools.partial(result_kernel, own, 512),
        out_shape=[pltpu.HBM((rows, columns), BF16), pltpu.HBM((rank, columns), F32)],
        in_specs=[SCALAR] + [WHOLE] * 4 + [ANY] * len(held),
        out_specs=[ANY, ANY],
        scratch_shapes=[
            pltpu.VMEM((rows, columns // 2), BF16),
            pltpu.VMEM((rank, columns // 2), F32),
            pltpu.SemaphoreType.DMA((2,)),
        ],
        input_output_aliases={5 + i: i for i in range(len(held))},
        compiler_params=params(16),
        cost_estimate=cost(rank * rows * columns, rows * columns + 2 * rank * columns),
        name="result",
    )(core, totals, merged, solve, p_hat, *held)


def tie_kernel(value_ref, after_ref, out_ref):
    del value_ref, after_ref, out_ref


def tie(value, after):
    return pl.pallas_call(
        tie_kernel,
        out_shape=jax.ShapeDtypeStruct(value.shape, value.dtype),
        in_specs=[ANY] * 2,
        out_specs=ANY,
        input_output_aliases={0: 0},
        compiler_params=params(4),
        name="tie",
    )(value, after)


def body(gradient, error, q_start):
    rank, columns = q_start.shape
    replicas = SIZES[0] * SIZES[1]
    size = rank * columns // (2 * replicas * 128)
    core = lax.axis_index("c").reshape(1)

    merged, p = merge(core, gradient[0], error[0], q_start)
    a, b, c = ring_x_or_z(p, 0)
    p = (p + a) + (b + c)
    sent, ext, p_mean, pieces = first_right(
        core, (p, *ring_x_or_z(p, 1)), merged, rank, replicas, size
    )
    got = swap(sent)
    kept = second_right(core, pieces, merged, replicas, size)
    parts, ext = pair(kept, got, ext)
    parts = lax.all_to_all(parts, DP, 0, 0)
    parts = add_parts(parts, ext)
    totals, ext = across((parts, *ring_y(parts)), replicas, size)
    totals = lax.all_to_all(totals, DP, 0, 0)
    solve, p_hat = factor(ext, p_mean, replicas)
    totals = tie(totals, solve)
    others = swap(totals)
    first = result(core, True, totals, merged, solve, p_hat, None)
    new_error, q_new = result(core, False, others, merged, solve, p_hat, first)
    return (new_error[None], p_hat, q_new)


def solution(mesh):
    fine = Mesh(mesh.devices.reshape(SIZES), AXES)
    return jax.shard_map(
        body,
        mesh=fine,
        in_specs=(P(DP, ("y", "c"), None), P(DP, ("y", "c"), None), P()),
        out_specs=(P(DP, ("y", "c"), None), P(None, ("y", "c")), P()),
        check_vma=False,
    )
```

```python
import functools

import jax
import jax.numpy as jnp
from jax import lax
from jax.experimental import pallas as pl
from jax.experimental.pallas import tpu as pltpu
from jax.sharding import Mesh, PartitionSpec as P

DP = ("z", "x")
AXES = ("z", "x", "y", "c")
SIZES = (4, 4, 4, 2)
HIGHEST = lax.Precision.HIGHEST
F32 = jnp.float32
BF16 = jnp.bfloat16
MIB = 1 << 20
ROWS = 8
QUARTERS = 4
SHIFTS = (1, 3, 2)
ANY = pl.BlockSpec(memory_space=pl.ANY)
WHOLE = pl.BlockSpec(memory_space=pltpu.VMEM)
SCALAR = pl.BlockSpec(memory_space=pltpu.SMEM)


def params(mib):
    return pltpu.CompilerParams(vmem_limit_bytes=mib * MIB)


def cost(flops, nbytes):
    return pl.CostEstimate(flops=flops, bytes_accessed=nbytes, transcendentals=0)


def index(z, x, y, c):
    return ((z * SIZES[1] + x) * SIZES[2] + y) * SIZES[3] + c


def everyone():
    return [
        (z, x, y, c)
        for z in range(SIZES[0])
        for x in range(SIZES[1])
        for y in range(SIZES[2])
        for c in range(SIZES[3])
    ]


def ring_x_or_z(values, phase):
    out = []
    for k, value in zip(SHIFTS, values):
        pairs = []
        for z, x, y, c in everyone():
            to = (z, (x + k) % SIZES[1], y, c) if c == phase else ((z + k) % SIZES[0], x, y, c)
            pairs.append((index(z, x, y, c), index(*to)))
        out.append(lax.ppermute(value, AXES, pairs))
    return out


def ring_y(value):
    n = SIZES[2]
    return [lax.ppermute(value, "y", [(i, (i + k) % n) for i in range(n)]) for k in SHIFTS]


def swap(value):
    return lax.ppermute(value, "c", [(0, 1), (1, 0)])


def merge_kernel(width, meta_ref, g_hbm, e_hbm, q_hbm, m_ref, p_ref, g_ref, e_ref, q_ref, sems):
    rows, columns = g_ref.shape
    rank = q_ref.shape[0]
    steps = columns // width
    del meta_ref

    def copies(i):
        at = pl.ds(i * width, width)
        return [
            pltpu.make_async_copy(src.at[:, at], dst.at[:, at], sems.at[n, i])
            for n, (src, dst) in enumerate(((g_hbm, g_ref), (e_hbm, e_ref), (q_hbm, q_ref)))
        ]

    for i in range(steps):
        for c in copies(i):
            c.start()
    acc = jnp.zeros((rows, rank), F32)
    for i in range(steps):
        for c in copies(i):
            c.wait()
        at = pl.ds(i * width, width)
        m = (g_ref[:, at].astype(F32) + e_ref[:, at].astype(F32)).astype(BF16)
        m_ref[:, at] = m
        acc = acc + lax.dot_general(
            m, q_ref[:, at], (((1,), (1,)), ((), ())), preferred_element_type=F32
        )
    p_ref[...] = pack(acc.T)


def pack(p):
    rank, rows = p.shape
    full = rows // 128
    half = rank // 2
    parts = [p[:, i * 128 : (i + 1) * 128] for i in range(full)]
    rest = p[:, full * 128 :]
    return jnp.concatenate(parts + [jnp.concatenate([rest[:half], rest[half:]], axis=1)], axis=0)


def unpack(packed, rank):
    full = packed.shape[0] // rank
    last = packed[full * rank :]
    rest = jnp.concatenate([last[:, :64], last[:, 64:]], axis=0)
    return jnp.concatenate(
        [packed[i * rank : (i + 1) * rank] for i in range(full)] + [rest], axis=1
    )


def merge(meta, gradient, error, q_start):
    rows, columns = gradient.shape
    rank = q_start.shape[0]
    width = 1024
    gradient, error, q_start = (
        pltpu.with_memory_space_constraint(a, pltpu.HBM) for a in (gradient, error, q_start)
    )
    return pl.pallas_call(
        functools.partial(merge_kernel, width),
        out_shape=[pltpu.VMEM((rows, columns), BF16), pltpu.VMEM((rank * rows // 128, 128), F32)],
        in_specs=[SCALAR, ANY, ANY, ANY],
        out_specs=[WHOLE, WHOLE],
        scratch_shapes=[
            pltpu.VMEM((rows, columns), BF16),
            pltpu.VMEM((rows, columns), BF16),
            pltpu.VMEM((rank, columns), BF16),
            pltpu.SemaphoreType.DMA((3, columns // width)),
        ],
        compiler_params=params(24),
        cost_estimate=cost(2 * rank * rows * columns, 4 * rows * columns),
        name="merge",
    )(meta, gradient, error, q_start)


def right_tiles(half, pieces, m_ref, out_ref):
    rank = pieces.shape[0] // 3
    width = m_ref.shape[1] // 2 // QUARTERS
    for a in range(QUARTERS):
        at = pl.multiple_of(half * (QUARTERS * width) + a * width, width)
        t = jnp.dot(pieces, m_ref[:, pl.ds(at, width)], preferred_element_type=F32)
        t = t[:rank] + (t[rank : 2 * rank] + t[2 * rank :])
        to = a * (rank * width // 128)
        for g in range(rank // ROWS):
            for n in range(width // 128):
                out_ref[to : to + ROWS, :] = t[g * ROWS : (g + 1) * ROWS, n * 128 : (n + 1) * 128]
                to += ROWS


def split(n):
    high = n.astype(BF16)
    n = n - high.astype(F32)
    middle = n.astype(BF16)
    return high, middle, (n - middle.astype(F32)).astype(BF16)


def first_right_kernel(replicas, rank, meta_ref, a_ref, b_ref, c_ref, d_ref, m_ref, out_ref, ext_ref, p_ref, pieces_ref):
    p = (a_ref[...] + b_ref[...] + (c_ref[...] + d_ref[...])) * (1.0 / replicas)
    peak = jnp.max(jnp.abs(p), axis=(0, 1), keepdims=True)
    peak = jnp.where(peak > 0, peak, 1.0)
    p = unpack(p, rank)
    p_ref[...] = p
    gram = lax.dot_general(
        p, p, (((1,), (1,)), ((), ())), precision=HIGHEST, preferred_element_type=F32
    )
    two = 2 * ROWS
    ext = jnp.concatenate(
        [
            jnp.concatenate([gram[i : i + ROWS], gram[i + ROWS : i + two]], axis=1)
            for i in range(0, rank, two)
        ]
        + [jnp.broadcast_to(peak, (ROWS, 128))],
        axis=0,
    )
    ext_ref[...] = ext
    out_ref[out_ref.shape[0] - ext.shape[0] :, :] = ext
    pieces = jnp.concatenate(split(p / peak), axis=0)
    pieces_ref[...] = pieces
    right_tiles(1 - meta_ref[0], pieces, m_ref, out_ref)


def second_right_kernel(meta_ref, pieces_ref, m_ref, out_ref):
    right_tiles(meta_ref[0], pieces_ref[...], m_ref, out_ref)


def first_right(meta, parts, merged, rank, replicas):
    rows, columns = merged.shape
    size = rank * columns // 256
    extra = rank * rank // 128 + ROWS
    return pl.pallas_call(
        functools.partial(first_right_kernel, replicas, rank),
        out_shape=[
            jax.ShapeDtypeStruct((size + extra, 128), F32),
            pltpu.VMEM((extra, 128), F32),
            pltpu.VMEM((rank, rows), F32),
            pltpu.VMEM((3 * rank, rows), BF16),
        ],
        in_specs=[SCALAR] + [WHOLE] * 5,
        out_specs=[WHOLE] * 4,
        compiler_params=params(12),
        cost_estimate=cost(3 * rank * rows * columns, 512 * size),
        name="first_right",
    )(meta, *parts, merged)


def second_right(meta, pieces, merged):
    size = pieces.shape[0] // 3 * merged.shape[1] // 256
    return pl.pallas_call(
        second_right_kernel,
        out_shape=pltpu.VMEM((size, 128), F32),
        in_specs=[SCALAR, WHOLE, WHOLE],
        out_specs=WHOLE,
        compiler_params=params(12),
        cost_estimate=cost(pieces.shape[0] * merged.size, 512 * size),
        name="second_right",
    )(meta, pieces, merged)


def pair_kernel(meta_ref, kept_ref, got_ref, ext_ref, *out):
    pair_ref = out[-1]
    grams = ext_ref.shape[0] - ROWS
    ext = kept_ref.shape[0]
    size = ext // QUARTERS
    own, its = ext_ref[grams : grams + 1, :1], got_ref[ext + grams : ext + grams + 1, :1]
    top = jnp.maximum(own, its)
    pair_ref[:grams] = ext_ref[:grams] + got_ref[ext : ext + grams]
    pair_ref[grams:] = jnp.broadcast_to(top, (ROWS, 128))
    own, its = own / top, its / top
    for k, ref in zip((0,) + SHIFTS, out):
        at = pl.ds(pl.multiple_of((meta_ref[1] + k) % QUARTERS * size, size), size)
        ref[...] = kept_ref[at] * own + got_ref[at] * its


def pair(meta, kept, got, ext):
    size = kept.shape[0] // QUARTERS
    return pl.pallas_call(
        pair_kernel,
        out_shape=[jax.ShapeDtypeStruct((size, 128), F32)] * QUARTERS
        + [pltpu.VMEM(ext.shape, F32)],
        in_specs=[SCALAR] + [WHOLE] * 3,
        out_specs=[WHOLE] * (QUARTERS + 1),
        compiler_params=params(8),
        name="pair",
    )(meta, kept, got, ext)


def add_quarters_kernel(meta_ref, a_ref, b_ref, c_ref, d_ref, *out):
    size = a_ref.shape[0] // QUARTERS
    for k, ref in zip((0,) + SHIFTS, out):
        at = pl.ds(pl.multiple_of((meta_ref[2] + k) % QUARTERS * size, size), size)
        ref[...] = (a_ref[at] + b_ref[at]) + (c_ref[at] + d_ref[at])


def add_quarters(meta, parts):
    size = parts[0].shape[0] // QUARTERS
    return pl.pallas_call(
        add_quarters_kernel,
        out_shape=[jax.ShapeDtypeStruct((size, 128), F32)] * QUARTERS,
        in_specs=[SCALAR] + [WHOLE] * QUARTERS,
        out_specs=[WHOLE] * QUARTERS,
        compiler_params=params(8),
        name="add_quarters",
    )(meta, *parts)


def add_parts_kernel(a_ref, b_ref, c_ref, d_ref, ext_ref, out_ref):
    size = a_ref.shape[0]
    out_ref[:size] = (a_ref[...] + b_ref[...]) + (c_ref[...] + d_ref[...])
    out_ref[size:] = ext_ref[...]


def add_parts(parts, ext):
    return pl.pallas_call(
        add_parts_kernel,
        out_shape=jax.ShapeDtypeStruct((parts[0].shape[0] + ext.shape[0], 128), F32),
        in_specs=[WHOLE] * 5,
        out_specs=WHOLE,
        compiler_params=params(8),
        name="add_parts",
    )(*parts, ext)


def across_kernel(a_ref, b_ref, c_ref, d_ref, out_ref, ext_ref):
    size = out_ref.shape[0]
    grams = ext_ref.shape[0] - ROWS
    refs = (a_ref, b_ref, c_ref, d_ref)
    peaks = [r[size + grams : size + grams + 1, :1] for r in refs]
    top = jnp.maximum(jnp.maximum(peaks[0], peaks[1]), jnp.maximum(peaks[2], peaks[3]))
    a, b, c, d = (r[:size] * (k / top) for r, k in zip(refs, peaks))
    out_ref[...] = (a + b) + (c + d)
    a, b, c, d = (r[size : size + grams] for r in refs)
    ext_ref[:grams] = (a + b) + (c + d)
    ext_ref[grams:] = jnp.broadcast_to(top, (ROWS, 128))


def across(parts, extra):
    return pl.pallas_call(
        across_kernel,
        out_shape=[
            jax.ShapeDtypeStruct((parts[0].shape[0] - extra, 128), F32),
            pltpu.VMEM((extra, 128), F32),
        ],
        in_specs=[WHOLE] * 4,
        out_specs=[WHOLE] * 2,
        compiler_params=params(8),
        name="across",
    )(*parts)


def assemble_kernel(meta_ref, a_ref, b_ref, c_ref, d_ref, out_ref):
    size = a_ref.shape[0]
    for k, ref in zip((0,) + SHIFTS, (a_ref, b_ref, c_ref, d_ref)):
        at = pl.multiple_of((meta_ref[2] + QUARTERS - k) % QUARTERS * size, size)
        out_ref[pl.ds(at, size)] = ref[...]


def assemble(meta, parts):
    return pl.pallas_call(
        assemble_kernel,
        out_shape=jax.ShapeDtypeStruct((parts[0].shape[0] * QUARTERS, 128), F32),
        in_specs=[SCALAR] + [WHOLE] * 4,
        out_specs=WHOLE,
        compiler_params=params(8),
        name="assemble",
    )(meta, *parts)


def factor_kernel(replicas, ext_ref, p_ref, solve_ref, hat_ref):
    rank = p_ref.shape[0]
    groups = rank // ROWS
    sub = lax.broadcasted_iota(jnp.int32, (ROWS, 2 * rank), 0)
    lane = lax.broadcasted_iota(jnp.int32, (ROWS, 2 * rank), 1)
    blocks = []
    for g in range(groups):
        tile = ext_ref[g // 2 * ROWS : (g // 2 + 1) * ROWS, (g % 2) * rank : (g % 2 + 1) * rank]
        unit = jnp.where(lane[:, :rank] == sub[:, :rank] + g * ROWS, 1.0, 0.0)
        blocks.append(jnp.concatenate([tile, unit], axis=1))
    for j in range(rank):
        own, at = j // ROWS, j % ROWS
        row = blocks[own][at : at + 1]
        row = row / row[:, j : j + 1]
        for g in range(own, groups):
            column = blocks[g][:, j : j + 1]
            if g == own:
                column = jnp.where(sub[:, :1] > at, column, 0.0)
            blocks[g] = blocks[g] - column * row
    inverse = []
    for g in range(groups):
        diagonal = jnp.sum(
            jnp.where(lane == sub + g * ROWS, blocks[g], 0.0), axis=1, keepdims=True
        )
        inverse.append(blocks[g][:, rank:] / jnp.sqrt(diagonal))
    inverse = jnp.concatenate(inverse, axis=0)
    grams = ext_ref.shape[0] - ROWS
    solve_ref[...] = inverse * (ext_ref[grams : grams + 1, :1] * (1.0 / replicas))
    hat_ref[...] = jnp.dot(inverse, p_ref[...], precision=HIGHEST, preferred_element_type=F32)


def factor(ext, p_mean, replicas):
    rank, rows = p_mean.shape
    return pl.pallas_call(
        functools.partial(factor_kernel, replicas),
        out_shape=[
            jax.ShapeDtypeStruct((rank, rank), F32),
            jax.ShapeDtypeStruct((rank, rows), F32),
        ],
        in_specs=[WHOLE] * 2,
        out_specs=[WHOLE] * 2,
        compiler_params=params(8),
        cost_estimate=cost(1 << 32, 1 << 20),
        name="factor",
    )(ext, p_mean)


def result_kernel(sources, width, meta_ref, solve_ref, p_ref, m_ref, *refs):
    error_hbm, q_hbm, error_ref, q_ref, sems = refs[-5:]
    rank = solve_ref.shape[0]
    columns = q_ref.shape[2]
    left = p_ref[...].T.astype(BF16)
    s1, s2, s3 = split(solve_ref[...])
    solve = jnp.concatenate([s1, s1, s2, s2, s1, s3], axis=1)

    def copies(n, base, at, size):
        to, here = pl.ds(pl.multiple_of(base + at, 128), size), pl.ds(at, size)
        return (
            pltpu.make_async_copy(error_ref.at[n, :, here], error_hbm.at[:, to], sems.at[0, n]),
            pltpu.make_async_copy(q_ref.at[n, :, here], q_hbm.at[:, to], sems.at[1, n]),
        )

    bases = []
    for n, (own, k) in enumerate(sources):
        t_ref = refs[n]
        core = meta_ref[0] if own else 1 - meta_ref[0]
        quarter = (meta_ref[1 if own else 2] + QUARTERS - k) % QUARTERS
        base = (core * QUARTERS + quarter) * columns
        bases.append(base)
        for at in range(0, columns, width):
            t = jnp.concatenate(
                [
                    jnp.concatenate(
                        [
                            t_ref[(g * columns + i) // 128 * ROWS : (g * columns + i) // 128 * ROWS + ROWS, :]
                            for i in range(at, at + width, 128)
                        ],
                        axis=1,
                    )
                    for g in range(rank // ROWS)
                ],
                axis=0,
            )
            t1, t2, t3 = split(t)
            t = jnp.concatenate([t1, t2, t1, t2, t3, t1], axis=0)
            new = jnp.dot(solve, t, preferred_element_type=F32)
            q_ref[n, :, at : at + width] = new
            decoded = jnp.dot(left, new.astype(BF16), preferred_element_type=F32)
            m = m_ref[:, pl.ds(pl.multiple_of(base + at, 128), width)]
            error_ref[n, :, at : at + width] = (m.astype(F32) - decoded).astype(BF16)
            for c in copies(n, base, at, width):
                c.start()
    for n, base in enumerate(bases):
        for c in copies(n, base, 0, columns):
            c.wait()


def result(meta, sources, totals, merged, solve, p_hat, before):
    rank = solve.shape[0]
    rows, columns = merged.shape
    quarter = columns // 2 // QUARTERS
    n = len(sources)
    held = [] if before is None else list(before)
    return pl.pallas_call(
        functools.partial(result_kernel, sources, quarter // 2),
        out_shape=[pltpu.HBM((rows, columns), BF16), pltpu.HBM((rank, columns), F32)],
        in_specs=[SCALAR] + [WHOLE] * (3 + n) + [ANY] * len(held),
        out_specs=[ANY, ANY],
        scratch_shapes=[
            pltpu.VMEM((n, rows, quarter), BF16),
            pltpu.VMEM((n, rank, quarter), F32),
            pltpu.SemaphoreType.DMA((2, n)),
        ],
        input_output_aliases={4 + n + i: i for i in range(len(held))},
        compiler_params=params(12),
        cost_estimate=cost(2 * n * rank * rows * quarter, 4 * n * rows * quarter),
        name="result",
    )(meta, solve, p_hat, merged, *totals, *held)


def body(gradient, error, q_start):
    rank = q_start.shape[0]
    replicas = SIZES[0] * SIZES[1]
    core, x, z = (lax.axis_index(a) for a in ("c", "x", "z"))
    meta = jnp.stack([core, jnp.where(core == 0, x, z), jnp.where(core == 0, z, x)])

    merged, p = merge(meta, gradient[0], error[0], q_start)
    a, b, c = ring_x_or_z([p] * 3, 0)
    p = (p + a) + (b + c)
    sent, ext, p_mean, pieces = first_right(
        meta, (p, *ring_x_or_z([p] * 3, 1)), merged, rank, replicas
    )
    got = swap(sent)
    kept = second_right(meta, pieces, merged)
    own, *sent, ext = pair(meta, kept, got, ext)
    own, *sent = add_quarters(meta, (own, *ring_x_or_z(sent, 0)))
    part = add_parts((own, *ring_x_or_z(sent, 1)), ext)
    total, ext = across((part, *ring_y(part)), ext.shape[0])
    solve, p_hat = factor(ext, p_mean, replicas)
    total = assemble(meta, (total, *ring_x_or_z([total] * 3, 1)))
    totals = dict(zip((0,) + SHIFTS, (total, *ring_x_or_z([total] * 3, 0))))
    out = None
    for own, turns in ((True, (0,)), (False, (0,)), (True, (1, 3)), (False, (1, 3)), (True, (2,)), (False, (2,))):
        sources = tuple((own, k) for k in turns)
        held = [totals[k] if own else swap(totals[k]) for k in turns]
        out = result(meta, sources, held, merged, solve, p_hat, out)
    new_error, q_new = out
    return (new_error[None], p_hat, q_new)


def solution(mesh):
    fine = Mesh(mesh.devices.reshape(SIZES), AXES)
    return jax.shard_map(
        body,
        mesh=fine,
        in_specs=(P(DP, ("y", "c"), None), P(DP, ("y", "c"), None), P()),
        out_specs=(P(DP, ("y", "c"), None), P(None, ("y", "c")), P()),
        check_vma=False,
    )
```

```python
import functools

import jax
import jax.numpy as jnp
from jax import lax
from jax.experimental import pallas as pl
from jax.experimental.pallas import tpu as pltpu
from jax.sharding import Mesh, PartitionSpec as P

DP = ("z", "x")
AXES = ("z", "x", "y", "c")
SIZES = (4, 4, 4, 2)
HIGHEST = lax.Precision.HIGHEST
F32 = jnp.float32
BF16 = jnp.bfloat16
MIB = 1 << 20
ROWS = 8
QUARTERS = 4
SHIFTS = (1, 3, 2)
ANY = pl.BlockSpec(memory_space=pl.ANY)
WHOLE = pl.BlockSpec(memory_space=pltpu.VMEM)
SCALAR = pl.BlockSpec(memory_space=pltpu.SMEM)


def params(mib):
    return pltpu.CompilerParams(vmem_limit_bytes=mib * MIB)


def cost(flops, nbytes):
    return pl.CostEstimate(flops=flops, bytes_accessed=nbytes, transcendentals=0)


def index(z, x, y, c):
    return ((z * SIZES[1] + x) * SIZES[2] + y) * SIZES[3] + c


def everyone():
    return [
        (z, x, y, c)
        for z in range(SIZES[0])
        for x in range(SIZES[1])
        for y in range(SIZES[2])
        for c in range(SIZES[3])
    ]


def ring_x_or_z(values, phase):
    out = []
    for k, value in zip(SHIFTS, values):
        pairs = []
        for z, x, y, c in everyone():
            to = (z, (x + k) % SIZES[1], y, c) if c == phase else ((z + k) % SIZES[0], x, y, c)
            pairs.append((index(z, x, y, c), index(*to)))
        out.append(lax.ppermute(value, AXES, pairs))
    return out


def ring_y(value):
    n = SIZES[2]
    return [lax.ppermute(value, "y", [(i, (i + k) % n) for i in range(n)]) for k in SHIFTS]


def swap(value):
    return lax.ppermute(value, "c", [(0, 1), (1, 0)])


def merge_kernel(width, meta_ref, g_hbm, e_hbm, q_hbm, m_ref, p_ref, g_ref, e_ref, q_ref, sems):
    rows, columns = g_ref.shape
    rank = q_ref.shape[0]
    steps = columns // width
    del meta_ref

    def copies(i):
        at = pl.ds(i * width, width)
        return [
            pltpu.make_async_copy(src.at[:, at], dst.at[:, at], sems.at[n, i])
            for n, (src, dst) in enumerate(((g_hbm, g_ref), (e_hbm, e_ref), (q_hbm, q_ref)))
        ]

    for i in range(steps):
        for c in copies(i):
            c.start()
    acc = jnp.zeros((rows, rank), F32)
    for i in range(steps):
        for c in copies(i):
            c.wait()
        at = pl.ds(i * width, width)
        m = (g_ref[:, at].astype(F32) + e_ref[:, at].astype(F32)).astype(BF16)
        m_ref[:, at] = m
        acc = acc + lax.dot_general(
            m, q_ref[:, at], (((1,), (1,)), ((), ())), preferred_element_type=F32
        )
    p_ref[...] = pack(acc.T)


def pack(p):
    rank, rows = p.shape
    full = rows // 128
    half = rank // 2
    parts = [p[:, i * 128 : (i + 1) * 128] for i in range(full)]
    rest = p[:, full * 128 :]
    return jnp.concatenate(parts + [jnp.concatenate([rest[:half], rest[half:]], axis=1)], axis=0)


def unpack(packed, rank):
    full = packed.shape[0] // rank
    last = packed[full * rank :]
    rest = jnp.concatenate([last[:, :64], last[:, 64:]], axis=0)
    return jnp.concatenate(
        [packed[i * rank : (i + 1) * rank] for i in range(full)] + [rest], axis=1
    )


def merge(meta, gradient, error, q_start):
    rows, columns = gradient.shape
    rank = q_start.shape[0]
    width = 1024
    gradient, error, q_start = (
        pltpu.with_memory_space_constraint(a, pltpu.HBM) for a in (gradient, error, q_start)
    )
    return pl.pallas_call(
        functools.partial(merge_kernel, width),
        out_shape=[pltpu.VMEM((rows, columns), BF16), pltpu.VMEM((rank * rows // 128, 128), F32)],
        in_specs=[SCALAR, ANY, ANY, ANY],
        out_specs=[WHOLE, WHOLE],
        scratch_shapes=[
            pltpu.VMEM((rows, columns), BF16),
            pltpu.VMEM((rows, columns), BF16),
            pltpu.VMEM((rank, columns), BF16),
            pltpu.SemaphoreType.DMA((3, columns // width)),
        ],
        compiler_params=params(24),
        cost_estimate=cost(2 * rank * rows * columns, 4 * rows * columns),
        name="merge",
    )(meta, gradient, error, q_start)


def right_tiles(half, pieces, m_ref, out_ref):
    rank = pieces.shape[0] // 3
    width = m_ref.shape[1] // 2 // QUARTERS
    size = rank * width // 128

    def step(a, carry):
        at = pl.multiple_of((half * QUARTERS + a) * width, width)
        t = jnp.dot(pieces, m_ref[:, pl.ds(at, width)], preferred_element_type=F32)
        t = t[:rank] + (t[rank : 2 * rank] + t[2 * rank :])
        to = 0
        for g in range(rank // ROWS):
            for n in range(width // 128):
                here = pl.ds(pl.multiple_of(a * size + to, ROWS), ROWS)
                out_ref[here, :] = t[g * ROWS : (g + 1) * ROWS, n * 128 : (n + 1) * 128]
                to += ROWS
        return carry

    lax.fori_loop(0, QUARTERS, step, 0, unroll=2)


def split(n):
    high = n.astype(BF16)
    n = n - high.astype(F32)
    middle = n.astype(BF16)
    return high, middle, (n - middle.astype(F32)).astype(BF16)


def first_right_kernel(replicas, rank, meta_ref, a_ref, b_ref, c_ref, d_ref, m_ref, out_ref, ext_ref, p_ref, pieces_ref):
    p = (a_ref[...] + b_ref[...] + (c_ref[...] + d_ref[...])) * (1.0 / replicas)
    peak = jnp.max(jnp.abs(p), axis=(0, 1), keepdims=True)
    peak = jnp.where(peak > 0, peak, 1.0)
    p = unpack(p, rank)
    p_ref[...] = p
    gram = lax.dot_general(
        p, p, (((1,), (1,)), ((), ())), precision=HIGHEST, preferred_element_type=F32
    )
    two = 2 * ROWS
    ext = jnp.concatenate(
        [
            jnp.concatenate([gram[i : i + ROWS], gram[i + ROWS : i + two]], axis=1)
            for i in range(0, rank, two)
        ]
        + [jnp.broadcast_to(peak, (ROWS, 128))],
        axis=0,
    )
    ext_ref[...] = ext
    out_ref[out_ref.shape[0] - ext.shape[0] :, :] = ext
    pieces = jnp.concatenate(split(p / peak), axis=0)
    pieces_ref[...] = pieces
    right_tiles(1 - meta_ref[0], pieces, m_ref, out_ref)


def second_right_kernel(meta_ref, pieces_ref, m_ref, out_ref):
    right_tiles(meta_ref[0], pieces_ref[...], m_ref, out_ref)


def first_right(meta, parts, merged, rank, replicas):
    rows, columns = merged.shape
    size = rank * columns // 256
    extra = rank * rank // 128 + ROWS
    return pl.pallas_call(
        functools.partial(first_right_kernel, replicas, rank),
        out_shape=[
            jax.ShapeDtypeStruct((size + extra, 128), F32),
            pltpu.VMEM((extra, 128), F32),
            pltpu.VMEM((rank, rows), F32),
            pltpu.VMEM((3 * rank, rows), BF16),
        ],
        in_specs=[SCALAR] + [WHOLE] * 5,
        out_specs=[WHOLE] * 4,
        compiler_params=params(12),
        cost_estimate=cost(3 * rank * rows * columns, 512 * size),
        name="first_right",
    )(meta, *parts, merged)


def second_right(meta, pieces, merged):
    size = pieces.shape[0] // 3 * merged.shape[1] // 256
    return pl.pallas_call(
        second_right_kernel,
        out_shape=pltpu.VMEM((size, 128), F32),
        in_specs=[SCALAR, WHOLE, WHOLE],
        out_specs=WHOLE,
        compiler_params=params(12),
        cost_estimate=cost(pieces.shape[0] * merged.size, 512 * size),
        name="second_right",
    )(meta, pieces, merged)


def pair_kernel(meta_ref, kept_ref, got_ref, ext_ref, *out):
    pair_ref = out[-1]
    grams = ext_ref.shape[0] - ROWS
    ext = kept_ref.shape[0]
    size = ext // QUARTERS
    own, its = ext_ref[grams : grams + 1, :1], got_ref[ext + grams : ext + grams + 1, :1]
    top = jnp.maximum(own, its)
    pair_ref[:grams] = ext_ref[:grams] + got_ref[ext : ext + grams]
    pair_ref[grams:] = jnp.broadcast_to(top, (ROWS, 128))
    own, its = own / top, its / top
    for k, ref in zip((0,) + SHIFTS, out):
        at = pl.ds(pl.multiple_of((meta_ref[1] + k) % QUARTERS * size, size), size)
        ref[...] = kept_ref[at] * own + got_ref[at] * its


def pair(meta, kept, got, ext):
    size = kept.shape[0] // QUARTERS
    return pl.pallas_call(
        pair_kernel,
        out_shape=[jax.ShapeDtypeStruct((size, 128), F32)] * QUARTERS
        + [pltpu.VMEM(ext.shape, F32)],
        in_specs=[SCALAR] + [WHOLE] * 3,
        out_specs=[WHOLE] * (QUARTERS + 1),
        compiler_params=params(8),
        name="pair",
    )(meta, kept, got, ext)


def add_quarters_kernel(meta_ref, a_ref, b_ref, c_ref, d_ref, *out):
    size = a_ref.shape[0] // QUARTERS
    for k, ref in zip((0,) + SHIFTS, out):
        at = pl.ds(pl.multiple_of((meta_ref[2] + k) % QUARTERS * size, size), size)
        ref[...] = (a_ref[at] + b_ref[at]) + (c_ref[at] + d_ref[at])


def add_quarters(meta, parts):
    size = parts[0].shape[0] // QUARTERS
    return pl.pallas_call(
        add_quarters_kernel,
        out_shape=[jax.ShapeDtypeStruct((size, 128), F32)] * QUARTERS,
        in_specs=[SCALAR] + [WHOLE] * QUARTERS,
        out_specs=[WHOLE] * QUARTERS,
        compiler_params=params(8),
        name="add_quarters",
    )(meta, *parts)


def add_parts_kernel(a_ref, b_ref, c_ref, d_ref, ext_ref, out_ref):
    size = a_ref.shape[0]
    out_ref[:size] = (a_ref[...] + b_ref[...]) + (c_ref[...] + d_ref[...])
    out_ref[size:] = ext_ref[...]


def add_parts(parts, ext):
    return pl.pallas_call(
        add_parts_kernel,
        out_shape=jax.ShapeDtypeStruct((parts[0].shape[0] + ext.shape[0], 128), F32),
        in_specs=[WHOLE] * 5,
        out_specs=WHOLE,
        compiler_params=params(8),
        name="add_parts",
    )(*parts, ext)


def across_kernel(a_ref, b_ref, c_ref, d_ref, out_ref, ext_ref):
    size = out_ref.shape[0]
    grams = ext_ref.shape[0] - ROWS
    refs = (a_ref, b_ref, c_ref, d_ref)
    peaks = [r[size + grams : size + grams + 1, :1] for r in refs]
    top = jnp.maximum(jnp.maximum(peaks[0], peaks[1]), jnp.maximum(peaks[2], peaks[3]))
    a, b, c, d = (r[:size] * (k / top) for r, k in zip(refs, peaks))
    out_ref[...] = (a + b) + (c + d)
    a, b, c, d = (r[size : size + grams] for r in refs)
    ext_ref[:grams] = (a + b) + (c + d)
    ext_ref[grams:] = jnp.broadcast_to(top, (ROWS, 128))


def across(parts, extra):
    return pl.pallas_call(
        across_kernel,
        out_shape=[
            jax.ShapeDtypeStruct((parts[0].shape[0] - extra, 128), F32),
            pltpu.VMEM((extra, 128), F32),
        ],
        in_specs=[WHOLE] * 4,
        out_specs=[WHOLE] * 2,
        compiler_params=params(8),
        name="across",
    )(*parts)


def assemble_kernel(meta_ref, a_ref, b_ref, c_ref, d_ref, after_ref, out_ref):
    del after_ref
    size = a_ref.shape[0]
    for k, ref in zip((0,) + SHIFTS, (a_ref, b_ref, c_ref, d_ref)):
        at = pl.multiple_of((meta_ref[2] + QUARTERS - k) % QUARTERS * size, size)
        out_ref[pl.ds(at, size)] = ref[...]


def assemble(meta, parts, after):
    return pl.pallas_call(
        assemble_kernel,
        out_shape=jax.ShapeDtypeStruct((parts[0].shape[0] * QUARTERS, 128), F32),
        in_specs=[SCALAR] + [WHOLE] * 4 + [ANY],
        out_specs=WHOLE,
        compiler_params=params(8),
        name="assemble",
    )(meta, *parts, after)


def factor_kernel(replicas, ext_ref, p_ref, solve_ref, hat_ref):
    rank = p_ref.shape[0]
    groups = rank // ROWS
    sub = lax.broadcasted_iota(jnp.int32, (ROWS, 2 * rank), 0)
    lane = lax.broadcasted_iota(jnp.int32, (ROWS, 2 * rank), 1)
    blocks = []
    for g in range(groups):
        tile = ext_ref[g // 2 * ROWS : (g // 2 + 1) * ROWS, (g % 2) * rank : (g % 2 + 1) * rank]
        unit = jnp.where(lane[:, :rank] == sub[:, :rank] + g * ROWS, 1.0, 0.0)
        blocks.append(jnp.concatenate([tile, unit], axis=1))
    for j in range(rank):
        own, at = j // ROWS, j % ROWS
        row = blocks[own][at : at + 1]
        row = row / row[:, j : j + 1]
        for g in range(own, groups):
            column = blocks[g][:, j : j + 1]
            if g == own:
                column = jnp.where(sub[:, :1] > at, column, 0.0)
            blocks[g] = blocks[g] - column * row
    inverse = []
    for g in range(groups):
        diagonal = jnp.sum(
            jnp.where(lane == sub + g * ROWS, blocks[g], 0.0), axis=1, keepdims=True
        )
        inverse.append(blocks[g][:, rank:] / jnp.sqrt(diagonal))
    inverse = jnp.concatenate(inverse, axis=0)
    grams = ext_ref.shape[0] - ROWS
    solve_ref[...] = inverse * (ext_ref[grams : grams + 1, :1] * (1.0 / replicas))
    hat_ref[...] = jnp.dot(inverse, p_ref[...], precision=HIGHEST, preferred_element_type=F32)


def factor(ext, p_mean, replicas):
    rank, rows = p_mean.shape
    return pl.pallas_call(
        functools.partial(factor_kernel, replicas),
        out_shape=[
            jax.ShapeDtypeStruct((rank, rank), F32),
            jax.ShapeDtypeStruct((rank, rows), F32),
        ],
        in_specs=[WHOLE] * 2,
        out_specs=[WHOLE] * 2,
        compiler_params=params(8),
        cost_estimate=cost(1 << 32, 1 << 20),
        name="factor",
    )(ext, p_mean)


def result_kernel(sources, width, meta_ref, solve_ref, p_ref, m_ref, *refs):
    error_hbm, q_hbm, token_ref, error_ref, q_ref, sems = refs[-6:]
    token_ref[...] = jnp.zeros_like(token_ref)
    rank = solve_ref.shape[0]
    columns = q_ref.shape[2]
    left = p_ref[...].T.astype(BF16)
    s1, s2, s3 = split(solve_ref[...])
    solve = jnp.concatenate([s1, s1, s2, s2, s1, s3], axis=1)

    def copies(n, base, at, size):
        to, here = pl.ds(pl.multiple_of(base + at, 128), size), pl.ds(at, size)
        return (
            pltpu.make_async_copy(error_ref.at[n, :, here], error_hbm.at[:, to], sems.at[0, n]),
            pltpu.make_async_copy(q_ref.at[n, :, here], q_hbm.at[:, to], sems.at[1, n]),
        )

    bases = []
    for n, (own, k) in enumerate(sources):
        t_ref = refs[n]
        core = meta_ref[0] if own else 1 - meta_ref[0]
        quarter = (meta_ref[1 if own else 2] + QUARTERS - k) % QUARTERS
        base = (core * QUARTERS + quarter) * columns
        bases.append(base)
        for at in range(0, columns, width):
            t = jnp.concatenate(
                [
                    jnp.concatenate(
                        [
                            t_ref[(g * columns + i) // 128 * ROWS : (g * columns + i) // 128 * ROWS + ROWS, :]
                            for i in range(at, at + width, 128)
                        ],
                        axis=1,
                    )
                    for g in range(rank // ROWS)
                ],
                axis=0,
            )
            t1, t2, t3 = split(t)
            t = jnp.concatenate([t1, t2, t1, t2, t3, t1], axis=0)
            new = jnp.dot(solve, t, preferred_element_type=F32)
            q_ref[n, :, at : at + width] = new
            decoded = jnp.dot(left, new.astype(BF16), preferred_element_type=F32)
            m = m_ref[:, pl.ds(pl.multiple_of(base + at, 128), width)]
            error_ref[n, :, at : at + width] = (m.astype(F32) - decoded).astype(BF16)
            for c in copies(n, base, at, width):
                c.start()
    for n, base in enumerate(bases):
        for c in copies(n, base, 0, columns):
            c.wait()


def result(meta, sources, totals, merged, solve, p_hat, before):
    rank = solve.shape[0]
    rows, columns = merged.shape
    quarter = columns // 2 // QUARTERS
    n = len(sources)
    held = [] if before is None else list(before)
    return pl.pallas_call(
        functools.partial(result_kernel, sources, quarter // 2),
        out_shape=[
            pltpu.HBM((rows, columns), BF16),
            pltpu.HBM((rank, columns), F32),
            pltpu.VMEM((ROWS, 128), F32),
        ],
        in_specs=[SCALAR] + [WHOLE] * (3 + n) + [ANY] * len(held),
        out_specs=[ANY, ANY, WHOLE],
        scratch_shapes=[
            pltpu.VMEM((n, rows, quarter), BF16),
            pltpu.VMEM((n, rank, quarter), F32),
            pltpu.SemaphoreType.DMA((2, n)),
        ],
        input_output_aliases={4 + n + i: i for i in range(len(held))},
        compiler_params=params(12),
        cost_estimate=cost(2 * n * rank * rows * quarter, 4 * n * rows * quarter),
        name="result",
    )(meta, solve, p_hat, merged, *totals, *held)


def tie_kernel(value_ref, after_ref, out_ref):
    del value_ref, after_ref, out_ref


def tie(value, after):
    return pl.pallas_call(
        tie_kernel,
        out_shape=jax.ShapeDtypeStruct(value.shape, value.dtype),
        in_specs=[ANY] * 2,
        out_specs=ANY,
        input_output_aliases={0: 0},
        compiler_params=params(4),
        name="tie",
    )(value, after)


def body(gradient, error, q_start):
    rank = q_start.shape[0]
    replicas = SIZES[0] * SIZES[1]
    core, x, z = (lax.axis_index(a) for a in ("c", "x", "z"))
    meta = jnp.stack([core, jnp.where(core == 0, x, z), jnp.where(core == 0, z, x)])

    merged, p = merge(meta, gradient[0], error[0], q_start)
    a, b, c = ring_x_or_z([p] * 3, 0)
    p = (p + a) + (b + c)
    sent, ext, p_mean, pieces = first_right(
        meta, (p, *ring_x_or_z([p] * 3, 1)), merged, rank, replicas
    )
    got = swap(sent)
    kept = second_right(meta, pieces, merged)
    own, *sent, ext = pair(meta, kept, got, ext)
    own, *sent = add_quarters(meta, (own, *ring_x_or_z(sent, 0)))
    part = add_parts((own, *ring_x_or_z(sent, 1)), ext)
    total, ext = across((part, *ring_y(part)), ext.shape[0])
    solve, p_hat = factor(ext, p_mean, replicas)
    total = assemble(meta, (total, *ring_x_or_z([total] * 3, 1)), solve)
    one, three, two = ring_x_or_z([total] * 3, 0)

    def write(sources, totals, before):
        return result(meta, sources, totals, merged, solve, p_hat, before)

    *out, token = write(((True, 0), (False, 0)), (total, swap(total)), None)
    one, three = tie(one, token), tie(three, token)
    *out, _ = write(((True, 1), (True, 3)), (one, three), out)
    *out, token = write(((False, 1), (False, 3)), (swap(one), swap(three)), out)
    two = tie(two, token)
    *out, _ = write(((True, 2),), (two,), out)
    new_error, q_new, _ = write(((False, 2),), (swap(two),), out)
    return (new_error[None], p_hat, q_new)


def solution(mesh):
    fine = Mesh(mesh.devices.reshape(SIZES), AXES)
    return jax.shard_map(
        body,
        mesh=fine,
        in_specs=(P(DP, ("y", "c"), None), P(DP, ("y", "c"), None), P()),
        out_specs=(P(DP, ("y", "c"), None), P(None, ("y", "c")), P()),
        check_vma=False,
    )
```

```python
import functools

import jax
import jax.numpy as jnp
from jax import lax
from jax.experimental import pallas as pl
from jax.experimental.pallas import tpu as pltpu
from jax.sharding import Mesh, PartitionSpec as P

DP = ("z", "x")
AXES = ("z", "x", "y", "c")
SIZES = (4, 4, 4, 2)
HIGHEST = lax.Precision.HIGHEST
F32 = jnp.float32
BF16 = jnp.bfloat16
MIB = 1 << 20
ROWS = 8
QUARTERS = 4
SHIFTS = (1, 3, 2)
ANY = pl.BlockSpec(memory_space=pl.ANY)
WHOLE = pl.BlockSpec(memory_space=pltpu.VMEM)


def params(mib):
    return pltpu.CompilerParams(vmem_limit_bytes=mib * MIB)


def cost(flops, nbytes):
    return pl.CostEstimate(flops=flops, bytes_accessed=nbytes, transcendentals=0)


def place():
    core, x, z = (lax.axis_index(a) for a in ("c", "x", "z"))
    return core, jnp.where(core == 0, x, z), jnp.where(core == 0, z, x)


def index(z, x, y, c):
    return ((z * SIZES[1] + x) * SIZES[2] + y) * SIZES[3] + c


def everyone():
    return [
        (z, x, y, c)
        for z in range(SIZES[0])
        for x in range(SIZES[1])
        for y in range(SIZES[2])
        for c in range(SIZES[3])
    ]


def ring_x_or_z(values, phase):
    out = []
    for k, value in zip(SHIFTS, values):
        pairs = []
        for z, x, y, c in everyone():
            to = (z, (x + k) % SIZES[1], y, c) if c == phase else ((z + k) % SIZES[0], x, y, c)
            pairs.append((index(z, x, y, c), index(*to)))
        out.append(lax.ppermute(value, AXES, pairs))
    return out


def ring_y(value):
    n = SIZES[2]
    return [lax.ppermute(value, "y", [(i, (i + k) % n) for i in range(n)]) for k in SHIFTS]


def swap(value):
    return lax.ppermute(value, "c", [(0, 1), (1, 0)])


def merge_kernel(width, g_hbm, e_hbm, q_hbm, m_ref, p_ref, g_ref, e_ref, q_ref, sems):
    rows, columns = g_ref.shape
    rank = q_ref.shape[0]
    steps = columns // width

    def copies(i):
        at = pl.ds(i * width, width)
        return [
            pltpu.make_async_copy(src.at[:, at], dst.at[:, at], sems.at[n, i])
            for n, (src, dst) in enumerate(((g_hbm, g_ref), (e_hbm, e_ref), (q_hbm, q_ref)))
        ]

    for i in range(steps):
        for c in copies(i):
            c.start()
    acc = jnp.zeros((rows, rank), F32)
    for i in range(steps):
        for c in copies(i):
            c.wait()
        at = pl.ds(i * width, width)
        m = (g_ref[:, at].astype(F32) + e_ref[:, at].astype(F32)).astype(BF16)
        m_ref[:, at] = m
        acc = acc + lax.dot_general(
            m, q_ref[:, at], (((1,), (1,)), ((), ())), preferred_element_type=F32
        )
    p_ref[...] = pack(acc.T)


def pack(p):
    rank, rows = p.shape
    full = rows // 128
    half = rank // 2
    parts = [p[:, i * 128 : (i + 1) * 128] for i in range(full)]
    rest = p[:, full * 128 :]
    return jnp.concatenate(parts + [jnp.concatenate([rest[:half], rest[half:]], axis=1)], axis=0)


def unpack(packed, rank):
    full = packed.shape[0] // rank
    last = packed[full * rank :]
    rest = jnp.concatenate([last[:, :64], last[:, 64:]], axis=0)
    return jnp.concatenate(
        [packed[i * rank : (i + 1) * rank] for i in range(full)] + [rest], axis=1
    )


def merge(gradient, error, q_start):
    rows, columns = gradient.shape
    rank = q_start.shape[0]
    width = 1024
    gradient, error, q_start = (
        pltpu.with_memory_space_constraint(a, pltpu.HBM) for a in (gradient, error, q_start)
    )
    return pl.pallas_call(
        functools.partial(merge_kernel, width),
        out_shape=[pltpu.VMEM((rows, columns), BF16), pltpu.VMEM((rank * rows // 128, 128), F32)],
        in_specs=[ANY, ANY, ANY],
        out_specs=[WHOLE, WHOLE],
        scratch_shapes=[
            pltpu.VMEM((rows, columns), BF16),
            pltpu.VMEM((rows, columns), BF16),
            pltpu.VMEM((rank, columns), BF16),
            pltpu.SemaphoreType.DMA((3, columns // width)),
        ],
        compiler_params=params(24),
        cost_estimate=cost(2 * rank * rows * columns, 4 * rows * columns),
        name="merge",
    )(gradient, error, q_start)


def right_tiles(half, pieces, m_ref, out_ref):
    rank = pieces.shape[0] // 3
    width = m_ref.shape[1] // 2 // QUARTERS
    size = rank * width // 128

    def step(a, carry):
        at = pl.multiple_of((half * QUARTERS + a) * width, width)
        t = jnp.dot(pieces, m_ref[:, pl.ds(at, width)], preferred_element_type=F32)
        t = t[:rank] + (t[rank : 2 * rank] + t[2 * rank :])
        to = 0
        for g in range(rank // ROWS):
            for n in range(width // 128):
                here = pl.ds(pl.multiple_of(a * size + to, ROWS), ROWS)
                out_ref[here, :] = t[g * ROWS : (g + 1) * ROWS, n * 128 : (n + 1) * 128]
                to += ROWS
        return carry

    lax.fori_loop(0, QUARTERS, step, 0, unroll=2)


def split(n):
    high = n.astype(BF16)
    n = n - high.astype(F32)
    middle = n.astype(BF16)
    return high, middle, (n - middle.astype(F32)).astype(BF16)


def first_right_kernel(replicas, rank, a_ref, b_ref, c_ref, d_ref, m_ref, out_ref, ext_ref, p_ref, pieces_ref):
    p = (a_ref[...] + b_ref[...] + (c_ref[...] + d_ref[...])) * (1.0 / replicas)
    peak = jnp.max(jnp.abs(p), axis=(0, 1), keepdims=True)
    peak = jnp.where(peak > 0, peak, 1.0)
    p = unpack(p, rank)
    p_ref[...] = p
    gram = lax.dot_general(
        p, p, (((1,), (1,)), ((), ())), precision=HIGHEST, preferred_element_type=F32
    )
    two = 2 * ROWS
    ext = jnp.concatenate(
        [
            jnp.concatenate([gram[i : i + ROWS], gram[i + ROWS : i + two]], axis=1)
            for i in range(0, rank, two)
        ]
        + [jnp.broadcast_to(peak, (ROWS, 128))],
        axis=0,
    )
    ext_ref[...] = ext
    out_ref[out_ref.shape[0] - ext.shape[0] :, :] = ext
    pieces = jnp.concatenate(split(p / peak), axis=0)
    pieces_ref[...] = pieces
    right_tiles(1 - place()[0], pieces, m_ref, out_ref)


def second_right_kernel(pieces_ref, m_ref, out_ref):
    right_tiles(place()[0], pieces_ref[...], m_ref, out_ref)


def first_right(parts, merged, rank, replicas):
    rows, columns = merged.shape
    size = rank * columns // 256
    extra = rank * rank // 128 + ROWS
    return pl.pallas_call(
        functools.partial(first_right_kernel, replicas, rank),
        out_shape=[
            jax.ShapeDtypeStruct((size + extra, 128), F32),
            pltpu.VMEM((extra, 128), F32),
            pltpu.VMEM((rank, rows), F32),
            pltpu.VMEM((3 * rank, rows), BF16),
        ],
        in_specs=[WHOLE] * 5,
        out_specs=[WHOLE] * 4,
        compiler_params=params(12),
        cost_estimate=cost(3 * rank * rows * columns, 512 * size),
        name="first_right",
    )(*parts, merged)


def second_right(pieces, merged):
    size = pieces.shape[0] // 3 * merged.shape[1] // 256
    return pl.pallas_call(
        second_right_kernel,
        out_shape=pltpu.VMEM((size, 128), F32),
        in_specs=[WHOLE, WHOLE],
        out_specs=WHOLE,
        compiler_params=params(12),
        cost_estimate=cost(pieces.shape[0] * merged.size, 512 * size),
        name="second_right",
    )(pieces, merged)


def pair_kernel(kept_ref, got_ref, ext_ref, *out):
    pair_ref = out[-1]
    grams = ext_ref.shape[0] - ROWS
    ext = kept_ref.shape[0]
    size = ext // QUARTERS
    own, its = ext_ref[grams : grams + 1, :1], got_ref[ext + grams : ext + grams + 1, :1]
    top = jnp.maximum(own, its)
    pair_ref[:grams] = ext_ref[:grams] + got_ref[ext : ext + grams]
    pair_ref[grams:] = jnp.broadcast_to(top, (ROWS, 128))
    own, its = own / top, its / top
    for k, ref in zip((0,) + SHIFTS, out):
        at = pl.ds(pl.multiple_of((place()[1] + k) % QUARTERS * size, size), size)
        ref[...] = kept_ref[at] * own + got_ref[at] * its


def pair(kept, got, ext):
    size = kept.shape[0] // QUARTERS
    return pl.pallas_call(
        pair_kernel,
        out_shape=[jax.ShapeDtypeStruct((size, 128), F32)] * QUARTERS
        + [pltpu.VMEM(ext.shape, F32)],
        in_specs=[WHOLE] * 3,
        out_specs=[WHOLE] * (QUARTERS + 1),
        compiler_params=params(8),
        name="pair",
    )(kept, got, ext)


def add_quarters_kernel(a_ref, b_ref, c_ref, d_ref, *out):
    size = a_ref.shape[0] // QUARTERS
    for k, ref in zip((0,) + SHIFTS, out):
        at = pl.ds(pl.multiple_of((place()[2] + k) % QUARTERS * size, size), size)
        ref[...] = (a_ref[at] + b_ref[at]) + (c_ref[at] + d_ref[at])


def add_quarters(parts):
    size = parts[0].shape[0] // QUARTERS
    return pl.pallas_call(
        add_quarters_kernel,
        out_shape=[jax.ShapeDtypeStruct((size, 128), F32)] * QUARTERS,
        in_specs=[WHOLE] * QUARTERS,
        out_specs=[WHOLE] * QUARTERS,
        compiler_params=params(8),
        name="add_quarters",
    )(*parts)


def add_parts_kernel(a_ref, b_ref, c_ref, d_ref, ext_ref, out_ref):
    size = a_ref.shape[0]
    out_ref[:size] = (a_ref[...] + b_ref[...]) + (c_ref[...] + d_ref[...])
    out_ref[size:] = ext_ref[...]


def add_parts(parts, ext):
    return pl.pallas_call(
        add_parts_kernel,
        out_shape=jax.ShapeDtypeStruct((parts[0].shape[0] + ext.shape[0], 128), F32),
        in_specs=[WHOLE] * 5,
        out_specs=WHOLE,
        compiler_params=params(8),
        name="add_parts",
    )(*parts, ext)


def across_kernel(a_ref, b_ref, c_ref, d_ref, out_ref, ext_ref):
    size = out_ref.shape[0]
    grams = ext_ref.shape[0] - ROWS
    refs = (a_ref, b_ref, c_ref, d_ref)
    peaks = [r[size + grams : size + grams + 1, :1] for r in refs]
    top = jnp.maximum(jnp.maximum(peaks[0], peaks[1]), jnp.maximum(peaks[2], peaks[3]))
    a, b, c, d = (r[:size] * (k / top) for r, k in zip(refs, peaks))
    out_ref[...] = (a + b) + (c + d)
    a, b, c, d = (r[size : size + grams] for r in refs)
    ext_ref[:grams] = (a + b) + (c + d)
    ext_ref[grams:] = jnp.broadcast_to(top, (ROWS, 128))


def across(parts, extra):
    return pl.pallas_call(
        across_kernel,
        out_shape=[
            jax.ShapeDtypeStruct((parts[0].shape[0] - extra, 128), F32),
            pltpu.VMEM((extra, 128), F32),
        ],
        in_specs=[WHOLE] * 4,
        out_specs=[WHOLE] * 2,
        compiler_params=params(8),
        name="across",
    )(*parts)


def assemble_kernel(a_ref, b_ref, c_ref, d_ref, after_ref, out_ref):
    del after_ref
    size = a_ref.shape[0]
    for k, ref in zip((0,) + SHIFTS, (a_ref, b_ref, c_ref, d_ref)):
        at = pl.multiple_of((place()[2] + QUARTERS - k) % QUARTERS * size, size)
        out_ref[pl.ds(at, size)] = ref[...]


def assemble(parts, after):
    return pl.pallas_call(
        assemble_kernel,
        out_shape=jax.ShapeDtypeStruct((parts[0].shape[0] * QUARTERS, 128), F32),
        in_specs=[WHOLE] * 4 + [ANY],
        out_specs=WHOLE,
        compiler_params=params(8),
        name="assemble",
    )(*parts, after)


def factor_kernel(replicas, ext_ref, p_ref, solve_ref, hat_ref):
    rank = p_ref.shape[0]
    groups = rank // ROWS
    sub = lax.broadcasted_iota(jnp.int32, (ROWS, 2 * rank), 0)
    lane = lax.broadcasted_iota(jnp.int32, (ROWS, 2 * rank), 1)
    blocks = []
    for g in range(groups):
        tile = ext_ref[g // 2 * ROWS : (g // 2 + 1) * ROWS, (g % 2) * rank : (g % 2 + 1) * rank]
        unit = jnp.where(lane[:, :rank] == sub[:, :rank] + g * ROWS, 1.0, 0.0)
        blocks.append(jnp.concatenate([tile, unit], axis=1))
    for own in range(groups):
        spread = lambda g: [
            jnp.broadcast_to(blocks[g][:, own * ROWS + k : own * ROWS + k + 1], (ROWS, 2 * rank))
            for k in range(ROWS)
        ]
        columns = spread(own)
        rows, heads = [], []
        for k in range(ROWS):
            scale = 1.0 / columns[k][k : k + 1]
            row = blocks[own][k : k + 1] * scale
            head = {m: columns[m][k : k + 1] * scale for m in range(k + 1, ROWS)}
            factors = jnp.where(sub > k, columns[k], 0.0)
            blocks[own] = blocks[own] - factors * row
            for m, h in head.items():
                columns[m] = columns[m] - factors * h
            rows.append(row)
            heads.append(head)
        for g in range(own + 1, groups):
            columns = spread(g)
            for k in range(ROWS):
                blocks[g] = blocks[g] - columns[k] * rows[k]
                for m, h in heads[k].items():
                    columns[m] = columns[m] - columns[k] * h
    inverse = []
    for g in range(groups):
        diagonal = jnp.sum(
            jnp.where(lane == sub + g * ROWS, blocks[g], 0.0), axis=1, keepdims=True
        )
        inverse.append(blocks[g][:, rank:] / jnp.sqrt(diagonal))
    inverse = jnp.concatenate(inverse, axis=0)
    grams = ext_ref.shape[0] - ROWS
    solve_ref[...] = inverse * (ext_ref[grams : grams + 1, :1] * (1.0 / replicas))
    hat_ref[...] = jnp.dot(inverse, p_ref[...], precision=HIGHEST, preferred_element_type=F32)


def factor(ext, p_mean, replicas):
    rank, rows = p_mean.shape
    return pl.pallas_call(
        functools.partial(factor_kernel, replicas),
        out_shape=[
            jax.ShapeDtypeStruct((rank, rank), F32),
            jax.ShapeDtypeStruct((rank, rows), F32),
        ],
        in_specs=[WHOLE] * 2,
        out_specs=[WHOLE] * 2,
        compiler_params=params(8),
        cost_estimate=cost(1 << 32, 1 << 20),
        name="factor",
    )(ext, p_mean)


def result_kernel(sources, last, width, solve_ref, p_ref, m_ref, *refs):
    if last:
        hat_hbm, refs = refs[-4], refs[:-4] + refs[-3:]
        hat = pltpu.make_async_copy(p_ref, hat_hbm, refs[-1].at[0, len(sources)])
        hat.start()
    error_hbm, q_hbm, token_ref, error_ref, q_ref, sems = refs[-6:]
    token_ref[...] = jnp.zeros_like(token_ref)
    rank = solve_ref.shape[0]
    columns = q_ref.shape[2]
    left = p_ref[...].T.astype(BF16)
    s1, s2, s3 = split(solve_ref[...])
    solve = jnp.concatenate([s1, s1, s2, s2, s1, s3], axis=1)

    def copies(n, base, at, size):
        to, here = pl.ds(pl.multiple_of(base + at, 128), size), pl.ds(at, size)
        return (
            pltpu.make_async_copy(error_ref.at[n, :, here], error_hbm.at[:, to], sems.at[0, n]),
            pltpu.make_async_copy(q_ref.at[n, :, here], q_hbm.at[:, to], sems.at[1, n]),
        )

    bases = []
    for n, (own, k) in enumerate(sources):
        t_ref = refs[n]
        core, one, two = place()
        core, turn = (core, one) if own else (1 - core, two)
        quarter = (turn + QUARTERS - k) % QUARTERS
        base = (core * QUARTERS + quarter) * columns
        bases.append(base)
        for at in range(0, columns, width):
            t = jnp.concatenate(
                [
                    jnp.concatenate(
                        [
                            t_ref[(g * columns + i) // 128 * ROWS : (g * columns + i) // 128 * ROWS + ROWS, :]
                            for i in range(at, at + width, 128)
                        ],
                        axis=1,
                    )
                    for g in range(rank // ROWS)
                ],
                axis=0,
            )
            t1, t2, t3 = split(t)
            t = jnp.concatenate([t1, t2, t1, t2, t3, t1], axis=0)
            new = jnp.dot(solve, t, preferred_element_type=F32)
            q_ref[n, :, at : at + width] = new
            decoded = jnp.dot(left, new.astype(BF16), preferred_element_type=F32)
            m = m_ref[:, pl.ds(pl.multiple_of(base + at, 128), width)]
            error_ref[n, :, at : at + width] = (m.astype(F32) - decoded).astype(BF16)
            for c in copies(n, base, at, width):
                c.start()
    for n, base in enumerate(bases):
        for c in copies(n, base, 0, columns):
            c.wait()
    if last:
        hat.wait()


def result(sources, last, totals, merged, solve, p_hat, before):
    rank = solve.shape[0]
    rows, columns = merged.shape
    quarter = columns // 2 // QUARTERS
    n = len(sources)
    held = [] if before is None else list(before)
    return pl.pallas_call(
        functools.partial(result_kernel, sources, last, quarter // 2),
        out_shape=[
            pltpu.HBM((rows, columns), BF16),
            pltpu.HBM((rank, columns), F32),
            pltpu.VMEM((ROWS, 128), F32),
        ]
        + [pltpu.HBM(p_hat.shape, F32)] * last,
        in_specs=[WHOLE] * (3 + n) + [ANY] * len(held),
        out_specs=[ANY, ANY, WHOLE] + [ANY] * last,
        scratch_shapes=[
            pltpu.VMEM((n, rows, quarter), BF16),
            pltpu.VMEM((n, rank, quarter), F32),
            pltpu.SemaphoreType.DMA((2, n + 1)),
        ],
        input_output_aliases={3 + n + i: i for i in range(len(held))},
        compiler_params=params(12),
        cost_estimate=cost(1<<33, 1<<20),
        name="result",
    )(solve, p_hat, merged, *totals, *held)


def tie_kernel(value_ref, after_ref, out_ref):
    del value_ref, after_ref, out_ref


def tie(value, after):
    return pl.pallas_call(
        tie_kernel,
        out_shape=jax.ShapeDtypeStruct(value.shape, value.dtype),
        in_specs=[ANY] * 2,
        out_specs=ANY,
        input_output_aliases={0: 0},
        compiler_params=params(4),
        name="tie",
    )(value, after)


def body(gradient, error, q_start):
    rank = q_start.shape[0]
    replicas = SIZES[0] * SIZES[1]
    merged, p = merge(gradient[0], error[0], q_start)
    a, b, c = ring_x_or_z([p] * 3, 0)
    p = (p + a) + (b + c)
    sent, ext, p_mean, pieces = first_right(
        (p, *ring_x_or_z([p] * 3, 1)), merged, rank, replicas
    )
    got = swap(sent)
    kept = second_right(pieces, merged)
    own, *sent, ext = pair(kept, got, ext)
    own, *sent = add_quarters((own, *ring_x_or_z(sent, 0)))
    part = add_parts((own, *ring_x_or_z(sent, 1)), ext)
    total, ext = across((part, *ring_y(part)), ext.shape[0])
    solve, p_hat = factor(ext, p_mean, replicas)
    total = assemble((total, *ring_x_or_z([total] * 3, 1)), solve)
    one, three, two = ring_x_or_z([total] * 3, 0)

    def write(sources, totals, before, last=False):
        return result(sources, last, totals, merged, solve, p_hat, before)

    *out, token = write(((True, 0), (False, 0)), (total, swap(total)), None)
    one, three = tie(one, token), tie(three, token)
    *out, _ = write(((True, 1), (True, 3)), (one, three), out)
    *out, token = write(((False, 1), (False, 3)), (swap(one), swap(three)), out)
    two = tie(two, token)
    *out, _ = write(((True, 2),), (two,), out)
    new_error, q_new, _, p_hat = write(((False, 2),), (swap(two),), out, True)
    return (new_error[None], p_hat, q_new)


def solution(mesh):
    fine = Mesh(mesh.devices.reshape(SIZES), AXES)
    return jax.shard_map(
        body,
        mesh=fine,
        in_specs=(P(DP, ("y", "c"), None), P(DP, ("y", "c"), None), P()),
        out_specs=(P(DP, ("y", "c"), None), P(None, ("y", "c")), P()),
        check_vma=False,
    )
```

```python
import functools

import jax
import jax.numpy as jnp
from jax import lax
from jax.experimental import pallas as pl
from jax.experimental.pallas import tpu as pltpu
from jax.sharding import Mesh, PartitionSpec as P

DP = ("z", "x")
AXES = ("z", "x", "y", "c")
SIZES = (4, 4, 4, 2)
HIGHEST = lax.Precision.HIGHEST
F32 = jnp.float32
BF16 = jnp.bfloat16
MIB = 1 << 20
ROWS = 8
QUARTERS = 4
SHIFTS = (1, 3, 2)
ANY = pl.BlockSpec(memory_space=pl.ANY)
WHOLE = pl.BlockSpec(memory_space=pltpu.VMEM)


def params(mib):
    return pltpu.CompilerParams(vmem_limit_bytes=mib * MIB)


def cost(flops, nbytes):
    return pl.CostEstimate(flops=flops, bytes_accessed=nbytes, transcendentals=0)


def place():
    core, x, z = (lax.axis_index(a) for a in ("c", "x", "z"))
    return core, jnp.where(core == 0, x, z), jnp.where(core == 0, z, x)


def index(z, x, y, c):
    return ((z * SIZES[1] + x) * SIZES[2] + y) * SIZES[3] + c


def everyone():
    return [
        (z, x, y, c)
        for z in range(SIZES[0])
        for x in range(SIZES[1])
        for y in range(SIZES[2])
        for c in range(SIZES[3])
    ]


def ring_x_or_z(values, phase, shifts=SHIFTS):
    out = []
    for k, value in zip(shifts, values):
        pairs = []
        for z, x, y, c in everyone():
            to = (z, (x + k) % SIZES[1], y, c) if c == phase else ((z + k) % SIZES[0], x, y, c)
            pairs.append((index(z, x, y, c), index(*to)))
        out.append(lax.ppermute(value, AXES, pairs))
    return out


def ring_y(value):
    n = SIZES[2]
    return [lax.ppermute(value, "y", [(i, (i + k) % n) for i in range(n)]) for k in SHIFTS]


def swap(value):
    return lax.ppermute(value, "c", [(0, 1), (1, 0)])


def merge_kernel(width, g_hbm, e_hbm, q_hbm, m_ref, p_ref, g_ref, e_ref, q_ref, sems):
    rows, columns = g_ref.shape
    rank = q_ref.shape[0]
    steps = columns // width

    def copies(i):
        at = pl.ds(i * width, width)
        return [
            pltpu.make_async_copy(src.at[:, at], dst.at[:, at], sems.at[n, i])
            for n, (src, dst) in enumerate(((g_hbm, g_ref), (e_hbm, e_ref), (q_hbm, q_ref)))
        ]

    for i in range(steps):
        for c in copies(i):
            c.start()
    acc = jnp.zeros((rows, rank), F32)
    for i in range(steps):
        for c in copies(i):
            c.wait()
        at = pl.ds(i * width, width)
        m = (g_ref[:, at].astype(F32) + e_ref[:, at].astype(F32)).astype(BF16)
        m_ref[:, at] = m
        acc = acc + lax.dot_general(
            m, q_ref[:, at], (((1,), (1,)), ((), ())), preferred_element_type=F32
        )
    p_ref[...] = pack(acc.T)


def pack(p):
    rank, rows = p.shape
    full = rows // 128
    half = rank // 2
    parts = [p[:, i * 128 : (i + 1) * 128] for i in range(full)]
    rest = p[:, full * 128 :]
    return jnp.concatenate(parts + [jnp.concatenate([rest[:half], rest[half:]], axis=1)], axis=0)


def unpack(packed, rank):
    full = packed.shape[0] // rank
    last = packed[full * rank :]
    rest = jnp.concatenate([last[:, :64], last[:, 64:]], axis=0)
    return jnp.concatenate(
        [packed[i * rank : (i + 1) * rank] for i in range(full)] + [rest], axis=1
    )


def merge(gradient, error, q_start):
    rows, columns = gradient.shape
    rank = q_start.shape[0]
    width = 1024
    gradient, error, q_start = (
        pltpu.with_memory_space_constraint(a, pltpu.HBM) for a in (gradient, error, q_start)
    )
    return pl.pallas_call(
        functools.partial(merge_kernel, width),
        out_shape=[pltpu.VMEM((rows, columns), BF16), pltpu.VMEM((rank * rows // 128, 128), F32)],
        in_specs=[ANY, ANY, ANY],
        out_specs=[WHOLE, WHOLE],
        scratch_shapes=[
            pltpu.VMEM((rows, columns), BF16),
            pltpu.VMEM((rows, columns), BF16),
            pltpu.VMEM((rank, columns), BF16),
            pltpu.SemaphoreType.DMA((3, columns // width)),
        ],
        compiler_params=params(24),
        cost_estimate=cost(2 * rank * rows * columns, 4 * rows * columns),
        name="merge",
    )(gradient, error, q_start)


def right_tiles(half, pieces, m_ref, out_ref):
    rank = pieces.shape[0] // 3
    width = m_ref.shape[1] // 2 // QUARTERS
    size = rank * width // 128

    def step(a, carry):
        at = pl.multiple_of((half * QUARTERS + a) * width, width)
        t = jnp.dot(pieces, m_ref[:, pl.ds(at, width)], preferred_element_type=F32)
        t = t[:rank] + (t[rank : 2 * rank] + t[2 * rank :])
        to = 0
        for g in range(rank // ROWS):
            for n in range(width // 128):
                here = pl.ds(pl.multiple_of(a * size + to, ROWS), ROWS)
                out_ref[here, :] = t[g * ROWS : (g + 1) * ROWS, n * 128 : (n + 1) * 128]
                to += ROWS
        return carry

    lax.fori_loop(0, QUARTERS, step, 0, unroll=2)


def split(n):
    high = n.astype(BF16)
    n = n - high.astype(F32)
    middle = n.astype(BF16)
    return high, middle, (n - middle.astype(F32)).astype(BF16)


def first_right_kernel(replicas, rank, a_ref, b_ref, c_ref, d_ref, m_ref, out_ref, ext_ref, p_ref, pieces_ref):
    p = (a_ref[...] + b_ref[...] + (c_ref[...] + d_ref[...])) * (1.0 / replicas)
    peak = jnp.max(jnp.abs(p), axis=(0, 1), keepdims=True)
    peak = jnp.where(peak > 0, peak, 1.0)
    p = unpack(p, rank)
    p_ref[...] = p
    gram = lax.dot_general(
        p, p, (((1,), (1,)), ((), ())), precision=HIGHEST, preferred_element_type=F32
    )
    two = 2 * ROWS
    ext = jnp.concatenate(
        [
            jnp.concatenate([gram[i : i + ROWS], gram[i + ROWS : i + two]], axis=1)
            for i in range(0, rank, two)
        ]
        + [jnp.broadcast_to(peak, (ROWS, 128))],
        axis=0,
    )
    ext_ref[...] = ext
    out_ref[out_ref.shape[0] - ext.shape[0] :, :] = ext
    pieces = jnp.concatenate(split(p / peak), axis=0)
    pieces_ref[...] = pieces
    right_tiles(1 - place()[0], pieces, m_ref, out_ref)


def second_right_kernel(pieces_ref, m_ref, out_ref):
    right_tiles(place()[0], pieces_ref[...], m_ref, out_ref)


def first_right(parts, merged, rank, replicas):
    rows, columns = merged.shape
    size = rank * columns // 256
    extra = rank * rank // 128 + ROWS
    return pl.pallas_call(
        functools.partial(first_right_kernel, replicas, rank),
        out_shape=[
            jax.ShapeDtypeStruct((size + extra, 128), F32),
            pltpu.VMEM((extra, 128), F32),
            pltpu.VMEM((rank, rows), F32),
            pltpu.VMEM((3 * rank, rows), BF16),
        ],
        in_specs=[WHOLE] * 5,
        out_specs=[WHOLE] * 4,
        compiler_params=params(12),
        cost_estimate=cost(3 * rank * rows * columns, 512 * size),
        name="first_right",
    )(*parts, merged)


def second_right(pieces, merged):
    size = pieces.shape[0] // 3 * merged.shape[1] // 256
    return pl.pallas_call(
        second_right_kernel,
        out_shape=pltpu.VMEM((size, 128), F32),
        in_specs=[WHOLE, WHOLE],
        out_specs=WHOLE,
        compiler_params=params(12),
        cost_estimate=cost(pieces.shape[0] * merged.size, 512 * size),
        name="second_right",
    )(pieces, merged)


def pair_kernel(kept_ref, got_ref, ext_ref, *out):
    pair_ref = out[-1]
    grams = ext_ref.shape[0] - ROWS
    ext = kept_ref.shape[0]
    size = ext // QUARTERS
    own, its = ext_ref[grams : grams + 1, :1], got_ref[ext + grams : ext + grams + 1, :1]
    top = jnp.maximum(own, its)
    pair_ref[:grams] = ext_ref[:grams] + got_ref[ext : ext + grams]
    pair_ref[grams:] = jnp.broadcast_to(top, (ROWS, 128))
    own, its = own / top, its / top
    for k, ref in zip((0,) + SHIFTS, out):
        at = pl.ds(pl.multiple_of((place()[1] + k) % QUARTERS * size, size), size)
        ref[...] = kept_ref[at] * own + got_ref[at] * its


def pair(kept, got, ext):
    size = kept.shape[0] // QUARTERS
    return pl.pallas_call(
        pair_kernel,
        out_shape=[jax.ShapeDtypeStruct((size, 128), F32)] * QUARTERS
        + [pltpu.VMEM(ext.shape, F32)],
        in_specs=[WHOLE] * 3,
        out_specs=[WHOLE] * (QUARTERS + 1),
        compiler_params=params(8),
        name="pair",
    )(kept, got, ext)


def add_quarters_kernel(a_ref, b_ref, c_ref, d_ref, *out):
    size = a_ref.shape[0] // QUARTERS
    for k, ref in zip((0,) + SHIFTS, out):
        at = pl.ds(pl.multiple_of((place()[2] + k) % QUARTERS * size, size), size)
        ref[...] = (a_ref[at] + b_ref[at]) + (c_ref[at] + d_ref[at])


def add_quarters(parts):
    size = parts[0].shape[0] // QUARTERS
    return pl.pallas_call(
        add_quarters_kernel,
        out_shape=[jax.ShapeDtypeStruct((size, 128), F32)] * QUARTERS,
        in_specs=[WHOLE] * QUARTERS,
        out_specs=[WHOLE] * QUARTERS,
        compiler_params=params(8),
        name="add_quarters",
    )(*parts)


def add_parts_kernel(a_ref, b_ref, c_ref, d_ref, ext_ref, out_ref):
    size = a_ref.shape[0]
    out_ref[:size] = (a_ref[...] + b_ref[...]) + (c_ref[...] + d_ref[...])
    out_ref[size:] = ext_ref[...]


def add_parts(parts, ext):
    return pl.pallas_call(
        add_parts_kernel,
        out_shape=jax.ShapeDtypeStruct((parts[0].shape[0] + ext.shape[0], 128), F32),
        in_specs=[WHOLE] * 5,
        out_specs=WHOLE,
        compiler_params=params(8),
        name="add_parts",
    )(*parts, ext)


def across_kernel(a_ref, b_ref, c_ref, d_ref, out_ref, ext_ref):
    size = out_ref.shape[0]
    grams = ext_ref.shape[0] - ROWS
    refs = (a_ref, b_ref, c_ref, d_ref)
    peaks = [r[size + grams : size + grams + 1, :1] for r in refs]
    top = jnp.maximum(jnp.maximum(peaks[0], peaks[1]), jnp.maximum(peaks[2], peaks[3]))
    a, b, c, d = (r[:size] * (k / top) for r, k in zip(refs, peaks))
    out_ref[...] = (a + b) + (c + d)
    a, b, c, d = (r[size : size + grams] for r in refs)
    ext_ref[:grams] = (a + b) + (c + d)
    ext_ref[grams:] = jnp.broadcast_to(top, (ROWS, 128))


def across(parts, extra):
    return pl.pallas_call(
        across_kernel,
        out_shape=[
            jax.ShapeDtypeStruct((parts[0].shape[0] - extra, 128), F32),
            pltpu.VMEM((extra, 128), F32),
        ],
        in_specs=[WHOLE] * 4,
        out_specs=[WHOLE] * 2,
        compiler_params=params(8),
        name="across",
    )(*parts)


def assemble_kernel(a_ref, b_ref, c_ref, d_ref, after_ref, out_ref):
    del after_ref
    size = a_ref.shape[0]
    for k, ref in zip((0,) + SHIFTS, (a_ref, b_ref, c_ref, d_ref)):
        at = pl.multiple_of((place()[2] + QUARTERS - k) % QUARTERS * size, size)
        out_ref[pl.ds(at, size)] = ref[...]


def assemble(parts, after):
    return pl.pallas_call(
        assemble_kernel,
        out_shape=jax.ShapeDtypeStruct((parts[0].shape[0] * QUARTERS, 128), F32),
        in_specs=[WHOLE] * 4 + [ANY],
        out_specs=WHOLE,
        compiler_params=params(8),
        name="assemble",
    )(*parts, after)


def factor_kernel(replicas, ext_ref, p_ref, solve_ref, hat_ref):
    rank = p_ref.shape[0]
    groups = rank // ROWS
    sub = lax.broadcasted_iota(jnp.int32, (ROWS, 2 * rank), 0)
    lane = lax.broadcasted_iota(jnp.int32, (ROWS, 2 * rank), 1)
    blocks = []
    for g in range(groups):
        tile = ext_ref[g // 2 * ROWS : (g // 2 + 1) * ROWS, (g % 2) * rank : (g % 2 + 1) * rank]
        unit = jnp.where(lane[:, :rank] == sub[:, :rank] + g * ROWS, 1.0, 0.0)
        blocks.append(jnp.concatenate([tile, unit], axis=1))
    for own in range(groups):
        spread = lambda g: [
            jnp.broadcast_to(blocks[g][:, own * ROWS + k : own * ROWS + k + 1], (ROWS, 2 * rank))
            for k in range(ROWS)
        ]
        columns = spread(own)
        rows, heads = [], []
        for k in range(ROWS):
            scale = 1.0 / columns[k][k : k + 1]
            row = blocks[own][k : k + 1] * scale
            head = {m: columns[m][k : k + 1] * scale for m in range(k + 1, ROWS)}
            factors = jnp.where(sub > k, columns[k], 0.0)
            blocks[own] = blocks[own] - factors * row
            for m, h in head.items():
                columns[m] = columns[m] - factors * h
            rows.append(row)
            heads.append(head)
        for g in range(own + 1, groups):
            columns = spread(g)
            for k in range(ROWS):
                blocks[g] = blocks[g] - columns[k] * rows[k]
                for m, h in heads[k].items():
                    columns[m] = columns[m] - columns[k] * h
    inverse = []
    for g in range(groups):
        diagonal = jnp.sum(
            jnp.where(lane == sub + g * ROWS, blocks[g], 0.0), axis=1, keepdims=True
        )
        inverse.append(blocks[g][:, rank:] / jnp.sqrt(diagonal))
    inverse = jnp.concatenate(inverse, axis=0)
    grams = ext_ref.shape[0] - ROWS
    solve_ref[...] = inverse * (ext_ref[grams : grams + 1, :1] * (1.0 / replicas))
    hat_ref[...] = jnp.dot(inverse, p_ref[...], precision=HIGHEST, preferred_element_type=F32)


def factor(ext, p_mean, replicas):
    rank, rows = p_mean.shape
    return pl.pallas_call(
        functools.partial(factor_kernel, replicas),
        out_shape=[
            jax.ShapeDtypeStruct((rank, rank), F32),
            jax.ShapeDtypeStruct((rank, rows), F32),
        ],
        in_specs=[WHOLE] * 2,
        out_specs=[WHOLE] * 2,
        compiler_params=params(8),
        cost_estimate=cost(1 << 32, 1 << 20),
        name="factor",
    )(ext, p_mean)


def result_kernel(sources, last, width, solve_ref, p_ref, m_ref, *refs):
    if last:
        hat_hbm, refs = refs[-4], refs[:-4] + refs[-3:]
        hat = pltpu.make_async_copy(p_ref, hat_hbm, refs[-1].at[0, len(sources)])
        hat.start()
    error_hbm, q_hbm, token_ref, error_ref, q_ref, sems = refs[-6:]
    token_ref[...] = jnp.zeros_like(token_ref)
    rank = solve_ref.shape[0]
    columns = q_ref.shape[2]
    left = p_ref[...].T.astype(BF16)
    s1, s2, s3 = split(solve_ref[...])
    solve = jnp.concatenate([s1, s1, s2, s2, s1, s3], axis=1)

    def copies(n, base, at, size):
        to, here = pl.ds(pl.multiple_of(base + at, 128), size), pl.ds(at, size)
        return (
            pltpu.make_async_copy(error_ref.at[n, :, here], error_hbm.at[:, to], sems.at[0, n]),
            pltpu.make_async_copy(q_ref.at[n, :, here], q_hbm.at[:, to], sems.at[1, n]),
        )

    bases = []
    for n, (own, k) in enumerate(sources):
        t_ref = refs[n]
        core, one, two = place()
        core, turn = (core, one) if own else (1 - core, two)
        quarter = (turn + QUARTERS - k) % QUARTERS
        base = (core * QUARTERS + quarter) * columns
        bases.append(base)
        for at in range(0, columns, width):
            t = jnp.concatenate(
                [
                    jnp.concatenate(
                        [
                            t_ref[(g * columns + i) // 128 * ROWS : (g * columns + i) // 128 * ROWS + ROWS, :]
                            for i in range(at, at + width, 128)
                        ],
                        axis=1,
                    )
                    for g in range(rank // ROWS)
                ],
                axis=0,
            )
            t1, t2, t3 = split(t)
            t = jnp.concatenate([t1, t2, t1, t2, t3, t1], axis=0)
            new = jnp.dot(solve, t, preferred_element_type=F32)
            q_ref[n, :, at : at + width] = new
            decoded = jnp.dot(left, new.astype(BF16), preferred_element_type=F32)
            m = m_ref[:, pl.ds(pl.multiple_of(base + at, 128), width)]
            error_ref[n, :, at : at + width] = (m.astype(F32) - decoded).astype(BF16)
            for c in copies(n, base, at, width):
                c.start()
    for n, base in enumerate(bases):
        for c in copies(n, base, 0, columns):
            c.wait()
    if last:
        hat.wait()


def result(sources, last, totals, merged, solve, p_hat, before):
    rank = solve.shape[0]
    rows, columns = merged.shape
    quarter = columns // 2 // QUARTERS
    n = len(sources)
    held = [] if before is None else list(before)
    return pl.pallas_call(
        functools.partial(result_kernel, sources, last, quarter // 2),
        out_shape=[
            pltpu.HBM((rows, columns), BF16),
            pltpu.HBM((rank, columns), F32),
            pltpu.VMEM((ROWS, 128), F32),
        ]
        + [pltpu.HBM(p_hat.shape, F32)] * last,
        in_specs=[WHOLE] * (3 + n) + [ANY] * len(held),
        out_specs=[ANY, ANY, WHOLE] + [ANY] * last,
        scratch_shapes=[
            pltpu.VMEM((n, rows, quarter), BF16),
            pltpu.VMEM((n, rank, quarter), F32),
            pltpu.SemaphoreType.DMA((2, n + 1)),
        ],
        input_output_aliases={3 + n + i: i for i in range(len(held))},
        compiler_params=params(12),
        cost_estimate=cost(1<<33, 1<<20),
        name="result",
    )(solve, p_hat, merged, *totals, *held)


def halves_kernel(a_ref, b_ref, after_ref, low_ref, high_ref):
    del after_ref
    half = low_ref.shape[0]
    low_ref[...] = a_ref[:half]
    high_ref[...] = b_ref[half:]


def halves(a, b, after):
    return pl.pallas_call(
        halves_kernel,
        out_shape=[jax.ShapeDtypeStruct((a.shape[0] // 2, 128), F32)] * 2,
        in_specs=[WHOLE, WHOLE, ANY],
        out_specs=[WHOLE, WHOLE],
        compiler_params=params(4),
        name="halves",
    )(a, b, after)


def join_kernel(low_ref, high_ref, after_ref, out_ref):
    del after_ref
    half = low_ref.shape[0]
    out_ref[:half] = low_ref[...]
    out_ref[half:] = high_ref[...]


def join(low, high, after):
    return pl.pallas_call(
        join_kernel,
        out_shape=jax.ShapeDtypeStruct((low.shape[0] * 2, 128), F32),
        in_specs=[WHOLE, WHOLE, ANY],
        out_specs=WHOLE,
        compiler_params=params(4),
        name="join",
    )(low, high, after)


def tie_kernel(value_ref, after_ref, out_ref):
    del value_ref, after_ref, out_ref


def tie(value, after):
    return pl.pallas_call(
        tie_kernel,
        out_shape=jax.ShapeDtypeStruct(value.shape, value.dtype),
        in_specs=[ANY] * 2,
        out_specs=ANY,
        input_output_aliases={0: 0},
        compiler_params=params(4),
        name="tie",
    )(value, after)


def body(gradient, error, q_start):
    rank = q_start.shape[0]
    replicas = SIZES[0] * SIZES[1]
    merged, p = merge(gradient[0], error[0], q_start)
    a, b, c = ring_x_or_z([p] * 3, 0)
    p = (p + a) + (b + c)
    sent, ext, p_mean, pieces = first_right(
        (p, *ring_x_or_z([p] * 3, 1)), merged, rank, replicas
    )
    got = swap(sent)
    kept = second_right(pieces, merged)
    own, *sent, ext = pair(kept, got, ext)
    own, *sent = add_quarters((own, *ring_x_or_z(sent, 0)))
    part = add_parts((own, *ring_x_or_z(sent, 1)), ext)
    total, ext = across((part, *ring_y(part)), ext.shape[0])
    solve, p_hat = factor(ext, p_mean, replicas)
    total = assemble((total, *ring_x_or_z([total] * 3, 1)), solve)
    one, three = ring_x_or_z([total] * 2, 0, (1, 3))

    def write(sources, totals, before, last=False):
        return result(sources, last, totals, merged, solve, p_hat, before)

    *out, token = write(((True, 0), (False, 0)), (total, swap(total)), None)
    low, high = ring_x_or_z(halves(one, three, token), 0, (1, 3))
    one, three = tie(one, token), tie(three, token)
    *out, _ = write(((True, 1), (True, 3)), (one, three), out)
    *out, token = write(((False, 1), (False, 3)), (swap(one), swap(three)), out)
    two = join(low, high, token)
    *out, _ = write(((True, 2),), (two,), out)
    new_error, q_new, _, p_hat = write(((False, 2),), (swap(two),), out, True)
    return (new_error[None], p_hat, q_new)


def solution(mesh):
    fine = Mesh(mesh.devices.reshape(SIZES), AXES)
    return jax.shard_map(
        body,
        mesh=fine,
        in_specs=(P(DP, ("y", "c"), None), P(DP, ("y", "c"), None), P()),
        out_specs=(P(DP, ("y", "c"), None), P(None, ("y", "c")), P()),
        check_vma=False,
    )
```

```python
import functools

import jax
import jax.numpy as jnp
from jax import lax
from jax.experimental import pallas as pl
from jax.experimental.pallas import tpu as pltpu
from jax.sharding import Mesh, PartitionSpec as P

DP = ("z", "x")
AXES = ("z", "x", "y", "c")
SIZES = (4, 4, 4, 2)
HIGHEST = lax.Precision.HIGHEST
F32 = jnp.float32
BF16 = jnp.bfloat16
MIB = 1 << 20
ROWS = 8
QUARTERS = 4
RIGHT = 1 << 33
SHIFTS = (1, 3, 2)
ANY = pl.BlockSpec(memory_space=pl.ANY)
WHOLE = pl.BlockSpec(memory_space=pltpu.VMEM)


def params(mib):
    return pltpu.CompilerParams(vmem_limit_bytes=mib * MIB)


def cost(flops, nbytes):
    return pl.CostEstimate(flops=flops, bytes_accessed=nbytes, transcendentals=0)


def place():
    core, x, z = (lax.axis_index(a) for a in ("c", "x", "z"))
    return core, jnp.where(core == 0, x, z), jnp.where(core == 0, z, x)


def index(z, x, y, c):
    return ((z * SIZES[1] + x) * SIZES[2] + y) * SIZES[3] + c


def everyone():
    return [
        (z, x, y, c)
        for z in range(SIZES[0])
        for x in range(SIZES[1])
        for y in range(SIZES[2])
        for c in range(SIZES[3])
    ]


def ring_x_or_z(values, phase, shifts=SHIFTS):
    out = []
    for k, value in zip(shifts, values):
        pairs = []
        for z, x, y, c in everyone():
            to = (z, (x + k) % SIZES[1], y, c) if c == phase else ((z + k) % SIZES[0], x, y, c)
            pairs.append((index(z, x, y, c), index(*to)))
        out.append(lax.ppermute(value, AXES, pairs))
    return out


def ring_y(value):
    n = SIZES[2]
    return [lax.ppermute(value, "y", [(i, (i + k) % n) for i in range(n)]) for k in SHIFTS]


def swap(value):
    return lax.ppermute(value, "c", [(0, 1), (1, 0)])


def merge_kernel(width, g_hbm, e_hbm, q_hbm, m_ref, p_ref, g_ref, e_ref, q_ref, sems):
    rows, columns = g_ref.shape
    rank = q_ref.shape[0]
    steps = columns // width

    def copies(i):
        at = pl.ds(i * width, width)
        return [
            pltpu.make_async_copy(src.at[:, at], dst.at[:, at], sems.at[n, i])
            for n, (src, dst) in enumerate(((g_hbm, g_ref), (e_hbm, e_ref), (q_hbm, q_ref)))
        ]

    for i in range(steps):
        for c in copies(i):
            c.start()
    acc = jnp.zeros((rows, rank), F32)
    for i in range(steps):
        for c in copies(i):
            c.wait()
        at = pl.ds(i * width, width)
        m = (g_ref[:, at].astype(F32) + e_ref[:, at].astype(F32)).astype(BF16)
        m_ref[:, at] = m
        acc = acc + lax.dot_general(
            m, q_ref[:, at], (((1,), (1,)), ((), ())), preferred_element_type=F32
        )
    p_ref[...] = pack(acc.T)


def pack(p):
    rank, rows = p.shape
    full = rows // 128
    half = rank // 2
    parts = [p[:, i * 128 : (i + 1) * 128] for i in range(full)]
    rest = p[:, full * 128 :]
    return jnp.concatenate(parts + [jnp.concatenate([rest[:half], rest[half:]], axis=1)], axis=0)


def unpack(packed, rank):
    full = packed.shape[0] // rank
    last = packed[full * rank :]
    rest = jnp.concatenate([last[:, :64], last[:, 64:]], axis=0)
    return jnp.concatenate(
        [packed[i * rank : (i + 1) * rank] for i in range(full)] + [rest], axis=1
    )


def merge(gradient, error, q_start):
    rows, columns = gradient.shape
    rank = q_start.shape[0]
    width = 1024
    gradient, error, q_start = (
        pltpu.with_memory_space_constraint(a, pltpu.HBM) for a in (gradient, error, q_start)
    )
    return pl.pallas_call(
        functools.partial(merge_kernel, width),
        out_shape=[pltpu.VMEM((rows, columns), BF16), pltpu.VMEM((rank * rows // 128, 128), F32)],
        in_specs=[ANY, ANY, ANY],
        out_specs=[WHOLE, WHOLE],
        scratch_shapes=[
            pltpu.VMEM((rows, columns), BF16),
            pltpu.VMEM((rows, columns), BF16),
            pltpu.VMEM((rank, columns), BF16),
            pltpu.SemaphoreType.DMA((3, columns // width)),
        ],
        compiler_params=params(24),
        cost_estimate=cost(2 * rank * rows * columns, 4 * rows * columns),
        name="merge",
    )(gradient, error, q_start)


def right_tiles(quarters, pieces, m_ref, out_ref):
    rank = pieces.shape[0] // 3
    width = m_ref.shape[1] // 2 // QUARTERS
    to = 0
    for quarter in quarters:
        at = pl.multiple_of(quarter * width, width)
        t = jnp.dot(pieces, m_ref[:, pl.ds(at, width)], preferred_element_type=F32)
        t = t[:rank] + (t[rank : 2 * rank] + t[2 * rank :])
        for g in range(rank // ROWS):
            for n in range(width // 128):
                out_ref[to : to + ROWS, :] = t[g * ROWS : (g + 1) * ROWS, n * 128 : (n + 1) * 128]
                to += ROWS


def quarters_of(own, turns):
    core, one, two = place()
    core, turn = (core, one) if own else (1 - core, two)
    return [core * QUARTERS + (turn + k) % QUARTERS for k in turns]


def split(n):
    high = n.astype(BF16)
    n = n - high.astype(F32)
    middle = n.astype(BF16)
    return high, middle, (n - middle.astype(F32)).astype(BF16)


def first_right_kernel(replicas, rank, turns, a_ref, b_ref, c_ref, d_ref, m_ref, out_ref, ext_ref, p_ref, pieces_ref):
    p = (a_ref[...] + b_ref[...] + (c_ref[...] + d_ref[...])) * (1.0 / replicas)
    peak = jnp.max(jnp.abs(p), axis=(0, 1), keepdims=True)
    peak = jnp.where(peak > 0, peak, 1.0)
    p = unpack(p, rank)
    p_ref[...] = p
    pieces = jnp.concatenate(split(p / peak), axis=0)
    pieces_ref[...] = pieces
    right_tiles(quarters_of(False, turns), pieces, m_ref, out_ref)
    gram = lax.dot_general(
        p, p, (((1,), (1,)), ((), ())), precision=HIGHEST, preferred_element_type=F32
    )
    two = 2 * ROWS
    ext = jnp.concatenate(
        [
            jnp.concatenate([gram[i : i + ROWS], gram[i + ROWS : i + two]], axis=1)
            for i in range(0, rank, two)
        ]
        + [jnp.broadcast_to(peak, (ROWS, 128))],
        axis=0,
    )
    ext_ref[...] = ext
    out_ref[out_ref.shape[0] - ext.shape[0] :, :] = ext


def next_right_kernel(own, turns, pieces_ref, m_ref, after_ref, out_ref):
    del after_ref
    right_tiles(quarters_of(own, turns), pieces_ref[...], m_ref, out_ref)


def first_right(turns, parts, merged, rank, replicas):
    rows, columns = merged.shape
    size = rank * columns // 1024
    extra = rank * rank // 128 + ROWS
    return pl.pallas_call(
        functools.partial(first_right_kernel, replicas, rank, turns),
        out_shape=[
            jax.ShapeDtypeStruct((size + extra, 128), F32),
            pltpu.VMEM((extra, 128), F32),
            pltpu.VMEM((rank, rows), F32),
            pltpu.VMEM((3 * rank, rows), BF16),
        ],
        in_specs=[WHOLE] * 5,
        out_specs=[WHOLE] * 4,
        compiler_params=params(12),
        cost_estimate=cost(RIGHT, 1 << 20),
        name="first_right",
    )(*parts, merged)


def next_right(own, turns, pieces, merged, after):
    size = pieces.shape[0] // 3 * merged.shape[1] // 1024 * len(turns)
    return pl.pallas_call(
        functools.partial(next_right_kernel, own, turns),
        out_shape=jax.ShapeDtypeStruct((size, 128), F32),
        in_specs=[WHOLE, WHOLE, ANY],
        out_specs=WHOLE,
        compiler_params=params(12),
        cost_estimate=cost(RIGHT, 1 << 20),
        name="next_right",
    )(pieces, merged, after)


def first_pair_kernel(kept_ref, got_ref, ext_ref, low_ref, high_ref, pair_ref, weight_ref):
    grams = ext_ref.shape[0] - ROWS
    size = kept_ref.shape[0]
    half = size // 2
    own, its = ext_ref[grams : grams + 1, :1], got_ref[size + grams : size + grams + 1, :1]
    top = jnp.maximum(own, its)
    pair_ref[:grams] = ext_ref[:grams] + got_ref[size : size + grams]
    pair_ref[grams:] = jnp.broadcast_to(top, (ROWS, 128))
    own, its = own / top, its / top
    weight_ref[:ROWS] = jnp.broadcast_to(own, (ROWS, 128))
    weight_ref[ROWS:] = jnp.broadcast_to(its, (ROWS, 128))
    low_ref[...] = kept_ref[:half] * own + got_ref[:half] * its
    high_ref[...] = kept_ref[half:] * own + got_ref[half:size] * its


def first_pair(kept, got, ext):
    half = jax.ShapeDtypeStruct((kept.shape[0] // 2, 128), F32)
    return pl.pallas_call(
        first_pair_kernel,
        out_shape=[half, half, pltpu.VMEM(ext.shape, F32), pltpu.VMEM((2 * ROWS, 128), F32)],
        in_specs=[WHOLE] * 3,
        out_specs=[WHOLE] * 4,
        compiler_params=params(8),
        name="first_pair",
    )(kept, got, ext)


def next_pair_kernel(kept_ref, got_ref, weight_ref, low_ref, high_ref, *out):
    own, its = weight_ref[:1, :1], weight_ref[ROWS : ROWS + 1, :1]
    size = out[0].shape[0]
    half = size // 2
    for n, ref in enumerate(out):
        for part in (0, 1):
            at = slice(n * size + part * half, n * size + (part + 1) * half)
            x = kept_ref[at] * own + got_ref[at] * its
            if (n, part) == (0, 0):
                x = x + low_ref[...]
            if (n, part) == (1, 1):
                x = x + high_ref[...]
            ref[part * half : (part + 1) * half] = x


def next_pair(kept, got, weight, low, high):
    size = kept.shape[0] // 3
    return pl.pallas_call(
        next_pair_kernel,
        out_shape=[jax.ShapeDtypeStruct((size, 128), F32)] * 3,
        in_specs=[WHOLE] * 5,
        out_specs=[WHOLE] * 3,
        compiler_params=params(8),
        name="next_pair",
    )(kept, got, weight, low, high)


def add_quarters_kernel(a_ref, b_ref, c_ref, *out):
    size = a_ref.shape[0] // QUARTERS
    for k, ref in zip((0,) + SHIFTS, out):
        at = pl.ds(pl.multiple_of((place()[2] + k) % QUARTERS * size, size), size)
        ref[...] = a_ref[at] + (b_ref[at] + c_ref[at])


def add_quarters(parts):
    size = parts[0].shape[0] // QUARTERS
    return pl.pallas_call(
        add_quarters_kernel,
        out_shape=[jax.ShapeDtypeStruct((size, 128), F32)] * QUARTERS,
        in_specs=[WHOLE] * 3,
        out_specs=[WHOLE] * QUARTERS,
        compiler_params=params(8),
        name="add_quarters",
    )(*parts)


def add_parts_kernel(a_ref, b_ref, c_ref, d_ref, ext_ref, out_ref):
    size = a_ref.shape[0]
    out_ref[:size] = (a_ref[...] + b_ref[...]) + (c_ref[...] + d_ref[...])
    out_ref[size:] = ext_ref[...]


def add_parts(parts, ext):
    return pl.pallas_call(
        add_parts_kernel,
        out_shape=jax.ShapeDtypeStruct((parts[0].shape[0] + ext.shape[0], 128), F32),
        in_specs=[WHOLE] * 5,
        out_specs=WHOLE,
        compiler_params=params(8),
        name="add_parts",
    )(*parts, ext)


def across_kernel(a_ref, b_ref, c_ref, d_ref, out_ref, ext_ref):
    size = out_ref.shape[0]
    grams = ext_ref.shape[0] - ROWS
    refs = (a_ref, b_ref, c_ref, d_ref)
    peaks = [r[size + grams : size + grams + 1, :1] for r in refs]
    top = jnp.maximum(jnp.maximum(peaks[0], peaks[1]), jnp.maximum(peaks[2], peaks[3]))
    a, b, c, d = (r[:size] * (k / top) for r, k in zip(refs, peaks))
    out_ref[...] = (a + b) + (c + d)
    a, b, c, d = (r[size : size + grams] for r in refs)
    ext_ref[:grams] = (a + b) + (c + d)
    ext_ref[grams:] = jnp.broadcast_to(top, (ROWS, 128))


def across(parts, extra):
    return pl.pallas_call(
        across_kernel,
        out_shape=[
            jax.ShapeDtypeStruct((parts[0].shape[0] - extra, 128), F32),
            pltpu.VMEM((extra, 128), F32),
        ],
        in_specs=[WHOLE] * 4,
        out_specs=[WHOLE] * 2,
        compiler_params=params(8),
        name="across",
    )(*parts)


def assemble_kernel(a_ref, b_ref, c_ref, d_ref, after_ref, out_ref):
    del after_ref
    size = a_ref.shape[0]
    for k, ref in zip((0,) + SHIFTS, (a_ref, b_ref, c_ref, d_ref)):
        at = pl.multiple_of((place()[2] + QUARTERS - k) % QUARTERS * size, size)
        out_ref[pl.ds(at, size)] = ref[...]


def assemble(parts, after):
    return pl.pallas_call(
        assemble_kernel,
        out_shape=jax.ShapeDtypeStruct((parts[0].shape[0] * QUARTERS, 128), F32),
        in_specs=[WHOLE] * 4 + [ANY],
        out_specs=WHOLE,
        compiler_params=params(8),
        name="assemble",
    )(*parts, after)


def factor_kernel(replicas, ext_ref, p_ref, solve_ref, hat_ref):
    rank = p_ref.shape[0]
    groups = rank // ROWS
    sub = lax.broadcasted_iota(jnp.int32, (ROWS, 2 * rank), 0)
    lane = lax.broadcasted_iota(jnp.int32, (ROWS, 2 * rank), 1)
    blocks = []
    for g in range(groups):
        tile = ext_ref[g // 2 * ROWS : (g // 2 + 1) * ROWS, (g % 2) * rank : (g % 2 + 1) * rank]
        unit = jnp.where(lane[:, :rank] == sub[:, :rank] + g * ROWS, 1.0, 0.0)
        blocks.append(jnp.concatenate([tile, unit], axis=1))
    for own in range(groups):
        spread = lambda g: [
            jnp.broadcast_to(blocks[g][:, own * ROWS + k : own * ROWS + k + 1], (ROWS, 2 * rank))
            for k in range(ROWS)
        ]
        columns = spread(own)
        rows, heads = [], []
        for k in range(ROWS):
            scale = 1.0 / columns[k][k : k + 1]
            row = blocks[own][k : k + 1] * scale
            head = {m: columns[m][k : k + 1] * scale for m in range(k + 1, ROWS)}
            factors = jnp.where(sub > k, columns[k], 0.0)
            blocks[own] = blocks[own] - factors * row
            for m, h in head.items():
                columns[m] = columns[m] - factors * h
            rows.append(row)
            heads.append(head)
        for g in range(own + 1, groups):
            columns = spread(g)
            for k in range(ROWS):
                blocks[g] = blocks[g] - columns[k] * rows[k]
                for m, h in heads[k].items():
                    columns[m] = columns[m] - columns[k] * h
    inverse = []
    for g in range(groups):
        diagonal = jnp.sum(
            jnp.where(lane == sub + g * ROWS, blocks[g], 0.0), axis=1, keepdims=True
        )
        inverse.append(blocks[g][:, rank:] / jnp.sqrt(diagonal))
    inverse = jnp.concatenate(inverse, axis=0)
    grams = ext_ref.shape[0] - ROWS
    solve_ref[...] = inverse * (ext_ref[grams : grams + 1, :1] * (1.0 / replicas))
    hat_ref[...] = jnp.dot(inverse, p_ref[...], precision=HIGHEST, preferred_element_type=F32)


def factor(ext, p_mean, replicas):
    rank, rows = p_mean.shape
    return pl.pallas_call(
        functools.partial(factor_kernel, replicas),
        out_shape=[
            jax.ShapeDtypeStruct((rank, rank), F32),
            jax.ShapeDtypeStruct((rank, rows), F32),
        ],
        in_specs=[WHOLE] * 2,
        out_specs=[WHOLE] * 2,
        compiler_params=params(8),
        cost_estimate=cost(1 << 32, 1 << 20),
        name="factor",
    )(ext, p_mean)


def result_kernel(sources, last, width, solve_ref, p_ref, m_ref, *refs):
    if last:
        hat_hbm, refs = refs[-4], refs[:-4] + refs[-3:]
        hat = pltpu.make_async_copy(p_ref, hat_hbm, refs[-1].at[0, len(sources)])
        hat.start()
    error_hbm, q_hbm, token_ref, error_ref, q_ref, sems = refs[-6:]
    token_ref[...] = jnp.zeros_like(token_ref)
    rank = solve_ref.shape[0]
    columns = q_ref.shape[2]
    left = p_ref[...].T.astype(BF16)
    s1, s2, s3 = split(solve_ref[...])
    solve = jnp.concatenate([s1, s1, s2, s2, s1, s3], axis=1)

    def copies(n, base, at, size):
        to, here = pl.ds(pl.multiple_of(base + at, 128), size), pl.ds(at, size)
        return (
            pltpu.make_async_copy(error_ref.at[n, :, here], error_hbm.at[:, to], sems.at[0, n]),
            pltpu.make_async_copy(q_ref.at[n, :, here], q_hbm.at[:, to], sems.at[1, n]),
        )

    bases = []
    for n, (own, k) in enumerate(sources):
        t_ref = refs[n]
        core, one, two = place()
        core, turn = (core, one) if own else (1 - core, two)
        quarter = (turn + QUARTERS - k) % QUARTERS
        base = (core * QUARTERS + quarter) * columns
        bases.append(base)
        for at in range(0, columns, width):
            t = jnp.concatenate(
                [
                    jnp.concatenate(
                        [
                            t_ref[(g * columns + i) // 128 * ROWS : (g * columns + i) // 128 * ROWS + ROWS, :]
                            for i in range(at, at + width, 128)
                        ],
                        axis=1,
                    )
                    for g in range(rank // ROWS)
                ],
                axis=0,
            )
            t1, t2, t3 = split(t)
            t = jnp.concatenate([t1, t2, t1, t2, t3, t1], axis=0)
            new = jnp.dot(solve, t, preferred_element_type=F32)
            q_ref[n, :, at : at + width] = new
            decoded = jnp.dot(left, new.astype(BF16), preferred_element_type=F32)
            m = m_ref[:, pl.ds(pl.multiple_of(base + at, 128), width)]
            error_ref[n, :, at : at + width] = (m.astype(F32) - decoded).astype(BF16)
            for c in copies(n, base, at, width):
                c.start()
    for n, base in enumerate(bases):
        for c in copies(n, base, 0, columns):
            c.wait()
    if last:
        hat.wait()


def result(sources, last, totals, merged, solve, p_hat, before):
    rank = solve.shape[0]
    rows, columns = merged.shape
    quarter = columns // 2 // QUARTERS
    n = len(sources)
    held = [] if before is None else list(before)
    return pl.pallas_call(
        functools.partial(result_kernel, sources, last, quarter // 2),
        out_shape=[
            pltpu.HBM((rows, columns), BF16),
            pltpu.HBM((rank, columns), F32),
            pltpu.VMEM((ROWS, 128), F32),
        ]
        + [pltpu.HBM(p_hat.shape, F32)] * last,
        in_specs=[WHOLE] * (3 + n) + [ANY] * len(held),
        out_specs=[ANY, ANY, WHOLE] + [ANY] * last,
        scratch_shapes=[
            pltpu.VMEM((n, rows, quarter), BF16),
            pltpu.VMEM((n, rank, quarter), F32),
            pltpu.SemaphoreType.DMA((2, n + 1)),
        ],
        input_output_aliases={3 + n + i: i for i in range(len(held))},
        compiler_params=params(12),
        cost_estimate=cost(1<<33, 1<<20),
        name="result",
    )(solve, p_hat, merged, *totals, *held)


def halves_kernel(a_ref, b_ref, after_ref, low_ref, high_ref):
    del after_ref
    half = low_ref.shape[0]
    low_ref[...] = a_ref[:half]
    high_ref[...] = b_ref[half:]


def halves(a, b, after):
    return pl.pallas_call(
        halves_kernel,
        out_shape=[jax.ShapeDtypeStruct((a.shape[0] // 2, 128), F32)] * 2,
        in_specs=[WHOLE, WHOLE, ANY],
        out_specs=[WHOLE, WHOLE],
        compiler_params=params(4),
        name="halves",
    )(a, b, after)


def join_kernel(low_ref, high_ref, after_ref, out_ref):
    del after_ref
    half = low_ref.shape[0]
    out_ref[:half] = low_ref[...]
    out_ref[half:] = high_ref[...]


def join(low, high, after):
    return pl.pallas_call(
        join_kernel,
        out_shape=jax.ShapeDtypeStruct((low.shape[0] * 2, 128), F32),
        in_specs=[WHOLE, WHOLE, ANY],
        out_specs=WHOLE,
        compiler_params=params(4),
        name="join",
    )(low, high, after)


def tie_kernel(value_ref, after_ref, out_ref):
    del value_ref, after_ref, out_ref


def tie(value, after):
    return pl.pallas_call(
        tie_kernel,
        out_shape=jax.ShapeDtypeStruct(value.shape, value.dtype),
        in_specs=[ANY] * 2,
        out_specs=ANY,
        input_output_aliases={0: 0},
        compiler_params=params(4),
        name="tie",
    )(value, after)


def body(gradient, error, q_start):
    rank = q_start.shape[0]
    replicas = SIZES[0] * SIZES[1]
    merged, p = merge(gradient[0], error[0], q_start)
    a, b, c = ring_x_or_z([p] * 3, 0)
    p = (p + a) + (b + c)
    sent, ext, p_mean, pieces = first_right(
        (2,), (p, *ring_x_or_z([p] * 3, 1)), merged, rank, replicas
    )
    got = swap(sent)
    sent = next_right(False, (1, 3, 0), pieces, merged, ext)
    got_next = swap(sent)
    kept = next_right(True, (2,), pieces, merged, sent)
    low, high, ext, weight = first_pair(kept, got, ext)
    kept = next_right(True, (1, 3, 0), pieces, merged, weight)
    low, high = ring_x_or_z((low, high), 0, (1, 3))
    up, down, own = next_pair(kept, got_next, weight, low, high)
    own, *sent = add_quarters((own, *ring_x_or_z((up, down), 0, (1, 3))))
    part = add_parts((own, *ring_x_or_z(sent, 1)), ext)
    total, ext = across((part, *ring_y(part)), ext.shape[0])
    solve, p_hat = factor(ext, p_mean, replicas)
    total = assemble((total, *ring_x_or_z([total] * 3, 1)), solve)
    one, three = ring_x_or_z([total] * 2, 0, (1, 3))

    def write(sources, totals, before, last=False):
        return result(sources, last, totals, merged, solve, p_hat, before)

    *out, token = write(((True, 0), (False, 0)), (total, swap(total)), None)
    low, high = ring_x_or_z(halves(one, three, token), 0, (1, 3))
    one, three = tie(one, token), tie(three, token)
    *out, _ = write(((True, 1), (True, 3)), (one, three), out)
    *out, token = write(((False, 1), (False, 3)), (swap(one), swap(three)), out)
    two = join(low, high, token)
    *out, _ = write(((True, 2),), (two,), out)
    new_error, q_new, _, p_hat = write(((False, 2),), (swap(two),), out, True)
    return (new_error[None], p_hat, q_new)


def solution(mesh):
    fine = Mesh(mesh.devices.reshape(SIZES), AXES)
    return jax.shard_map(
        body,
        mesh=fine,
        in_specs=(P(DP, ("y", "c"), None), P(DP, ("y", "c"), None), P()),
        out_specs=(P(DP, ("y", "c"), None), P(None, ("y", "c")), P()),
        check_vma=False,
    )
```

```python
import functools

import jax
import jax.numpy as jnp
from jax import lax
from jax.experimental import pallas as pl
from jax.experimental.pallas import tpu as pltpu
from jax.sharding import Mesh, PartitionSpec as P

DP = ("z", "x")
AXES = ("z", "x", "y", "c")
SIZES = (4, 4, 4, 2)
HIGHEST = lax.Precision.HIGHEST
F32 = jnp.float32
BF16 = jnp.bfloat16
MIB = 1 << 20
ROWS = 8
QUARTERS = 4
RIGHT = 1 << 33
SHIFTS = (1, 3, 2)
ANY = pl.BlockSpec(memory_space=pl.ANY)
WHOLE = pl.BlockSpec(memory_space=pltpu.VMEM)


def params(mib):
    return pltpu.CompilerParams(vmem_limit_bytes=mib * MIB)


def cost(flops, nbytes):
    return pl.CostEstimate(flops=flops, bytes_accessed=nbytes, transcendentals=0)


def place():
    core, x, z = (lax.axis_index(a) for a in ("c", "x", "z"))
    return core, jnp.where(core == 0, x, z), jnp.where(core == 0, z, x)


def index(z, x, y, c):
    return ((z * SIZES[1] + x) * SIZES[2] + y) * SIZES[3] + c


def everyone():
    return [
        (z, x, y, c)
        for z in range(SIZES[0])
        for x in range(SIZES[1])
        for y in range(SIZES[2])
        for c in range(SIZES[3])
    ]


def ring_x_or_z(values, phase, shifts=SHIFTS):
    out = []
    for k, value in zip(shifts, values):
        pairs = []
        for z, x, y, c in everyone():
            to = (z, (x + k) % SIZES[1], y, c) if c == phase else ((z + k) % SIZES[0], x, y, c)
            pairs.append((index(z, x, y, c), index(*to)))
        out.append(lax.ppermute(value, AXES, pairs))
    return out


def ring_y(value):
    n = SIZES[2]
    return [lax.ppermute(value, "y", [(i, (i + k) % n) for i in range(n)]) for k in SHIFTS]


def swap(value):
    return lax.ppermute(value, "c", [(0, 1), (1, 0)])


def merge_kernel(width, g_hbm, e_hbm, q_hbm, m_ref, p_ref, g_ref, e_ref, q_ref, sems):
    rows, columns = g_ref.shape
    rank = q_ref.shape[0]
    steps = columns // width

    def copies(i):
        at = pl.ds(i * width, width)
        return [
            pltpu.make_async_copy(src.at[:, at], dst.at[:, at], sems.at[n, i])
            for n, (src, dst) in enumerate(((g_hbm, g_ref), (e_hbm, e_ref), (q_hbm, q_ref)))
        ]

    for i in range(steps):
        for c in copies(i):
            c.start()
    acc = jnp.zeros((rows, rank), F32)
    for i in range(steps):
        for c in copies(i):
            c.wait()
        at = pl.ds(i * width, width)
        m = (g_ref[:, at].astype(F32) + e_ref[:, at].astype(F32)).astype(BF16)
        m_ref[:, at] = m
        acc = acc + lax.dot_general(
            m, q_ref[:, at], (((1,), (1,)), ((), ())), preferred_element_type=F32
        )
    p_ref[...] = pack(acc.T)


def pack(p):
    rank, rows = p.shape
    full = rows // 128
    half = rank // 2
    parts = [p[:, i * 128 : (i + 1) * 128] for i in range(full)]
    rest = p[:, full * 128 :]
    return jnp.concatenate(parts + [jnp.concatenate([rest[:half], rest[half:]], axis=1)], axis=0)


def unpack(packed, rank):
    full = packed.shape[0] // rank
    last = packed[full * rank :]
    rest = jnp.concatenate([last[:, :64], last[:, 64:]], axis=0)
    return jnp.concatenate(
        [packed[i * rank : (i + 1) * rank] for i in range(full)] + [rest], axis=1
    )


def merge(gradient, error, q_start):
    rows, columns = gradient.shape
    rank = q_start.shape[0]
    width = 1024
    gradient, error, q_start = (
        pltpu.with_memory_space_constraint(a, pltpu.HBM) for a in (gradient, error, q_start)
    )
    return pl.pallas_call(
        functools.partial(merge_kernel, width),
        out_shape=[pltpu.VMEM((rows, columns), BF16), pltpu.VMEM((rank * rows // 128, 128), F32)],
        in_specs=[ANY, ANY, ANY],
        out_specs=[WHOLE, WHOLE],
        scratch_shapes=[
            pltpu.VMEM((rows, columns), BF16),
            pltpu.VMEM((rows, columns), BF16),
            pltpu.VMEM((rank, columns), BF16),
            pltpu.SemaphoreType.DMA((3, columns // width)),
        ],
        compiler_params=params(24),
        cost_estimate=cost(2 * rank * rows * columns, 4 * rows * columns),
        name="merge",
    )(gradient, error, q_start)


def right_tiles(quarters, pieces, m_ref, out_ref):
    rank = pieces.shape[0] // 3
    width = m_ref.shape[1] // 2 // QUARTERS
    to = 0
    for quarter in quarters:
        at = pl.multiple_of(quarter * width, width)
        t = jnp.dot(pieces, m_ref[:, pl.ds(at, width)], preferred_element_type=F32)
        t = t[:rank] + (t[rank : 2 * rank] + t[2 * rank :])
        for g in range(rank // ROWS):
            for n in range(width // 128):
                out_ref[to : to + ROWS, :] = t[g * ROWS : (g + 1) * ROWS, n * 128 : (n + 1) * 128]
                to += ROWS


def quarters_of(own, turns):
    core, one, two = place()
    core, turn = (core, one) if own else (1 - core, two)
    return [core * QUARTERS + (turn + k) % QUARTERS for k in turns]


def split(n):
    high = n.astype(BF16)
    n = n - high.astype(F32)
    middle = n.astype(BF16)
    return high, middle, (n - middle.astype(F32)).astype(BF16)


def first_right_kernel(replicas, rank, turns, a_ref, b_ref, c_ref, d_ref, m_ref, out_ref, ext_ref, p_ref, pieces_ref):
    p = (a_ref[...] + b_ref[...] + (c_ref[...] + d_ref[...])) * (1.0 / replicas)
    peak = jnp.max(jnp.abs(p), axis=(0, 1), keepdims=True)
    peak = jnp.where(peak > 0, peak, 1.0)
    p = unpack(p, rank)
    p_ref[...] = p
    pieces = jnp.concatenate(split(p / peak), axis=0)
    pieces_ref[...] = pieces
    right_tiles(quarters_of(False, turns), pieces, m_ref, out_ref)
    gram = lax.dot_general(
        p, p, (((1,), (1,)), ((), ())), precision=HIGHEST, preferred_element_type=F32
    )
    two = 2 * ROWS
    ext = jnp.concatenate(
        [
            jnp.concatenate([gram[i : i + ROWS], gram[i + ROWS : i + two]], axis=1)
            for i in range(0, rank, two)
        ]
        + [jnp.broadcast_to(peak, (ROWS, 128))],
        axis=0,
    )
    ext_ref[...] = ext
    out_ref[out_ref.shape[0] - ext.shape[0] :, :] = ext


def next_right_kernel(own, turns, pieces_ref, m_ref, after_ref, out_ref):
    del after_ref
    right_tiles(quarters_of(own, turns), pieces_ref[...], m_ref, out_ref)


def first_right(turns, parts, merged, rank, replicas):
    rows, columns = merged.shape
    size = rank * columns // 1024
    extra = rank * rank // 128 + ROWS
    return pl.pallas_call(
        functools.partial(first_right_kernel, replicas, rank, turns),
        out_shape=[
            jax.ShapeDtypeStruct((size + extra, 128), F32),
            pltpu.VMEM((extra, 128), F32),
            pltpu.VMEM((rank, rows), F32),
            pltpu.VMEM((3 * rank, rows), BF16),
        ],
        in_specs=[WHOLE] * 5,
        out_specs=[WHOLE] * 4,
        compiler_params=params(12),
        cost_estimate=cost(RIGHT, 1 << 20),
        name="first_right",
    )(*parts, merged)


def next_right(own, turns, pieces, merged, after):
    size = pieces.shape[0] // 3 * merged.shape[1] // 1024 * len(turns)
    return pl.pallas_call(
        functools.partial(next_right_kernel, own, turns),
        out_shape=jax.ShapeDtypeStruct((size, 128), F32),
        in_specs=[WHOLE, WHOLE, ANY],
        out_specs=WHOLE,
        compiler_params=params(12),
        cost_estimate=cost(RIGHT, 1 << 20),
        name="next_right",
    )(pieces, merged, after)


def first_pair_kernel(kept_ref, got_ref, ext_ref, out_ref, pair_ref, weight_ref):
    grams = ext_ref.shape[0] - ROWS
    size = kept_ref.shape[0]
    own, its = ext_ref[grams : grams + 1, :1], got_ref[size + grams : size + grams + 1, :1]
    top = jnp.maximum(own, its)
    pair_ref[:grams] = ext_ref[:grams] + got_ref[size : size + grams]
    pair_ref[grams:] = jnp.broadcast_to(top, (ROWS, 128))
    own, its = own / top, its / top
    weight_ref[:ROWS] = jnp.broadcast_to(own, (ROWS, 128))
    weight_ref[ROWS:] = jnp.broadcast_to(its, (ROWS, 128))
    out_ref[...] = kept_ref[...] * own + got_ref[:size] * its


def first_pair(kept, got, ext):
    return pl.pallas_call(
        first_pair_kernel,
        out_shape=[
            jax.ShapeDtypeStruct(kept.shape, F32),
            pltpu.VMEM(ext.shape, F32),
            pltpu.VMEM((2 * ROWS, 128), F32),
        ],
        in_specs=[WHOLE] * 3,
        out_specs=[WHOLE] * 3,
        compiler_params=params(8),
        name="first_pair",
    )(kept, got, ext)


def next_pair_kernel(kept_ref, got_ref, weight_ref, *out):
    own, its = weight_ref[:1, :1], weight_ref[ROWS : ROWS + 1, :1]
    size = out[0].shape[0]
    for n, ref in enumerate(out):
        at = slice(n * size, (n + 1) * size)
        ref[...] = kept_ref[at] * own + got_ref[at] * its


def next_pair(kept, got, weight):
    size = kept.shape[0] // 3
    return pl.pallas_call(
        next_pair_kernel,
        out_shape=[jax.ShapeDtypeStruct((size, 128), F32)] * 3,
        in_specs=[WHOLE] * 3,
        out_specs=[WHOLE] * 3,
        compiler_params=params(8),
        name="next_pair",
    )(kept, got, weight)


def add_quarters_kernel(a_ref, b_ref, c_ref, d_ref, *out):
    size = a_ref.shape[0] // QUARTERS
    for k, ref in zip((0,) + SHIFTS, out):
        at = pl.ds(pl.multiple_of((place()[2] + k) % QUARTERS * size, size), size)
        ref[...] = (a_ref[at] + b_ref[at]) + (c_ref[at] + d_ref[at])


def add_quarters(parts):
    size = parts[0].shape[0] // QUARTERS
    return pl.pallas_call(
        add_quarters_kernel,
        out_shape=[jax.ShapeDtypeStruct((size, 128), F32)] * QUARTERS,
        in_specs=[WHOLE] * QUARTERS,
        out_specs=[WHOLE] * QUARTERS,
        compiler_params=params(8),
        name="add_quarters",
    )(*parts)


def add_parts_kernel(a_ref, b_ref, c_ref, d_ref, ext_ref, out_ref):
    size = a_ref.shape[0]
    out_ref[:size] = (a_ref[...] + b_ref[...]) + (c_ref[...] + d_ref[...])
    out_ref[size:] = ext_ref[...]


def add_parts(parts, ext):
    return pl.pallas_call(
        add_parts_kernel,
        out_shape=jax.ShapeDtypeStruct((parts[0].shape[0] + ext.shape[0], 128), F32),
        in_specs=[WHOLE] * 5,
        out_specs=WHOLE,
        compiler_params=params(8),
        name="add_parts",
    )(*parts, ext)


def across_kernel(a_ref, b_ref, c_ref, d_ref, out_ref, ext_ref):
    size = out_ref.shape[0]
    grams = ext_ref.shape[0] - ROWS
    refs = (a_ref, b_ref, c_ref, d_ref)
    peaks = [r[size + grams : size + grams + 1, :1] for r in refs]
    top = jnp.maximum(jnp.maximum(peaks[0], peaks[1]), jnp.maximum(peaks[2], peaks[3]))
    a, b, c, d = (r[:size] * (k / top) for r, k in zip(refs, peaks))
    out_ref[...] = (a + b) + (c + d)
    a, b, c, d = (r[size : size + grams] for r in refs)
    ext_ref[:grams] = (a + b) + (c + d)
    ext_ref[grams:] = jnp.broadcast_to(top, (ROWS, 128))


def across(parts, extra):
    return pl.pallas_call(
        across_kernel,
        out_shape=[
            jax.ShapeDtypeStruct((parts[0].shape[0] - extra, 128), F32),
            pltpu.VMEM((extra, 128), F32),
        ],
        in_specs=[WHOLE] * 4,
        out_specs=[WHOLE] * 2,
        compiler_params=params(8),
        name="across",
    )(*parts)


def assemble_kernel(a_ref, b_ref, c_ref, d_ref, after_ref, out_ref):
    del after_ref
    size = a_ref.shape[0]
    for k, ref in zip((0,) + SHIFTS, (a_ref, b_ref, c_ref, d_ref)):
        at = pl.multiple_of((place()[2] + QUARTERS - k) % QUARTERS * size, size)
        out_ref[pl.ds(at, size)] = ref[...]


def assemble(parts, after):
    return pl.pallas_call(
        assemble_kernel,
        out_shape=jax.ShapeDtypeStruct((parts[0].shape[0] * QUARTERS, 128), F32),
        in_specs=[WHOLE] * 4 + [ANY],
        out_specs=WHOLE,
        compiler_params=params(8),
        name="assemble",
    )(*parts, after)


def factor_kernel(replicas, ext_ref, p_ref, solve_ref, hat_ref):
    rank = p_ref.shape[0]
    groups = rank // ROWS
    sub = lax.broadcasted_iota(jnp.int32, (ROWS, 2 * rank), 0)
    lane = lax.broadcasted_iota(jnp.int32, (ROWS, 2 * rank), 1)
    blocks = []
    for g in range(groups):
        tile = ext_ref[g // 2 * ROWS : (g // 2 + 1) * ROWS, (g % 2) * rank : (g % 2 + 1) * rank]
        unit = jnp.where(lane[:, :rank] == sub[:, :rank] + g * ROWS, 1.0, 0.0)
        blocks.append(jnp.concatenate([tile, unit], axis=1))
    for own in range(groups):
        spread = lambda g: [
            jnp.broadcast_to(blocks[g][:, own * ROWS + k : own * ROWS + k + 1], (ROWS, 2 * rank))
            for k in range(ROWS)
        ]
        columns = spread(own)
        rows, heads = [], []
        for k in range(ROWS):
            scale = 1.0 / columns[k][k : k + 1]
            row = blocks[own][k : k + 1] * scale
            head = {m: columns[m][k : k + 1] * scale for m in range(k + 1, ROWS)}
            factors = jnp.where(sub > k, columns[k], 0.0)
            blocks[own] = blocks[own] - factors * row
            for m, h in head.items():
                columns[m] = columns[m] - factors * h
            rows.append(row)
            heads.append(head)
        for g in range(own + 1, groups):
            columns = spread(g)
            for k in range(ROWS):
                blocks[g] = blocks[g] - columns[k] * rows[k]
                for m, h in heads[k].items():
                    columns[m] = columns[m] - columns[k] * h
    inverse = []
    for g in range(groups):
        diagonal = jnp.sum(
            jnp.where(lane == sub + g * ROWS, blocks[g], 0.0), axis=1, keepdims=True
        )
        inverse.append(blocks[g][:, rank:] / jnp.sqrt(diagonal))
    inverse = jnp.concatenate(inverse, axis=0)
    grams = ext_ref.shape[0] - ROWS
    solve_ref[...] = inverse * (ext_ref[grams : grams + 1, :1] * (1.0 / replicas))
    hat_ref[...] = jnp.dot(inverse, p_ref[...], precision=HIGHEST, preferred_element_type=F32)


def factor(ext, p_mean, replicas):
    rank, rows = p_mean.shape
    return pl.pallas_call(
        functools.partial(factor_kernel, replicas),
        out_shape=[
            jax.ShapeDtypeStruct((rank, rank), F32),
            jax.ShapeDtypeStruct((rank, rows), F32),
        ],
        in_specs=[WHOLE] * 2,
        out_specs=[WHOLE] * 2,
        compiler_params=params(8),
        cost_estimate=cost(1 << 32, 1 << 20),
        name="factor",
    )(ext, p_mean)


def result_kernel(sources, last, width, solve_ref, p_ref, m_ref, *refs):
    if last:
        hat_hbm, refs = refs[-4], refs[:-4] + refs[-3:]
        hat = pltpu.make_async_copy(p_ref, hat_hbm, refs[-1].at[0, len(sources)])
        hat.start()
    error_hbm, q_hbm, token_ref, error_ref, q_ref, sems = refs[-6:]
    token_ref[...] = jnp.zeros_like(token_ref)
    rank = solve_ref.shape[0]
    columns = q_ref.shape[2]
    left = p_ref[...].T.astype(BF16)
    s1, s2, s3 = split(solve_ref[...])
    solve = jnp.concatenate([s1, s1, s2, s2, s1, s3], axis=1)

    def copies(n, base, at, size):
        to, here = pl.ds(pl.multiple_of(base + at, 128), size), pl.ds(at, size)
        return (
            pltpu.make_async_copy(error_ref.at[n, :, here], error_hbm.at[:, to], sems.at[0, n]),
            pltpu.make_async_copy(q_ref.at[n, :, here], q_hbm.at[:, to], sems.at[1, n]),
        )

    bases = []
    for n, (own, k) in enumerate(sources):
        t_ref = refs[n]
        core, one, two = place()
        core, turn = (core, one) if own else (1 - core, two)
        quarter = (turn + QUARTERS - k) % QUARTERS
        base = (core * QUARTERS + quarter) * columns
        bases.append(base)
        for at in range(0, columns, width):
            t = jnp.concatenate(
                [
                    jnp.concatenate(
                        [
                            t_ref[(g * columns + i) // 128 * ROWS : (g * columns + i) // 128 * ROWS + ROWS, :]
                            for i in range(at, at + width, 128)
                        ],
                        axis=1,
                    )
                    for g in range(rank // ROWS)
                ],
                axis=0,
            )
            t1, t2, t3 = split(t)
            t = jnp.concatenate([t1, t2, t1, t2, t3, t1], axis=0)
            new = jnp.dot(solve, t, preferred_element_type=F32)
            q_ref[n, :, at : at + width] = new
            decoded = jnp.dot(left, new.astype(BF16), preferred_element_type=F32)
            m = m_ref[:, pl.ds(pl.multiple_of(base + at, 128), width)]
            error_ref[n, :, at : at + width] = (m.astype(F32) - decoded).astype(BF16)
            for c in copies(n, base, at, width):
                c.start()
    for n, base in enumerate(bases):
        for c in copies(n, base, 0, columns):
            c.wait()
    if last:
        hat.wait()


def result(sources, last, totals, merged, solve, p_hat, before):
    rank = solve.shape[0]
    rows, columns = merged.shape
    quarter = columns // 2 // QUARTERS
    n = len(sources)
    held = [] if before is None else list(before)
    return pl.pallas_call(
        functools.partial(result_kernel, sources, last, quarter // 2),
        out_shape=[
            pltpu.HBM((rows, columns), BF16),
            pltpu.HBM((rank, columns), F32),
            pltpu.VMEM((ROWS, 128), F32),
        ]
        + [pltpu.HBM(p_hat.shape, F32)] * last,
        in_specs=[WHOLE] * (3 + n) + [ANY] * len(held),
        out_specs=[ANY, ANY, WHOLE] + [ANY] * last,
        scratch_shapes=[
            pltpu.VMEM((n, rows, quarter), BF16),
            pltpu.VMEM((n, rank, quarter), F32),
            pltpu.SemaphoreType.DMA((2, n + 1)),
        ],
        input_output_aliases={3 + n + i: i for i in range(len(held))},
        compiler_params=params(12),
        cost_estimate=cost(1<<33, 1<<20),
        name="result",
    )(solve, p_hat, merged, *totals, *held)


def tie_kernel(value_ref, after_ref, out_ref):
    del value_ref, after_ref, out_ref


def tie(value, after):
    return pl.pallas_call(
        tie_kernel,
        out_shape=jax.ShapeDtypeStruct(value.shape, value.dtype),
        in_specs=[ANY] * 2,
        out_specs=ANY,
        input_output_aliases={0: 0},
        compiler_params=params(4),
        name="tie",
    )(value, after)


def body(gradient, error, q_start):
    rank = q_start.shape[0]
    replicas = SIZES[0] * SIZES[1]
    merged, p = merge(gradient[0], error[0], q_start)
    a, b, c = ring_x_or_z([p] * 3, 0)
    p = (p + a) + (b + c)
    sent, ext, p_mean, pieces = first_right(
        (2,), (p, *ring_x_or_z([p] * 3, 1)), merged, rank, replicas
    )
    got = swap(sent)
    sent = next_right(False, (1, 3, 0), pieces, merged, ext)
    got_next = swap(sent)
    kept = next_right(True, (2,), pieces, merged, sent)
    two, ext, weight = first_pair(kept, got, ext)
    (two,) = ring_x_or_z((two,), 0, (2,))
    kept = next_right(True, (1, 3, 0), pieces, merged, weight)
    *near, own = next_pair(kept, got_next, weight)
    own, *sent = add_quarters((own, *ring_x_or_z(near, 0, (1, 3)), two))
    part = add_parts((own, *ring_x_or_z(sent, 1)), ext)
    total, ext = across((part, *ring_y(part)), ext.shape[0])
    solve, p_hat = factor(ext, p_mean, replicas)
    total = assemble((total, *ring_x_or_z([total] * 3, 1)), solve)
    others = ring_x_or_z([total] * 3, 0)

    def write(own, turns, totals, before, last=False):
        sources = tuple((own, k) for k in turns)
        return result(sources, last, totals, merged, solve, p_hat, before)

    *out, token = write(True, (0,), (total,), None)
    *out, token = write(False, (0,), (swap(total),), out)
    others = [tie(a, token) for a in others]
    *out, _ = write(True, SHIFTS, others, out)
    new_error, q_new, _, p_hat = write(False, SHIFTS, [swap(a) for a in others], out, True)
    return (new_error[None], p_hat, q_new)


def solution(mesh):
    fine = Mesh(mesh.devices.reshape(SIZES), AXES)
    return jax.shard_map(
        body,
        mesh=fine,
        in_specs=(P(DP, ("y", "c"), None), P(DP, ("y", "c"), None), P()),
        out_specs=(P(DP, ("y", "c"), None), P(None, ("y", "c")), P()),
        check_vma=False,
    )
```

```python
import functools

import jax
import jax.numpy as jnp
from jax import lax
from jax.experimental import pallas as pl
from jax.experimental.pallas import tpu as pltpu
from jax.sharding import Mesh, PartitionSpec as P

DP = ("z", "x")
AXES = ("z", "x", "y", "c")
SIZES = (4, 4, 4, 2)
HIGHEST = lax.Precision.HIGHEST
F32 = jnp.float32
BF16 = jnp.bfloat16
MIB = 1 << 20
ROWS = 8
QUARTERS = 4
RIGHT = 1 << 33
SHIFTS = (1, 3, 2)
ANY = pl.BlockSpec(memory_space=pl.ANY)
WHOLE = pl.BlockSpec(memory_space=pltpu.VMEM)


def params(mib):
    return pltpu.CompilerParams(vmem_limit_bytes=mib * MIB)


def cost(flops, nbytes):
    return pl.CostEstimate(flops=flops, bytes_accessed=nbytes, transcendentals=0)


def place():
    core, x, z = (lax.axis_index(a) for a in ("c", "x", "z"))
    return core, jnp.where(core == 0, x, z), jnp.where(core == 0, z, x)


def index(z, x, y, c):
    return ((z * SIZES[1] + x) * SIZES[2] + y) * SIZES[3] + c


def everyone():
    return [
        (z, x, y, c)
        for z in range(SIZES[0])
        for x in range(SIZES[1])
        for y in range(SIZES[2])
        for c in range(SIZES[3])
    ]


def ring_x_or_z(values, phase, shifts=SHIFTS):
    out = []
    for k, value in zip(shifts, values):
        pairs = []
        for z, x, y, c in everyone():
            to = (z, (x + k) % SIZES[1], y, c) if c == phase else ((z + k) % SIZES[0], x, y, c)
            pairs.append((index(z, x, y, c), index(*to)))
        out.append(lax.ppermute(value, AXES, pairs))
    return out


def ring_y(value):
    n = SIZES[2]
    return [lax.ppermute(value, "y", [(i, (i + k) % n) for i in range(n)]) for k in SHIFTS]


def swap(value):
    return lax.ppermute(value, "c", [(0, 1), (1, 0)])


def merge_kernel(width, g_hbm, e_hbm, q_hbm, m_ref, p_ref, g_ref, e_ref, q_ref, sems):
    rows, columns = g_ref.shape
    rank = q_ref.shape[0]
    steps = columns // width

    def copies(i):
        at = pl.ds(i * width, width)
        return [
            pltpu.make_async_copy(src.at[:, at], dst.at[:, at], sems.at[n, i])
            for n, (src, dst) in enumerate(((g_hbm, g_ref), (e_hbm, e_ref), (q_hbm, q_ref)))
        ]

    for i in range(steps):
        for c in copies(i):
            c.start()
    acc = jnp.zeros((rows, rank), F32)
    for i in range(steps):
        for c in copies(i):
            c.wait()
        at = pl.ds(i * width, width)
        m = (g_ref[:, at].astype(F32) + e_ref[:, at].astype(F32)).astype(BF16)
        m_ref[:, at] = m
        acc = acc + lax.dot_general(
            m, q_ref[:, at], (((1,), (1,)), ((), ())), preferred_element_type=F32
        )
    p_ref[...] = pack(acc.T)


def pack(p):
    rank, rows = p.shape
    full = rows // 128
    half = rank // 2
    parts = [p[:, i * 128 : (i + 1) * 128] for i in range(full)]
    rest = p[:, full * 128 :]
    return jnp.concatenate(parts + [jnp.concatenate([rest[:half], rest[half:]], axis=1)], axis=0)


def unpack(packed, rank):
    full = packed.shape[0] // rank
    last = packed[full * rank :]
    rest = jnp.concatenate([last[:, :64], last[:, 64:]], axis=0)
    return jnp.concatenate(
        [packed[i * rank : (i + 1) * rank] for i in range(full)] + [rest], axis=1
    )


def merge(gradient, error, q_start):
    rows, columns = gradient.shape
    rank = q_start.shape[0]
    width = 1024
    gradient, error, q_start = (
        pltpu.with_memory_space_constraint(a, pltpu.HBM) for a in (gradient, error, q_start)
    )
    return pl.pallas_call(
        functools.partial(merge_kernel, width),
        out_shape=[pltpu.VMEM((rows, columns), BF16), pltpu.VMEM((rank * rows // 128, 128), F32)],
        in_specs=[ANY, ANY, ANY],
        out_specs=[WHOLE, WHOLE],
        scratch_shapes=[
            pltpu.VMEM((rows, columns), BF16),
            pltpu.VMEM((rows, columns), BF16),
            pltpu.VMEM((rank, columns), BF16),
            pltpu.SemaphoreType.DMA((3, columns // width)),
        ],
        compiler_params=params(24),
        cost_estimate=cost(2 * rank * rows * columns, 4 * rows * columns),
        name="merge",
    )(gradient, error, q_start)


def right_tiles(quarters, pieces, m_ref, out_ref):
    rank = pieces.shape[0] // 3
    width = m_ref.shape[1] // 2 // QUARTERS
    to = 0
    for quarter in quarters:
        at = pl.multiple_of(quarter * width, width)
        t = jnp.dot(pieces, m_ref[:, pl.ds(at, width)], preferred_element_type=F32)
        t = t[:rank] + (t[rank : 2 * rank] + t[2 * rank :])
        for g in range(rank // ROWS):
            for n in range(width // 128):
                out_ref[to : to + ROWS, :] = t[g * ROWS : (g + 1) * ROWS, n * 128 : (n + 1) * 128]
                to += ROWS


def quarters_of(own, turns):
    core, one, two = place()
    core, turn = (core, one) if own else (1 - core, two)
    return [core * QUARTERS + (turn + k) % QUARTERS for k in turns]


def split(n):
    high = n.astype(BF16)
    n = n - high.astype(F32)
    middle = n.astype(BF16)
    return high, middle, (n - middle.astype(F32)).astype(BF16)


def first_right_kernel(replicas, rank, turns, a_ref, b_ref, c_ref, d_ref, m_ref, out_ref, ext_ref, p_ref, pieces_ref):
    p = (a_ref[...] + b_ref[...] + (c_ref[...] + d_ref[...])) * (1.0 / replicas)
    peak = jnp.max(jnp.abs(p), axis=(0, 1), keepdims=True)
    peak = jnp.where(peak > 0, peak, 1.0)
    p = unpack(p, rank)
    p_ref[...] = p
    pieces = jnp.concatenate(split(p / peak), axis=0)
    pieces_ref[...] = pieces
    right_tiles(quarters_of(False, turns), pieces, m_ref, out_ref)
    gram = lax.dot_general(
        p, p, (((1,), (1,)), ((), ())), precision=HIGHEST, preferred_element_type=F32
    )
    two = 2 * ROWS
    ext = jnp.concatenate(
        [
            jnp.concatenate([gram[i : i + ROWS], gram[i + ROWS : i + two]], axis=1)
            for i in range(0, rank, two)
        ]
        + [jnp.broadcast_to(peak, (ROWS, 128))],
        axis=0,
    )
    ext_ref[...] = ext
    out_ref[out_ref.shape[0] - ext.shape[0] :, :] = ext


def next_right_kernel(own, turns, pieces_ref, m_ref, after_ref, out_ref):
    del after_ref
    right_tiles(quarters_of(own, turns), pieces_ref[...], m_ref, out_ref)


def first_right(turns, parts, merged, rank, replicas):
    rows, columns = merged.shape
    size = rank * columns // 1024
    extra = rank * rank // 128 + ROWS
    return pl.pallas_call(
        functools.partial(first_right_kernel, replicas, rank, turns),
        out_shape=[
            jax.ShapeDtypeStruct((size + extra, 128), F32),
            pltpu.VMEM((extra, 128), F32),
            pltpu.VMEM((rank, rows), F32),
            pltpu.VMEM((3 * rank, rows), BF16),
        ],
        in_specs=[WHOLE] * 5,
        out_specs=[WHOLE] * 4,
        compiler_params=params(12),
        cost_estimate=cost(RIGHT, 1 << 20),
        name="first_right",
    )(*parts, merged)


def next_right(own, turns, pieces, merged, after):
    size = pieces.shape[0] // 3 * merged.shape[1] // 1024 * len(turns)
    return pl.pallas_call(
        functools.partial(next_right_kernel, own, turns),
        out_shape=jax.ShapeDtypeStruct((size, 128), F32),
        in_specs=[WHOLE, WHOLE, ANY],
        out_specs=WHOLE,
        compiler_params=params(12),
        cost_estimate=cost(RIGHT, 1 << 20),
        name="next_right",
    )(pieces, merged, after)


def first_pair_kernel(kept_ref, got_ref, ext_ref, out_ref, pair_ref, weight_ref):
    grams = ext_ref.shape[0] - ROWS
    size = kept_ref.shape[0]
    own, its = ext_ref[grams : grams + 1, :1], got_ref[size + grams : size + grams + 1, :1]
    top = jnp.maximum(own, its)
    pair_ref[:grams] = ext_ref[:grams] + got_ref[size : size + grams]
    pair_ref[grams:] = jnp.broadcast_to(top, (ROWS, 128))
    own, its = own / top, its / top
    weight_ref[:ROWS] = jnp.broadcast_to(own, (ROWS, 128))
    weight_ref[ROWS:] = jnp.broadcast_to(its, (ROWS, 128))
    out_ref[...] = kept_ref[...] * own + got_ref[:size] * its


def first_pair(kept, got, ext):
    return pl.pallas_call(
        first_pair_kernel,
        out_shape=[
            jax.ShapeDtypeStruct(kept.shape, F32),
            pltpu.VMEM(ext.shape, F32),
            pltpu.VMEM((2 * ROWS, 128), F32),
        ],
        in_specs=[WHOLE] * 3,
        out_specs=[WHOLE] * 3,
        compiler_params=params(8),
        name="first_pair",
    )(kept, got, ext)


def next_pair_kernel(kept_ref, got_ref, weight_ref, *out):
    own, its = weight_ref[:1, :1], weight_ref[ROWS : ROWS + 1, :1]
    size = out[0].shape[0]
    for n, ref in enumerate(out):
        at = slice(n * size, (n + 1) * size)
        ref[...] = kept_ref[at] * own + got_ref[at] * its


def next_pair(kept, got, weight):
    size = kept.shape[0] // 3
    return pl.pallas_call(
        next_pair_kernel,
        out_shape=[jax.ShapeDtypeStruct((size, 128), F32)] * 3,
        in_specs=[WHOLE] * 3,
        out_specs=[WHOLE] * 3,
        compiler_params=params(8),
        name="next_pair",
    )(kept, got, weight)


def add_quarters_kernel(a_ref, b_ref, c_ref, d_ref, *out):
    size = a_ref.shape[0] // QUARTERS
    for k, ref in zip((0,) + SHIFTS, out):
        at = pl.ds(pl.multiple_of((place()[2] + k) % QUARTERS * size, size), size)
        ref[...] = (a_ref[at] + b_ref[at]) + (c_ref[at] + d_ref[at])


def add_quarters(parts):
    size = parts[0].shape[0] // QUARTERS
    return pl.pallas_call(
        add_quarters_kernel,
        out_shape=[jax.ShapeDtypeStruct((size, 128), F32)] * QUARTERS,
        in_specs=[WHOLE] * QUARTERS,
        out_specs=[WHOLE] * QUARTERS,
        compiler_params=params(8),
        name="add_quarters",
    )(*parts)


def add_parts_kernel(a_ref, b_ref, c_ref, d_ref, ext_ref, out_ref):
    size = a_ref.shape[0]
    out_ref[:size] = (a_ref[...] + b_ref[...]) + (c_ref[...] + d_ref[...])
    out_ref[size:] = ext_ref[...]


def add_parts(parts, ext):
    return pl.pallas_call(
        add_parts_kernel,
        out_shape=jax.ShapeDtypeStruct((parts[0].shape[0] + ext.shape[0], 128), F32),
        in_specs=[WHOLE] * 5,
        out_specs=WHOLE,
        compiler_params=params(8),
        name="add_parts",
    )(*parts, ext)


def across_kernel(a_ref, b_ref, c_ref, d_ref, out_ref, ext_ref):
    size = out_ref.shape[0]
    grams = ext_ref.shape[0] - ROWS
    refs = (a_ref, b_ref, c_ref, d_ref)
    peaks = [r[size + grams : size + grams + 1, :1] for r in refs]
    top = jnp.maximum(jnp.maximum(peaks[0], peaks[1]), jnp.maximum(peaks[2], peaks[3]))
    a, b, c, d = (r[:size] * (k / top) for r, k in zip(refs, peaks))
    out_ref[...] = (a + b) + (c + d)
    a, b, c, d = (r[size : size + grams] for r in refs)
    ext_ref[:grams] = (a + b) + (c + d)
    ext_ref[grams:] = jnp.broadcast_to(top, (ROWS, 128))


def across(parts, extra):
    return pl.pallas_call(
        across_kernel,
        out_shape=[
            jax.ShapeDtypeStruct((parts[0].shape[0] - extra, 128), F32),
            pltpu.VMEM((extra, 128), F32),
        ],
        in_specs=[WHOLE] * 4,
        out_specs=[WHOLE] * 2,
        compiler_params=params(8),
        name="across",
    )(*parts)


def assemble_kernel(a_ref, b_ref, c_ref, d_ref, after_ref, out_ref):
    del after_ref
    size = a_ref.shape[0]
    for k, ref in zip((0,) + SHIFTS, (a_ref, b_ref, c_ref, d_ref)):
        at = pl.multiple_of((place()[2] + QUARTERS - k) % QUARTERS * size, size)
        out_ref[pl.ds(at, size)] = ref[...]


def assemble(parts, after):
    return pl.pallas_call(
        assemble_kernel,
        out_shape=jax.ShapeDtypeStruct((parts[0].shape[0] * QUARTERS, 128), F32),
        in_specs=[WHOLE] * 4 + [ANY],
        out_specs=WHOLE,
        compiler_params=params(8),
        name="assemble",
    )(*parts, after)


def factor_kernel(replicas, ext_ref, p_ref, solve_ref, left_ref, hat_ref):
    rank = p_ref.shape[0]
    groups = rank // ROWS
    sub = lax.broadcasted_iota(jnp.int32, (ROWS, 2 * rank), 0)
    lane = lax.broadcasted_iota(jnp.int32, (ROWS, 2 * rank), 1)
    blocks = []
    for g in range(groups):
        tile = ext_ref[g // 2 * ROWS : (g // 2 + 1) * ROWS, (g % 2) * rank : (g % 2 + 1) * rank]
        unit = jnp.where(lane[:, :rank] == sub[:, :rank] + g * ROWS, 1.0, 0.0)
        blocks.append(jnp.concatenate([tile, unit], axis=1))
    for own in range(groups):
        spread = lambda g: [
            jnp.broadcast_to(blocks[g][:, own * ROWS + k : own * ROWS + k + 1], (ROWS, 2 * rank))
            for k in range(ROWS)
        ]
        columns = spread(own)
        rows, heads = [], []
        for k in range(ROWS):
            scale = 1.0 / columns[k][k : k + 1]
            row = blocks[own][k : k + 1] * scale
            head = {m: columns[m][k : k + 1] * scale for m in range(k + 1, ROWS)}
            factors = jnp.where(sub > k, columns[k], 0.0)
            blocks[own] = blocks[own] - factors * row
            for m, h in head.items():
                columns[m] = columns[m] - factors * h
            rows.append(row)
            heads.append(head)
        for g in range(own + 1, groups):
            columns = spread(g)
            for k in range(ROWS):
                blocks[g] = blocks[g] - columns[k] * rows[k]
                for m, h in heads[k].items():
                    columns[m] = columns[m] - columns[k] * h
    inverse = []
    for g in range(groups):
        diagonal = jnp.sum(
            jnp.where(lane == sub + g * ROWS, blocks[g], 0.0), axis=1, keepdims=True
        )
        inverse.append(blocks[g][:, rank:] / jnp.sqrt(diagonal))
    inverse = jnp.concatenate(inverse, axis=0)
    grams = ext_ref.shape[0] - ROWS
    s1, s2, s3 = split(inverse * (ext_ref[grams : grams + 1, :1] * (1.0 / replicas)))
    solve_ref[...] = jnp.concatenate([s1, s1, s2, s2, s1, s3], axis=1)
    hat = jnp.dot(inverse, p_ref[...], precision=HIGHEST, preferred_element_type=F32)
    hat_ref[...] = hat
    left_ref[...] = hat.T.astype(BF16)


def factor(ext, p_mean, replicas):
    rank, rows = p_mean.shape
    return pl.pallas_call(
        functools.partial(factor_kernel, replicas),
        out_shape=[
            jax.ShapeDtypeStruct((rank, 6 * rank), BF16),
            jax.ShapeDtypeStruct((rows, rank), BF16),
            jax.ShapeDtypeStruct((rank, rows), F32),
        ],
        in_specs=[WHOLE] * 2,
        out_specs=[WHOLE] * 3,
        compiler_params=params(8),
        cost_estimate=cost(1 << 32, 1 << 20),
        name="factor",
    )(ext, p_mean)


def result_kernel(sources, last, width, solve_ref, left_ref, m_ref, *refs):
    if last:
        hat_hbm, refs = refs[-4], refs[:-4] + refs[-3:]
        hat = pltpu.make_async_copy(refs[len(sources)], hat_hbm, refs[-1].at[0, len(sources)])
        hat.start()
    error_hbm, q_hbm, token_ref, error_ref, q_ref, sems = refs[-6:]
    token_ref[...] = jnp.zeros_like(token_ref)
    rank = solve_ref.shape[0]
    columns = q_ref.shape[2]
    left = left_ref[...]
    solve = solve_ref[...]

    def copies(n, base, at, size):
        to, here = pl.ds(pl.multiple_of(base + at, 128), size), pl.ds(at, size)
        return (
            pltpu.make_async_copy(error_ref.at[n, :, here], error_hbm.at[:, to], sems.at[0, n]),
            pltpu.make_async_copy(q_ref.at[n, :, here], q_hbm.at[:, to], sems.at[1, n]),
        )

    bases = []
    for n, (own, k) in enumerate(sources):
        t_ref = refs[n]
        core, one, two = place()
        core, turn = (core, one) if own else (1 - core, two)
        quarter = (turn + QUARTERS - k) % QUARTERS
        base = (core * QUARTERS + quarter) * columns
        bases.append(base)
        for at in range(0, columns, width):
            t = jnp.concatenate(
                [
                    jnp.concatenate(
                        [
                            t_ref[(g * columns + i) // 128 * ROWS : (g * columns + i) // 128 * ROWS + ROWS, :]
                            for i in range(at, at + width, 128)
                        ],
                        axis=1,
                    )
                    for g in range(rank // ROWS)
                ],
                axis=0,
            )
            t1, t2, t3 = split(t)
            t = jnp.concatenate([t1, t2, t1, t2, t3, t1], axis=0)
            new = jnp.dot(solve, t, preferred_element_type=F32)
            q_ref[n, :, at : at + width] = new
            decoded = jnp.dot(left, new.astype(BF16), preferred_element_type=F32)
            m = m_ref[:, pl.ds(pl.multiple_of(base + at, 128), width)]
            error_ref[n, :, at : at + width] = (m.astype(F32) - decoded).astype(BF16)
            for c in copies(n, base, at, width):
                c.start()
    for n, base in enumerate(bases):
        for c in copies(n, base, 0, columns):
            c.wait()
    if last:
        hat.wait()


def result(sources, totals, merged, solve, left, before, p_hat=None):
    rank = solve.shape[0]
    rows, columns = merged.shape
    quarter = columns // 2 // QUARTERS
    n = len(sources)
    held = [] if before is None else list(before)
    last = [] if p_hat is None else [p_hat]
    return pl.pallas_call(
        functools.partial(result_kernel, sources, bool(last), quarter // 2),
        out_shape=[
            pltpu.HBM((rows, columns), BF16),
            pltpu.HBM((rank, columns), F32),
            pltpu.VMEM((ROWS, 128), F32),
        ]
        + [pltpu.HBM(a.shape, F32) for a in last],
        in_specs=[WHOLE] * (3 + n + len(last)) + [ANY] * len(held),
        out_specs=[ANY, ANY, WHOLE] + [ANY] * len(last),
        scratch_shapes=[
            pltpu.VMEM((n, rows, quarter), BF16),
            pltpu.VMEM((n, rank, quarter), F32),
            pltpu.SemaphoreType.DMA((2, n + 1)),
        ],
        input_output_aliases={3 + n + len(last) + i: i for i in range(len(held))},
        compiler_params=params(12),
        cost_estimate=cost(1<<33, 1<<20),
        name="result",
    )(solve, left, merged, *totals, *last, *held)


def tie_kernel(value_ref, after_ref, out_ref):
    del value_ref, after_ref, out_ref


def tie(value, after):
    return pl.pallas_call(
        tie_kernel,
        out_shape=jax.ShapeDtypeStruct(value.shape, value.dtype),
        in_specs=[ANY] * 2,
        out_specs=ANY,
        input_output_aliases={0: 0},
        compiler_params=params(4),
        name="tie",
    )(value, after)


def body(gradient, error, q_start):
    rank = q_start.shape[0]
    replicas = SIZES[0] * SIZES[1]
    merged, p = merge(gradient[0], error[0], q_start)
    a, b, c = ring_x_or_z([p] * 3, 0)
    p = (p + a) + (b + c)
    sent, ext, p_mean, pieces = first_right(
        (2,), (p, *ring_x_or_z([p] * 3, 1)), merged, rank, replicas
    )
    got = swap(sent)
    sent = next_right(False, (1, 3, 0), pieces, merged, ext)
    got_next = swap(sent)
    kept = next_right(True, (2,), pieces, merged, sent)
    two, ext, weight = first_pair(kept, got, ext)
    (two,) = ring_x_or_z((two,), 0, (2,))
    kept = next_right(True, (1, 3, 0), pieces, merged, weight)
    *near, own = next_pair(kept, got_next, weight)
    own, *sent = add_quarters((own, *ring_x_or_z(near, 0, (1, 3)), two))
    part = add_parts((own, *ring_x_or_z(sent, 1)), ext)
    total, ext = across((part, *ring_y(part)), ext.shape[0])
    solve, left, p_hat = factor(ext, p_mean, replicas)
    total = assemble((total, *ring_x_or_z([total] * 3, 1)), solve)
    two, one, three = ring_x_or_z([total] * 3, 0, (2, 1, 3))

    def write(sources, totals, *after):
        return result(sources, totals, merged, solve, left, *after)

    own, other = True, False
    *out, _ = write(((own, 0),), (total,), None)
    *out, token = write(((other, 0),), (swap(total),), out)
    two = tie(two, token)
    *out, token = write(((own, 2),), (two,), out)
    one, three = tie(one, token), tie(three, token)
    *out, _ = write(((own, 1), (own, 3), (other, 2)), (one, three, swap(two)), out)
    new_error, q_new, _, p_hat = write(
        ((other, 1), (other, 3)), (swap(one), swap(three)), out, p_hat
    )
    return (new_error[None], p_hat, q_new)


def solution(mesh):
    fine = Mesh(mesh.devices.reshape(SIZES), AXES)
    return jax.shard_map(
        body,
        mesh=fine,
        in_specs=(P(DP, ("y", "c"), None), P(DP, ("y", "c"), None), P()),
        out_specs=(P(DP, ("y", "c"), None), P(None, ("y", "c")), P()),
        check_vma=False,
    )
```

```python
import functools

import jax
import jax.numpy as jnp
from jax import lax
from jax.experimental import pallas as pl
from jax.experimental.pallas import tpu as pltpu
from jax.sharding import Mesh, PartitionSpec as P

DP = ("z", "x")
AXES = ("z", "x", "y", "c")
SIZES = (4, 4, 4, 2)
HIGHEST = lax.Precision.HIGHEST
F32 = jnp.float32
BF16 = jnp.bfloat16
MIB = 1 << 20
ROWS = 8
QUARTERS = 4
RIGHT = 1 << 33
SHIFTS = (1, 3, 2)
ANY = pl.BlockSpec(memory_space=pl.ANY)
WHOLE = pl.BlockSpec(memory_space=pltpu.VMEM)


def params(mib):
    return pltpu.CompilerParams(vmem_limit_bytes=mib * MIB)


def cost(flops, nbytes):
    return pl.CostEstimate(flops=flops, bytes_accessed=nbytes, transcendentals=0)


def half_of(x, y, z, c):
    return (x + y + z + c) % 2


def place():
    x, y, z, c = (lax.axis_index(a) for a in ("x", "y", "z", "c"))
    half = half_of(x, y, z, c)
    return half, jnp.where(half == 0, x, z), jnp.where(half == 0, z, x)


def index(z, x, y, c):
    return ((z * SIZES[1] + x) * SIZES[2] + y) * SIZES[3] + c


def everyone():
    return [
        (z, x, y, c)
        for z in range(SIZES[0])
        for x in range(SIZES[1])
        for y in range(SIZES[2])
        for c in range(SIZES[3])
    ]


def ring_x_or_z(values, phase, shifts=SHIFTS, halves=True):
    out = []
    for k, value in zip(shifts, values):
        pairs = []
        for z, x, y, c in everyone():
            along_x = (half_of(x, y, z, c) if halves else c) == phase
            to = (z, (x + k) % SIZES[1], y) if along_x else ((z + k) % SIZES[0], x, y)
            pairs.append((index(z, x, y, c), index(*to, (c + k) % 2 if halves else c)))
        out.append(lax.ppermute(value, AXES, pairs))
    return out


def ring_y(value):
    out = []
    for k in SHIFTS:
        pairs = [
            (index(z, x, y, c), index(z, x, (y + k) % SIZES[2], (c + k) % 2))
            for z, x, y, c in everyone()
        ]
        out.append(lax.ppermute(value, AXES, pairs))
    return out


def swap(value):
    return lax.ppermute(value, "c", [(0, 1), (1, 0)])


def merge_kernel(width, g_hbm, e_hbm, q_hbm, m_ref, p_ref, g_ref, e_ref, q_ref, sems):
    rows, columns = g_ref.shape
    rank = q_ref.shape[0]
    steps = columns // width

    def copies(i):
        at = pl.ds(i * width, width)
        return [
            pltpu.make_async_copy(src.at[:, at], dst.at[:, at], sems.at[n, i])
            for n, (src, dst) in enumerate(((g_hbm, g_ref), (e_hbm, e_ref), (q_hbm, q_ref)))
        ]

    for i in range(steps):
        for c in copies(i):
            c.start()
    acc = jnp.zeros((rows, rank), F32)
    for i in range(steps):
        for c in copies(i):
            c.wait()
        at = pl.ds(i * width, width)
        m = (g_ref[:, at].astype(F32) + e_ref[:, at].astype(F32)).astype(BF16)
        m_ref[:, at] = m
        acc = acc + lax.dot_general(
            m, q_ref[:, at], (((1,), (1,)), ((), ())), preferred_element_type=F32
        )
    p_ref[...] = pack(acc.T)


def pack(p):
    rank, rows = p.shape
    full = rows // 128
    half = rank // 2
    parts = [p[:, i * 128 : (i + 1) * 128] for i in range(full)]
    rest = p[:, full * 128 :]
    return jnp.concatenate(parts + [jnp.concatenate([rest[:half], rest[half:]], axis=1)], axis=0)


def unpack(packed, rank):
    full = packed.shape[0] // rank
    last = packed[full * rank :]
    rest = jnp.concatenate([last[:, :64], last[:, 64:]], axis=0)
    return jnp.concatenate(
        [packed[i * rank : (i + 1) * rank] for i in range(full)] + [rest], axis=1
    )


def merge(gradient, error, q_start):
    rows, columns = gradient.shape
    rank = q_start.shape[0]
    width = 1024
    gradient, error, q_start = (
        pltpu.with_memory_space_constraint(a, pltpu.HBM) for a in (gradient, error, q_start)
    )
    return pl.pallas_call(
        functools.partial(merge_kernel, width),
        out_shape=[pltpu.VMEM((rows, columns), BF16), pltpu.VMEM((rank * rows // 128, 128), F32)],
        in_specs=[ANY, ANY, ANY],
        out_specs=[WHOLE, WHOLE],
        scratch_shapes=[
            pltpu.VMEM((rows, columns), BF16),
            pltpu.VMEM((rows, columns), BF16),
            pltpu.VMEM((rank, columns), BF16),
            pltpu.SemaphoreType.DMA((3, columns // width)),
        ],
        compiler_params=params(24),
        cost_estimate=cost(2 * rank * rows * columns, 4 * rows * columns),
        name="merge",
    )(gradient, error, q_start)


def right_tiles(quarters, pieces, m_ref, out_ref):
    rank = pieces.shape[0] // 3
    width = m_ref.shape[1] // 2 // QUARTERS
    to = 0
    for quarter in quarters:
        at = pl.multiple_of(quarter * width, width)
        t = jnp.dot(pieces, m_ref[:, pl.ds(at, width)], preferred_element_type=F32)
        t = t[:rank] + (t[rank : 2 * rank] + t[2 * rank :])
        for g in range(rank // ROWS):
            for n in range(width // 128):
                out_ref[to : to + ROWS, :] = t[g * ROWS : (g + 1) * ROWS, n * 128 : (n + 1) * 128]
                to += ROWS


def quarters_of(own, turns):
    half, one, two = place()
    half, turn = (half, one) if own else (1 - half, two)
    return [half * QUARTERS + (turn + k) % QUARTERS for k in turns]


def split(n):
    high = n.astype(BF16)
    n = n - high.astype(F32)
    middle = n.astype(BF16)
    return high, middle, (n - middle.astype(F32)).astype(BF16)


def first_right_kernel(replicas, rank, turns, a_ref, b_ref, c_ref, d_ref, m_ref, out_ref, ext_ref, p_ref, pieces_ref):
    p = (a_ref[...] + b_ref[...] + (c_ref[...] + d_ref[...])) * (1.0 / replicas)
    peak = jnp.max(jnp.abs(p), axis=(0, 1), keepdims=True)
    peak = jnp.where(peak > 0, peak, 1.0)
    p = unpack(p, rank)
    p_ref[...] = p
    pieces = jnp.concatenate(split(p / peak), axis=0)
    pieces_ref[...] = pieces
    right_tiles(quarters_of(False, turns), pieces, m_ref, out_ref)
    gram = lax.dot_general(
        p, p, (((1,), (1,)), ((), ())), precision=HIGHEST, preferred_element_type=F32
    )
    two = 2 * ROWS
    ext = jnp.concatenate(
        [
            jnp.concatenate([gram[i : i + ROWS], gram[i + ROWS : i + two]], axis=1)
            for i in range(0, rank, two)
        ]
        + [jnp.broadcast_to(peak, (ROWS, 128))],
        axis=0,
    )
    ext_ref[...] = ext
    out_ref[out_ref.shape[0] - ext.shape[0] :, :] = ext


def next_right_kernel(own, turns, pieces_ref, m_ref, after_ref, out_ref):
    del after_ref
    right_tiles(quarters_of(own, turns), pieces_ref[...], m_ref, out_ref)


def first_right(turns, parts, merged, rank, replicas):
    rows, columns = merged.shape
    size = rank * columns // 1024
    extra = rank * rank // 128 + ROWS
    return pl.pallas_call(
        functools.partial(first_right_kernel, replicas, rank, turns),
        out_shape=[
            jax.ShapeDtypeStruct((size + extra, 128), F32),
            pltpu.VMEM((extra, 128), F32),
            pltpu.VMEM((rank, rows), F32),
            pltpu.VMEM((3 * rank, rows), BF16),
        ],
        in_specs=[WHOLE] * 5,
        out_specs=[WHOLE] * 4,
        compiler_params=params(12),
        cost_estimate=cost(RIGHT, 1 << 20),
        name="first_right",
    )(*parts, merged)


def next_right(own, turns, pieces, merged, after):
    size = pieces.shape[0] // 3 * merged.shape[1] // 1024 * len(turns)
    return pl.pallas_call(
        functools.partial(next_right_kernel, own, turns),
        out_shape=jax.ShapeDtypeStruct((size, 128), F32),
        in_specs=[WHOLE, WHOLE, ANY],
        out_specs=WHOLE,
        compiler_params=params(12),
        cost_estimate=cost(RIGHT, 1 << 20),
        name="next_right",
    )(pieces, merged, after)


def first_pair_kernel(kept_ref, got_ref, ext_ref, out_ref, pair_ref, weight_ref):
    grams = ext_ref.shape[0] - ROWS
    size = kept_ref.shape[0]
    own, its = ext_ref[grams : grams + 1, :1], got_ref[size + grams : size + grams + 1, :1]
    top = jnp.maximum(own, its)
    pair_ref[:grams] = ext_ref[:grams] + got_ref[size : size + grams]
    pair_ref[grams:] = jnp.broadcast_to(top, (ROWS, 128))
    own, its = own / top, its / top
    weight_ref[:ROWS] = jnp.broadcast_to(own, (ROWS, 128))
    weight_ref[ROWS:] = jnp.broadcast_to(its, (ROWS, 128))
    out_ref[...] = kept_ref[...] * own + got_ref[:size] * its


def first_pair(kept, got, ext):
    return pl.pallas_call(
        first_pair_kernel,
        out_shape=[
            jax.ShapeDtypeStruct(kept.shape, F32),
            pltpu.VMEM(ext.shape, F32),
            pltpu.VMEM((2 * ROWS, 128), F32),
        ],
        in_specs=[WHOLE] * 3,
        out_specs=[WHOLE] * 3,
        compiler_params=params(8),
        name="first_pair",
    )(kept, got, ext)


def next_pair_kernel(kept_ref, got_ref, weight_ref, *out):
    own, its = weight_ref[:1, :1], weight_ref[ROWS : ROWS + 1, :1]
    size = out[0].shape[0]
    for n, ref in enumerate(out):
        at = slice(n * size, (n + 1) * size)
        ref[...] = kept_ref[at] * own + got_ref[at] * its


def next_pair(kept, got, weight):
    size = kept.shape[0] // 3
    return pl.pallas_call(
        next_pair_kernel,
        out_shape=[jax.ShapeDtypeStruct((size, 128), F32)] * 3,
        in_specs=[WHOLE] * 3,
        out_specs=[WHOLE] * 3,
        compiler_params=params(8),
        name="next_pair",
    )(kept, got, weight)


def add_quarters_kernel(a_ref, b_ref, c_ref, d_ref, *out):
    size = a_ref.shape[0] // QUARTERS
    for k, ref in zip((0,) + SHIFTS, out):
        at = pl.ds(pl.multiple_of((place()[2] + k) % QUARTERS * size, size), size)
        ref[...] = (a_ref[at] + b_ref[at]) + (c_ref[at] + d_ref[at])


def add_quarters(parts):
    size = parts[0].shape[0] // QUARTERS
    return pl.pallas_call(
        add_quarters_kernel,
        out_shape=[jax.ShapeDtypeStruct((size, 128), F32)] * QUARTERS,
        in_specs=[WHOLE] * QUARTERS,
        out_specs=[WHOLE] * QUARTERS,
        compiler_params=params(8),
        name="add_quarters",
    )(*parts)


def add_parts_kernel(a_ref, b_ref, c_ref, d_ref, ext_ref, out_ref):
    size = a_ref.shape[0]
    out_ref[:size] = (a_ref[...] + b_ref[...]) + (c_ref[...] + d_ref[...])
    out_ref[size:] = ext_ref[...]


def add_parts(parts, ext):
    return pl.pallas_call(
        add_parts_kernel,
        out_shape=jax.ShapeDtypeStruct((parts[0].shape[0] + ext.shape[0], 128), F32),
        in_specs=[WHOLE] * 5,
        out_specs=WHOLE,
        compiler_params=params(8),
        name="add_parts",
    )(*parts, ext)


def across_kernel(a_ref, b_ref, c_ref, d_ref, out_ref, ext_ref):
    size = out_ref.shape[0]
    grams = ext_ref.shape[0] - ROWS
    refs = (a_ref, b_ref, c_ref, d_ref)
    peaks = [r[size + grams : size + grams + 1, :1] for r in refs]
    top = jnp.maximum(jnp.maximum(peaks[0], peaks[1]), jnp.maximum(peaks[2], peaks[3]))
    a, b, c, d = (r[:size] * (k / top) for r, k in zip(refs, peaks))
    out_ref[...] = (a + b) + (c + d)
    a, b, c, d = (r[size : size + grams] for r in refs)
    ext_ref[:grams] = (a + b) + (c + d)
    ext_ref[grams:] = jnp.broadcast_to(top, (ROWS, 128))


def across(parts, extra):
    return pl.pallas_call(
        across_kernel,
        out_shape=[
            jax.ShapeDtypeStruct((parts[0].shape[0] - extra, 128), F32),
            pltpu.VMEM((extra, 128), F32),
        ],
        in_specs=[WHOLE] * 4,
        out_specs=[WHOLE] * 2,
        compiler_params=params(8),
        name="across",
    )(*parts)


def assemble_kernel(a_ref, b_ref, c_ref, d_ref, after_ref, out_ref):
    del after_ref
    size = a_ref.shape[0]
    for k, ref in zip((0,) + SHIFTS, (a_ref, b_ref, c_ref, d_ref)):
        at = pl.multiple_of((place()[2] + QUARTERS - k) % QUARTERS * size, size)
        out_ref[pl.ds(at, size)] = ref[...]


def assemble(parts, after):
    return pl.pallas_call(
        assemble_kernel,
        out_shape=jax.ShapeDtypeStruct((parts[0].shape[0] * QUARTERS, 128), F32),
        in_specs=[WHOLE] * 4 + [ANY],
        out_specs=WHOLE,
        compiler_params=params(8),
        name="assemble",
    )(*parts, after)


def factor_kernel(replicas, ext_ref, p_ref, solve_ref, left_ref, hat_ref):
    rank = p_ref.shape[0]
    groups = rank // ROWS
    sub = lax.broadcasted_iota(jnp.int32, (ROWS, 2 * rank), 0)
    lane = lax.broadcasted_iota(jnp.int32, (ROWS, 2 * rank), 1)
    blocks = []
    for g in range(groups):
        tile = ext_ref[g // 2 * ROWS : (g // 2 + 1) * ROWS, (g % 2) * rank : (g % 2 + 1) * rank]
        unit = jnp.where(lane[:, :rank] == sub[:, :rank] + g * ROWS, 1.0, 0.0)
        blocks.append(jnp.concatenate([tile, unit], axis=1))
    for own in range(groups):
        spread = lambda g: [
            jnp.broadcast_to(blocks[g][:, own * ROWS + k : own * ROWS + k + 1], (ROWS, 2 * rank))
            for k in range(ROWS)
        ]
        columns = spread(own)
        rows, heads = [], []
        for k in range(ROWS):
            scale = 1.0 / columns[k][k : k + 1]
            row = blocks[own][k : k + 1] * scale
            head = {m: columns[m][k : k + 1] * scale for m in range(k + 1, ROWS)}
            factors = jnp.where(sub > k, columns[k], 0.0)
            blocks[own] = blocks[own] - factors * row
            for m, h in head.items():
                columns[m] = columns[m] - factors * h
            rows.append(row)
            heads.append(head)
        for g in range(own + 1, groups):
            columns = spread(g)
            for k in range(ROWS):
                blocks[g] = blocks[g] - columns[k] * rows[k]
                for m, h in heads[k].items():
                    columns[m] = columns[m] - columns[k] * h
    inverse = []
    for g in range(groups):
        diagonal = jnp.sum(
            jnp.where(lane == sub + g * ROWS, blocks[g], 0.0), axis=1, keepdims=True
        )
        inverse.append(blocks[g][:, rank:] / jnp.sqrt(diagonal))
    inverse = jnp.concatenate(inverse, axis=0)
    grams = ext_ref.shape[0] - ROWS
    s1, s2, s3 = split(inverse * (ext_ref[grams : grams + 1, :1] * (1.0 / replicas)))
    solve_ref[...] = jnp.concatenate([s1, s1, s2, s2, s1, s3], axis=1)
    hat = jnp.dot(inverse, p_ref[...], precision=HIGHEST, preferred_element_type=F32)
    hat_ref[...] = hat
    left_ref[...] = hat.T.astype(BF16)


def factor(ext, p_mean, replicas):
    rank, rows = p_mean.shape
    return pl.pallas_call(
        functools.partial(factor_kernel, replicas),
        out_shape=[
            jax.ShapeDtypeStruct((rank, 6 * rank), BF16),
            jax.ShapeDtypeStruct((rows, rank), BF16),
            jax.ShapeDtypeStruct((rank, rows), F32),
        ],
        in_specs=[WHOLE] * 2,
        out_specs=[WHOLE] * 3,
        compiler_params=params(8),
        cost_estimate=cost(1 << 32, 1 << 20),
        name="factor",
    )(ext, p_mean)


def result_kernel(sources, last, width, solve_ref, left_ref, m_ref, *refs):
    if last:
        hat_hbm, refs = refs[-4], refs[:-4] + refs[-3:]
        hat = pltpu.make_async_copy(refs[len(sources)], hat_hbm, refs[-1].at[0, len(sources)])
        hat.start()
    error_hbm, q_hbm, token_ref, error_ref, q_ref, sems = refs[-6:]
    token_ref[...] = jnp.zeros_like(token_ref)
    rank = solve_ref.shape[0]
    columns = q_ref.shape[2]
    left = left_ref[...]
    solve = solve_ref[...]

    def copies(n, base, at, size):
        to, here = pl.ds(pl.multiple_of(base + at, 128), size), pl.ds(at, size)
        return (
            pltpu.make_async_copy(error_ref.at[n, :, here], error_hbm.at[:, to], sems.at[0, n]),
            pltpu.make_async_copy(q_ref.at[n, :, here], q_hbm.at[:, to], sems.at[1, n]),
        )

    bases = []
    for n, (own, k) in enumerate(sources):
        t_ref = refs[n]
        half, one, two = place()
        half, turn = (half, one) if own else (1 - half, two)
        quarter = (turn + QUARTERS - k) % QUARTERS
        base = (half * QUARTERS + quarter) * columns
        bases.append(base)
        for at in range(0, columns, width):
            t = jnp.concatenate(
                [
                    jnp.concatenate(
                        [
                            t_ref[(g * columns + i) // 128 * ROWS : (g * columns + i) // 128 * ROWS + ROWS, :]
                            for i in range(at, at + width, 128)
                        ],
                        axis=1,
                    )
                    for g in range(rank // ROWS)
                ],
                axis=0,
            )
            t1, t2, t3 = split(t)
            t = jnp.concatenate([t1, t2, t1, t2, t3, t1], axis=0)
            new = jnp.dot(solve, t, preferred_element_type=F32)
            q_ref[n, :, at : at + width] = new
            decoded = jnp.dot(left, new.astype(BF16), preferred_element_type=F32)
            m = m_ref[:, pl.ds(pl.multiple_of(base + at, 128), width)]
            error_ref[n, :, at : at + width] = (m.astype(F32) - decoded).astype(BF16)
            for c in copies(n, base, at, width):
                c.start()
    for n, base in enumerate(bases):
        for c in copies(n, base, 0, columns):
            c.wait()
    if last:
        hat.wait()


def result(sources, totals, merged, solve, left, before, p_hat=None):
    rank = solve.shape[0]
    rows, columns = merged.shape
    quarter = columns // 2 // QUARTERS
    n = len(sources)
    held = [] if before is None else list(before)
    last = [] if p_hat is None else [p_hat]
    return pl.pallas_call(
        functools.partial(result_kernel, sources, bool(last), quarter // 2),
        out_shape=[
            pltpu.HBM((rows, columns), BF16),
            pltpu.HBM((rank, columns), F32),
            pltpu.VMEM((ROWS, 128), F32),
        ]
        + [pltpu.HBM(a.shape, F32) for a in last],
        in_specs=[WHOLE] * (3 + n + len(last)) + [ANY] * len(held),
        out_specs=[ANY, ANY, WHOLE] + [ANY] * len(last),
        scratch_shapes=[
            pltpu.VMEM((n, rows, quarter), BF16),
            pltpu.VMEM((n, rank, quarter), F32),
            pltpu.SemaphoreType.DMA((2, n + 1)),
        ],
        input_output_aliases={3 + n + len(last) + i: i for i in range(len(held))},
        compiler_params=params(12),
        cost_estimate=cost(1<<33, 1<<20),
        name="result",
    )(solve, left, merged, *totals, *last, *held)


def tie_kernel(value_ref, after_ref, out_ref):
    del value_ref, after_ref, out_ref


def tie(value, after):
    return pl.pallas_call(
        tie_kernel,
        out_shape=jax.ShapeDtypeStruct(value.shape, value.dtype),
        in_specs=[ANY] * 2,
        out_specs=ANY,
        input_output_aliases={0: 0},
        compiler_params=params(4),
        name="tie",
    )(value, after)


def body(gradient, error, q_start):
    rank = q_start.shape[0]
    replicas = SIZES[0] * SIZES[1]
    merged, p = merge(gradient[0], error[0], q_start)
    a, b, c = ring_x_or_z([p] * 3, 0, halves=False)
    p = (p + a) + (b + c)
    sent, ext, p_mean, pieces = first_right(
        (2,), (p, *ring_x_or_z([p] * 3, 1, halves=False)), merged, rank, replicas
    )
    got = swap(sent)
    sent = next_right(False, (1, 3, 0), pieces, merged, ext)
    got_next = swap(sent)
    kept = next_right(True, (2,), pieces, merged, sent)
    two, ext, weight = first_pair(kept, got, ext)
    (two,) = ring_x_or_z((two,), 0, (2,))
    kept = next_right(True, (1, 3, 0), pieces, merged, weight)
    *near, own = next_pair(kept, got_next, weight)
    own, *sent = add_quarters((own, *ring_x_or_z(near, 0, (1, 3)), two))
    part = add_parts((own, *ring_x_or_z(sent, 1)), ext)
    total, ext = across((part, *ring_y(part)), ext.shape[0])
    solve, left, p_hat = factor(ext, p_mean, replicas)
    total = assemble((total, *ring_x_or_z([total] * 3, 1)), solve)
    two, one, three = ring_x_or_z([total] * 3, 0, (2, 1, 3))

    def write(sources, totals, *after):
        return result(sources, totals, merged, solve, left, *after)

    own, other = True, False
    *out, _ = write(((own, 0),), (total,), None)
    *out, token = write(((other, 0),), (swap(total),), out)
    two = tie(two, token)
    *out, token = write(((own, 2),), (two,), out)
    one, three = tie(one, token), tie(three, token)
    *out, _ = write(((own, 1), (own, 3), (other, 2)), (one, three, swap(two)), out)
    new_error, q_new, _, p_hat = write(
        ((other, 1), (other, 3)), (swap(one), swap(three)), out, p_hat
    )
    return (new_error[None], p_hat, q_new)


def solution(mesh):
    fine = Mesh(mesh.devices.reshape(SIZES), AXES)
    return jax.shard_map(
        body,
        mesh=fine,
        in_specs=(P(DP, ("y", "c"), None), P(DP, ("y", "c"), None), P()),
        out_specs=(P(DP, ("y", "c"), None), P(None, ("y", "c")), P()),
        check_vma=False,
    )
```

```python
import functools

import jax
import jax.numpy as jnp
from jax import lax
from jax.experimental import pallas as pl
from jax.experimental.pallas import tpu as pltpu
from jax.sharding import Mesh, PartitionSpec as P

DP = ("z", "x")
AXES = ("z", "x", "y", "c")
SIZES = (4, 4, 4, 2)
HIGHEST = lax.Precision.HIGHEST
F32 = jnp.float32
BF16 = jnp.bfloat16
MIB = 1 << 20
ROWS = 8
QUARTERS = 4
RIGHT = 1 << 33
SHIFTS = (1, 3, 2)
ANY = pl.BlockSpec(memory_space=pl.ANY)
WHOLE = pl.BlockSpec(memory_space=pltpu.VMEM)


def params(mib):
    return pltpu.CompilerParams(vmem_limit_bytes=mib * MIB)


def cost(flops, nbytes):
    return pl.CostEstimate(flops=flops, bytes_accessed=nbytes, transcendentals=0)


def half_of(x, y, z, c):
    return (x + y + z + c) % 2


def core_of(x, y, z, c):
    return c


def place():
    x, y, z, c = (lax.axis_index(a) for a in ("x", "y", "z", "c"))
    half = half_of(x, y, z, c)
    return half, jnp.where(half == 0, x, z), jnp.where(half == 0, z, y)


def other_place():
    x, y, z, c = (lax.axis_index(a) for a in ("x", "y", "z", "c"))
    half = 1 - half_of(x, y, z, c)
    return half, jnp.where(half == 0, x, z), jnp.where(half == 0, z, y)


def index(z, x, y, c):
    return ((z * SIZES[1] + x) * SIZES[2] + y) * SIZES[3] + c


def everyone():
    return [
        (z, x, y, c)
        for z in range(SIZES[0])
        for x in range(SIZES[1])
        for y in range(SIZES[2])
        for c in range(SIZES[3])
    ]


def ring(values, phase, shifts=SHIFTS, orders=("xzy", "zyx"), group=half_of):
    out = []
    for k, value in zip(shifts, values):
        pairs = []
        for z, x, y, c in everyone():
            to = {"z": z, "x": x, "y": y}
            axis = orders[group(x, y, z, c)][phase]
            to[axis] = (to[axis] + k) % SIZES[AXES.index(axis)]
            core = c if group is core_of else (c + k) % 2
            pairs.append((index(z, x, y, c), index(*to.values(), core)))
        out.append(lax.ppermute(value, AXES, pairs))
    return out


def swap(value):
    return lax.ppermute(value, "c", [(0, 1), (1, 0)])


def merge_kernel(cuts, g_hbm, e_hbm, q_hbm, m_ref, p_ref, g_ref, e_ref, q_ref, sems):
    rows = g_ref.shape[0]
    rank = q_ref.shape[0]

    def copies(i):
        at = pl.ds(cuts[i], cuts[i + 1] - cuts[i])
        return [
            pltpu.make_async_copy(src.at[:, at], dst.at[:, at], sems.at[n, i])
            for n, (src, dst) in enumerate(((g_hbm, g_ref), (e_hbm, e_ref), (q_hbm, q_ref)))
        ]

    for i in range(len(cuts) - 1):
        for c in copies(i):
            c.start()
    acc = jnp.zeros((rows, rank), F32)
    for i in range(len(cuts) - 1):
        for c in copies(i):
            c.wait()
        at = pl.ds(cuts[i], cuts[i + 1] - cuts[i])
        m = (g_ref[:, at].astype(F32) + e_ref[:, at].astype(F32)).astype(BF16)
        m_ref[:, at] = m
        acc = acc + lax.dot_general(
            m, q_ref[:, at], (((1,), (1,)), ((), ())), preferred_element_type=F32
        )
    p_ref[...] = pack(acc.T)


def pack(p):
    rank, rows = p.shape
    full = rows // 128
    half = rank // 2
    parts = [p[:, i * 128 : (i + 1) * 128] for i in range(full)]
    rest = p[:, full * 128 :]
    return jnp.concatenate(parts + [jnp.concatenate([rest[:half], rest[half:]], axis=1)], axis=0)


def unpack(packed, rank):
    full = packed.shape[0] // rank
    last = packed[full * rank :]
    rest = jnp.concatenate([last[:, :64], last[:, 64:]], axis=0)
    return jnp.concatenate(
        [packed[i * rank : (i + 1) * rank] for i in range(full)] + [rest], axis=1
    )


def merge(gradient, error, q_start):
    rows, columns = gradient.shape
    rank = q_start.shape[0]
    step = columns // 20
    cuts = [n * step for n in (0, 2, 4, 6, 8, 10, 12, 14, 16, 18, 19, 20)]
    gradient, error, q_start = (
        pltpu.with_memory_space_constraint(a, pltpu.HBM) for a in (gradient, error, q_start)
    )
    return pl.pallas_call(
        functools.partial(merge_kernel, cuts),
        out_shape=[pltpu.VMEM((rows, columns), BF16), pltpu.VMEM((rank * rows // 128, 128), F32)],
        in_specs=[ANY, ANY, ANY],
        out_specs=[WHOLE, WHOLE],
        scratch_shapes=[
            pltpu.VMEM((rows, columns), BF16),
            pltpu.VMEM((rows, columns), BF16),
            pltpu.VMEM((rank, columns), BF16),
            pltpu.SemaphoreType.DMA((3, len(cuts) - 1)),
        ],
        compiler_params=params(24),
        cost_estimate=cost(2 * rank * rows * columns, 4 * rows * columns),
        name="merge",
    )(gradient, error, q_start)


def right_tiles(quarters, pieces, m_ref, out_ref):
    rank = pieces.shape[0] // 3
    width = m_ref.shape[1] // 2 // QUARTERS
    to = 0
    for quarter in quarters:
        at = pl.multiple_of(quarter * width, width)
        t = jnp.dot(pieces, m_ref[:, pl.ds(at, width)], preferred_element_type=F32)
        t = t[:rank] + (t[rank : 2 * rank] + t[2 * rank :])
        for g in range(rank // ROWS):
            for n in range(width // 128):
                out_ref[to : to + ROWS, :] = t[g * ROWS : (g + 1) * ROWS, n * 128 : (n + 1) * 128]
                to += ROWS


def quarters_of(own, turns):
    half, turn, _ = place() if own else other_place()
    return [half * QUARTERS + (turn + k) % QUARTERS for k in turns]


def split(n):
    high = n.astype(BF16)
    n = n - high.astype(F32)
    middle = n.astype(BF16)
    return high, middle, (n - middle.astype(F32)).astype(BF16)


def first_right_kernel(replicas, rank, turns, a_ref, b_ref, c_ref, d_ref, m_ref, out_ref, ext_ref, p_ref, pieces_ref):
    p = (a_ref[...] + b_ref[...] + (c_ref[...] + d_ref[...])) * (1.0 / replicas)
    peak = jnp.max(jnp.abs(p), axis=(0, 1), keepdims=True)
    peak = jnp.where(peak > 0, peak, 1.0)
    p = unpack(p, rank)
    p_ref[...] = p
    pieces = jnp.concatenate(split(p / peak), axis=0)
    pieces_ref[...] = pieces
    right_tiles(quarters_of(False, turns), pieces, m_ref, out_ref)
    gram = lax.dot_general(
        p, p, (((1,), (1,)), ((), ())), precision=HIGHEST, preferred_element_type=F32
    )
    two = 2 * ROWS
    ext = jnp.concatenate(
        [
            jnp.concatenate([gram[i : i + ROWS], gram[i + ROWS : i + two]], axis=1)
            for i in range(0, rank, two)
        ]
        + [jnp.broadcast_to(peak, (ROWS, 128))],
        axis=0,
    )
    ext_ref[...] = ext
    out_ref[out_ref.shape[0] - ext.shape[0] :, :] = ext


def next_right_kernel(own, turns, pieces_ref, m_ref, after_ref, out_ref):
    del after_ref
    right_tiles(quarters_of(own, turns), pieces_ref[...], m_ref, out_ref)


def first_right(turns, parts, merged, rank, replicas):
    rows, columns = merged.shape
    size = rank * columns // 1024
    extra = rank * rank // 128 + ROWS
    return pl.pallas_call(
        functools.partial(first_right_kernel, replicas, rank, turns),
        out_shape=[
            jax.ShapeDtypeStruct((size + extra, 128), F32),
            pltpu.VMEM((extra, 128), F32),
            pltpu.VMEM((rank, rows), F32),
            pltpu.VMEM((3 * rank, rows), BF16),
        ],
        in_specs=[WHOLE] * 5,
        out_specs=[WHOLE] * 4,
        compiler_params=params(12),
        cost_estimate=cost(RIGHT, 1 << 20),
        name="first_right",
    )(*parts, merged)


def next_right(own, turns, pieces, merged, after):
    size = pieces.shape[0] // 3 * merged.shape[1] // 1024 * len(turns)
    return pl.pallas_call(
        functools.partial(next_right_kernel, own, turns),
        out_shape=jax.ShapeDtypeStruct((size, 128), F32),
        in_specs=[WHOLE, WHOLE, ANY],
        out_specs=WHOLE,
        compiler_params=params(12),
        cost_estimate=cost(RIGHT, 1 << 20),
        name="next_right",
    )(pieces, merged, after)


def first_pair_kernel(kept_ref, got_ref, ext_ref, out_ref, pair_ref, weight_ref):
    grams = ext_ref.shape[0] - ROWS
    size = kept_ref.shape[0]
    own, its = ext_ref[grams : grams + 1, :1], got_ref[size + grams : size + grams + 1, :1]
    top = jnp.maximum(own, its)
    pair_ref[:grams] = ext_ref[:grams] + got_ref[size : size + grams]
    pair_ref[grams:] = jnp.broadcast_to(top, (ROWS, 128))
    own, its = own / top, its / top
    weight_ref[:ROWS] = jnp.broadcast_to(own, (ROWS, 128))
    weight_ref[ROWS:] = jnp.broadcast_to(its, (ROWS, 128))
    out_ref[...] = kept_ref[...] * own + got_ref[:size] * its


def first_pair(kept, got, ext):
    return pl.pallas_call(
        first_pair_kernel,
        out_shape=[
            jax.ShapeDtypeStruct(kept.shape, F32),
            pltpu.VMEM(ext.shape, F32),
            pltpu.VMEM((2 * ROWS, 128), F32),
        ],
        in_specs=[WHOLE] * 3,
        out_specs=[WHOLE] * 3,
        compiler_params=params(8),
        name="first_pair",
    )(kept, got, ext)


def next_pair_kernel(kept_ref, got_ref, weight_ref, *out):
    own, its = weight_ref[:1, :1], weight_ref[ROWS : ROWS + 1, :1]
    size = out[0].shape[0]
    for n, ref in enumerate(out):
        at = slice(n * size, (n + 1) * size)
        ref[...] = kept_ref[at] * own + got_ref[at] * its


def next_pair(kept, got, weight):
    size = kept.shape[0] // 3
    return pl.pallas_call(
        next_pair_kernel,
        out_shape=[jax.ShapeDtypeStruct((size, 128), F32)] * 3,
        in_specs=[WHOLE] * 3,
        out_specs=[WHOLE] * 3,
        compiler_params=params(8),
        name="next_pair",
    )(kept, got, weight)


def add_quarters_kernel(a_ref, b_ref, c_ref, d_ref, ext_ref, *out):
    size = a_ref.shape[0] // QUARTERS
    for k, ref in zip((0,) + SHIFTS, out):
        at = pl.ds(pl.multiple_of((place()[2] + k) % QUARTERS * size, size), size)
        ref[:size] = (a_ref[at] + b_ref[at]) + (c_ref[at] + d_ref[at])
        ref[size:] = ext_ref[...]


def add_quarters(parts, ext):
    size = parts[0].shape[0] // QUARTERS
    return pl.pallas_call(
        add_quarters_kernel,
        out_shape=[jax.ShapeDtypeStruct((size + ext.shape[0], 128), F32)] * QUARTERS,
        in_specs=[WHOLE] * (QUARTERS + 1),
        out_specs=[WHOLE] * QUARTERS,
        compiler_params=params(8),
        name="add_quarters",
    )(*parts, ext)


def across_kernel(half_along_y, a_ref, b_ref, c_ref, d_ref, out_ref, ext_ref):
    grams = ext_ref.shape[0] - ROWS
    size = a_ref.shape[0] - grams - ROWS
    refs = (a_ref, b_ref, c_ref, d_ref)
    peaks = [r[size + grams : size + grams + 1, :1] for r in refs]
    top = jnp.maximum(jnp.maximum(peaks[0], peaks[1]), jnp.maximum(peaks[2], peaks[3]))
    a, b, c, d = (r[:size] * (k / top) for r, k in zip(refs, peaks))
    out_ref[:size] = (a + b) + (c + d)
    a, b, c, d = (r[size : size + grams] for r in refs)
    gram = jnp.where(place()[0] == half_along_y, (a + b) + (c + d), a)
    ext_ref[:grams] = gram
    ext_ref[grams:] = jnp.broadcast_to(top, (ROWS, 128))
    if out_ref.shape[0] > size:
        out_ref[size : size + grams] = gram
        out_ref[size + grams :] = jnp.broadcast_to(top, (ROWS, 128))


def across(half_along_y, parts, extra, keep):
    rows = parts[0].shape[0]
    return pl.pallas_call(
        functools.partial(across_kernel, half_along_y),
        out_shape=[
            jax.ShapeDtypeStruct((rows if keep else rows - extra, 128), F32),
            pltpu.VMEM((extra, 128), F32),
        ],
        in_specs=[WHOLE] * 4,
        out_specs=[WHOLE] * 2,
        compiler_params=params(8),
        name="across",
    )(*parts)


def assemble_kernel(a_ref, b_ref, c_ref, d_ref, after_ref, out_ref):
    del after_ref
    size = a_ref.shape[0]
    for k, ref in zip((0,) + SHIFTS, (a_ref, b_ref, c_ref, d_ref)):
        at = pl.multiple_of((place()[2] + QUARTERS - k) % QUARTERS * size, size)
        out_ref[pl.ds(at, size)] = ref[...]


def assemble(parts, after):
    return pl.pallas_call(
        assemble_kernel,
        out_shape=jax.ShapeDtypeStruct((parts[0].shape[0] * QUARTERS, 128), F32),
        in_specs=[WHOLE] * 4 + [ANY],
        out_specs=WHOLE,
        compiler_params=params(8),
        name="assemble",
    )(*parts, after)


def factor_kernel(replicas, ext_ref, p_ref, solve_ref, left_ref, hat_ref):
    rank = p_ref.shape[0]
    groups = rank // ROWS
    sub = lax.broadcasted_iota(jnp.int32, (ROWS, 2 * rank), 0)
    lane = lax.broadcasted_iota(jnp.int32, (ROWS, 2 * rank), 1)
    blocks = []
    for g in range(groups):
        tile = ext_ref[g // 2 * ROWS : (g // 2 + 1) * ROWS, (g % 2) * rank : (g % 2 + 1) * rank]
        unit = jnp.where(lane[:, :rank] == sub[:, :rank] + g * ROWS, 1.0, 0.0)
        blocks.append(jnp.concatenate([tile, unit], axis=1))
    for own in range(groups):
        spread = lambda g: [
            jnp.broadcast_to(blocks[g][:, own * ROWS + k : own * ROWS + k + 1], (ROWS, 2 * rank))
            for k in range(ROWS)
        ]
        columns = spread(own)
        rows, heads = [], []
        for k in range(ROWS):
            scale = 1.0 / columns[k][k : k + 1]
            row = blocks[own][k : k + 1] * scale
            head = {m: columns[m][k : k + 1] * scale for m in range(k + 1, ROWS)}
            factors = jnp.where(sub > k, columns[k], 0.0)
            blocks[own] = blocks[own] - factors * row
            for m, h in head.items():
                columns[m] = columns[m] - factors * h
            rows.append(row)
            heads.append(head)
        for g in range(own + 1, groups):
            columns = spread(g)
            for k in range(ROWS):
                blocks[g] = blocks[g] - columns[k] * rows[k]
                for m, h in heads[k].items():
                    columns[m] = columns[m] - columns[k] * h
    inverse = []
    for g in range(groups):
        diagonal = jnp.sum(
            jnp.where(lane == sub + g * ROWS, blocks[g], 0.0), axis=1, keepdims=True
        )
        inverse.append(blocks[g][:, rank:] / jnp.sqrt(diagonal))
    inverse = jnp.concatenate(inverse, axis=0)
    grams = ext_ref.shape[0] - ROWS
    s1, s2, s3 = split(inverse * (ext_ref[grams : grams + 1, :1] * (1.0 / replicas)))
    solve_ref[...] = jnp.concatenate([s1, s1, s2, s2, s1, s3], axis=1)
    hat = jnp.dot(inverse, p_ref[...], precision=HIGHEST, preferred_element_type=F32)
    hat_ref[...] = hat
    left_ref[...] = hat.T.astype(BF16)


def factor(ext, p_mean, replicas):
    rank, rows = p_mean.shape
    return pl.pallas_call(
        functools.partial(factor_kernel, replicas),
        out_shape=[
            jax.ShapeDtypeStruct((rank, 6 * rank), BF16),
            jax.ShapeDtypeStruct((rows, rank), BF16),
            jax.ShapeDtypeStruct((rank, rows), F32),
        ],
        in_specs=[WHOLE] * 2,
        out_specs=[WHOLE] * 3,
        compiler_params=params(8),
        cost_estimate=cost(1 << 32, 1 << 20),
        name="factor",
    )(ext, p_mean)


def result_kernel(sources, last, width, solve_ref, left_ref, m_ref, *refs):
    if last:
        hat_hbm, refs = refs[-4], refs[:-4] + refs[-3:]
        hat = pltpu.make_async_copy(refs[len(sources)], hat_hbm, refs[-1].at[0, len(sources)])
        hat.start()
    error_hbm, q_hbm, token_ref, error_ref, q_ref, sems = refs[-6:]
    token_ref[...] = jnp.zeros_like(token_ref)
    rank = solve_ref.shape[0]
    columns = q_ref.shape[2]
    left = left_ref[...]
    solve = solve_ref[...]

    def copies(n, base, at, size):
        to, here = pl.ds(pl.multiple_of(base + at, 128), size), pl.ds(at, size)
        return (
            pltpu.make_async_copy(error_ref.at[n, :, here], error_hbm.at[:, to], sems.at[0, n]),
            pltpu.make_async_copy(q_ref.at[n, :, here], q_hbm.at[:, to], sems.at[1, n]),
        )

    bases = []
    for n, (own, k) in enumerate(sources):
        t_ref = refs[n]
        half, turn, _ = place() if own else other_place()
        quarter = (turn + QUARTERS - k) % QUARTERS
        base = (half * QUARTERS + quarter) * columns
        bases.append(base)
        for at in range(0, columns, width):
            t = jnp.concatenate(
                [
                    jnp.concatenate(
                        [
                            t_ref[(g * columns + i) // 128 * ROWS : (g * columns + i) // 128 * ROWS + ROWS, :]
                            for i in range(at, at + width, 128)
                        ],
                        axis=1,
                    )
                    for g in range(rank // ROWS)
                ],
                axis=0,
            )
            t1, t2, t3 = split(t)
            t = jnp.concatenate([t1, t2, t1, t2, t3, t1], axis=0)
            new = jnp.dot(solve, t, preferred_element_type=F32)
            q_ref[n, :, at : at + width] = new
            decoded = jnp.dot(left, new.astype(BF16), preferred_element_type=F32)
            m = m_ref[:, pl.ds(pl.multiple_of(base + at, 128), width)]
            error_ref[n, :, at : at + width] = (m.astype(F32) - decoded).astype(BF16)
            for c in copies(n, base, at, width):
                c.start()
    for n, base in enumerate(bases):
        for c in copies(n, base, 0, columns):
            c.wait()
    if last:
        hat.wait()


def result(sources, totals, merged, solve, left, before, p_hat=None):
    rank = solve.shape[0]
    rows, columns = merged.shape
    quarter = columns // 2 // QUARTERS
    n = len(sources)
    held = [] if before is None else list(before)
    last = [] if p_hat is None else [p_hat]
    return pl.pallas_call(
        functools.partial(result_kernel, sources, bool(last), quarter // 2),
        out_shape=[
            pltpu.HBM((rows, columns), BF16),
            pltpu.HBM((rank, columns), F32),
            pltpu.VMEM((ROWS, 128), F32),
        ]
        + [pltpu.HBM(a.shape, F32) for a in last],
        in_specs=[WHOLE] * (3 + n + len(last)) + [ANY] * len(held),
        out_specs=[ANY, ANY, WHOLE] + [ANY] * len(last),
        scratch_shapes=[
            pltpu.VMEM((n, rows, quarter), BF16),
            pltpu.VMEM((n, rank, quarter), F32),
            pltpu.SemaphoreType.DMA((2, n + 1)),
        ],
        input_output_aliases={3 + n + len(last) + i: i for i in range(len(held))},
        compiler_params=params(12),
        cost_estimate=cost(1<<33, 1<<20),
        name="result",
    )(solve, left, merged, *totals, *last, *held)


def tie_kernel(value_ref, after_ref, out_ref):
    del value_ref, after_ref, out_ref


def tie(value, after):
    return pl.pallas_call(
        tie_kernel,
        out_shape=jax.ShapeDtypeStruct(value.shape, value.dtype),
        in_specs=[ANY] * 2,
        out_specs=ANY,
        input_output_aliases={0: 0},
        compiler_params=params(4),
        name="tie",
    )(value, after)


def body(gradient, error, q_start):
    rank = q_start.shape[0]
    replicas = SIZES[0] * SIZES[1]
    merged, p = merge(gradient[0], error[0], q_start)
    a, b, c = ring([p] * 3, 0, orders=("xz", "zx"), group=core_of)
    p = (p + a) + (b + c)
    sent, ext, p_mean, pieces = first_right(
        (2,), (p, *ring([p] * 3, 1, orders=("xz", "zx"), group=core_of)), merged, rank, replicas
    )
    got = swap(sent)
    sent = next_right(False, (1, 3, 0), pieces, merged, ext)
    got_next = swap(sent)
    kept = next_right(True, (2,), pieces, merged, sent)
    two, ext, weight = first_pair(kept, got, ext)
    (two,) = ring((two,), 0, (2,))
    kept = next_right(True, (1, 3, 0), pieces, merged, weight)
    *near, own = next_pair(kept, got_next, weight)
    own, *sent = add_quarters((own, *ring(near, 0, (1, 3)), two), ext)
    extra = ext.shape[0]
    part, _ = across(1, (own, *ring(sent, 1)), extra, True)
    total, ext = across(0, (part, *ring([part] * 3, 2)), extra, False)
    solve, left, p_hat = factor(ext, p_mean, replicas)
    total = assemble((total, *ring([total] * 3, 1)), solve)
    two, one, three = ring([total] * 3, 0, (2, 1, 3))

    def write(sources, totals, *after):
        return result(sources, totals, merged, solve, left, *after)

    own, other = True, False
    *out, _ = write(((own, 0),), (total,), None)
    *out, token = write(((other, 0),), (swap(total),), out)
    two = tie(two, token)
    *out, token = write(((own, 2),), (two,), out)
    one, three = tie(one, token), tie(three, token)
    *out, _ = write(((own, 1), (own, 3), (other, 2)), (one, three, swap(two)), out)
    new_error, q_new, _, p_hat = write(
        ((other, 1), (other, 3)), (swap(one), swap(three)), out, p_hat
    )
    return (new_error[None], p_hat, q_new)


def solution(mesh):
    fine = Mesh(mesh.devices.reshape(SIZES), AXES)
    return jax.shard_map(
        body,
        mesh=fine,
        in_specs=(P(DP, ("y", "c"), None), P(DP, ("y", "c"), None), P()),
        out_specs=(P(DP, ("y", "c"), None), P(None, ("y", "c")), P()),
        check_vma=False,
    )
```

```python
import functools

import jax
import jax.numpy as jnp
from jax import lax
from jax.experimental import pallas as pl
from jax.experimental.pallas import tpu as pltpu
from jax.sharding import Mesh, PartitionSpec as P

DP = ("z", "x")
AXES = ("z", "x", "y", "c")
SIZES = (4, 4, 4, 2)
HIGHEST = lax.Precision.HIGHEST
F32 = jnp.float32
BF16 = jnp.bfloat16
MIB = 1 << 20
ROWS = 8
QUARTERS = 4
RIGHT = 1 << 33
SHIFTS = (1, 3, 2)
ANY = pl.BlockSpec(memory_space=pl.ANY)
WHOLE = pl.BlockSpec(memory_space=pltpu.VMEM)


def params(mib):
    return pltpu.CompilerParams(vmem_limit_bytes=mib * MIB)


def cost(flops, nbytes):
    return pl.CostEstimate(flops=flops, bytes_accessed=nbytes, transcendentals=0)


def half_of(x, y, z, c):
    return (x + y + z + c) % 2


def core_of(x, y, z, c):
    return c


def place():
    x, y, z, c = (lax.axis_index(a) for a in ("x", "y", "z", "c"))
    half = half_of(x, y, z, c)
    return half, jnp.where(half == 0, x, z), jnp.where(half == 0, z, y)


def other_place():
    x, y, z, c = (lax.axis_index(a) for a in ("x", "y", "z", "c"))
    half = 1 - half_of(x, y, z, c)
    return half, jnp.where(half == 0, x, z), jnp.where(half == 0, z, y)


def index(z, x, y, c):
    return ((z * SIZES[1] + x) * SIZES[2] + y) * SIZES[3] + c


def everyone():
    return [
        (z, x, y, c)
        for z in range(SIZES[0])
        for x in range(SIZES[1])
        for y in range(SIZES[2])
        for c in range(SIZES[3])
    ]


def ring(values, phase, shifts=SHIFTS, orders=("xzy", "zyx"), group=half_of):
    out = []
    for k, value in zip(shifts, values):
        pairs = []
        for z, x, y, c in everyone():
            to = {"z": z, "x": x, "y": y}
            axis = orders[group(x, y, z, c)][phase]
            to[axis] = (to[axis] + k) % SIZES[AXES.index(axis)]
            core = c if group is core_of else (c + k) % 2
            pairs.append((index(z, x, y, c), index(*to.values(), core)))
        out.append(lax.ppermute(value, AXES, pairs))
    return out


def swap(value):
    return lax.ppermute(value, "c", [(0, 1), (1, 0)])


def merge_kernel(cuts, g_hbm, e_hbm, q_hbm, m_ref, p_ref, g_ref, e_ref, q_ref, sems):
    rows = g_ref.shape[0]
    rank = q_ref.shape[0]

    def copies(i):
        at = pl.ds(cuts[i], cuts[i + 1] - cuts[i])
        return [
            pltpu.make_async_copy(src.at[:, at], dst.at[:, at], sems.at[n, i])
            for n, (src, dst) in enumerate(((g_hbm, g_ref), (e_hbm, e_ref), (q_hbm, q_ref)))
        ]

    for i in range(len(cuts) - 1):
        for c in copies(i):
            c.start()
    acc = jnp.zeros((rows, rank), F32)
    for i in range(len(cuts) - 1):
        for c in copies(i):
            c.wait()
        at = pl.ds(cuts[i], cuts[i + 1] - cuts[i])
        m = (g_ref[:, at].astype(F32) + e_ref[:, at].astype(F32)).astype(BF16)
        m_ref[:, at] = m
        acc = acc + lax.dot_general(
            m, q_ref[:, at], (((1,), (1,)), ((), ())), preferred_element_type=F32
        )
    p_ref[...] = pack(acc.T)


def pack(p):
    rank, rows = p.shape
    full = rows // 128
    half = rank // 2
    parts = [p[:, i * 128 : (i + 1) * 128] for i in range(full)]
    rest = p[:, full * 128 :]
    return jnp.concatenate(parts + [jnp.concatenate([rest[:half], rest[half:]], axis=1)], axis=0)


def unpack(packed, rank):
    full = packed.shape[0] // rank
    last = packed[full * rank :]
    rest = jnp.concatenate([last[:, :64], last[:, 64:]], axis=0)
    return jnp.concatenate(
        [packed[i * rank : (i + 1) * rank] for i in range(full)] + [rest], axis=1
    )


def merge(gradient, error, q_start):
    rows, columns = gradient.shape
    rank = q_start.shape[0]
    step = columns // 20
    cuts = [n * step for n in (0, 2, 4, 6, 8, 10, 12, 14, 16, 18, 19, 20)]
    gradient, error, q_start = (
        pltpu.with_memory_space_constraint(a, pltpu.HBM) for a in (gradient, error, q_start)
    )
    return pl.pallas_call(
        functools.partial(merge_kernel, cuts),
        out_shape=[pltpu.VMEM((rows, columns), BF16), pltpu.VMEM((rank * rows // 128, 128), F32)],
        in_specs=[ANY, ANY, ANY],
        out_specs=[WHOLE, WHOLE],
        scratch_shapes=[
            pltpu.VMEM((rows, columns), BF16),
            pltpu.VMEM((rows, columns), BF16),
            pltpu.VMEM((rank, columns), BF16),
            pltpu.SemaphoreType.DMA((3, len(cuts) - 1)),
        ],
        compiler_params=params(24),
        cost_estimate=cost(2 * rank * rows * columns, 4 * rows * columns),
        name="merge",
    )(gradient, error, q_start)


def right_tiles(quarters, pieces, m_ref, out_ref):
    rank = pieces.shape[0] // 3
    width = m_ref.shape[1] // 2 // QUARTERS
    to = 0
    for quarter in quarters:
        at = pl.multiple_of(quarter * width, width)
        t = jnp.dot(pieces, m_ref[:, pl.ds(at, width)], preferred_element_type=F32)
        t = t[:rank] + (t[rank : 2 * rank] + t[2 * rank :])
        for g in range(rank // ROWS):
            for n in range(width // 128):
                out_ref[to : to + ROWS, :] = t[g * ROWS : (g + 1) * ROWS, n * 128 : (n + 1) * 128]
                to += ROWS


def quarters_of(own, turns):
    half, turn, _ = place() if own else other_place()
    return [half * QUARTERS + (turn + k) % QUARTERS for k in turns]


def split(n):
    high = n.astype(BF16)
    n = n - high.astype(F32)
    middle = n.astype(BF16)
    return high, middle, (n - middle.astype(F32)).astype(BF16)


def first_right_kernel(replicas, rank, turns, a_ref, b_ref, c_ref, d_ref, m_ref, out_ref, ext_ref, p_ref, pieces_ref):
    p = (a_ref[...] + b_ref[...] + (c_ref[...] + d_ref[...])) * (1.0 / replicas)
    peak = jnp.max(jnp.abs(p), axis=(0, 1), keepdims=True)
    peak = jnp.where(peak > 0, peak, 1.0)
    p = unpack(p, rank)
    p_ref[...] = p
    pieces = jnp.concatenate(split(p / peak), axis=0)
    pieces_ref[...] = pieces
    right_tiles(quarters_of(False, turns), pieces, m_ref, out_ref)
    gram = lax.dot_general(
        p, p, (((1,), (1,)), ((), ())), precision=HIGHEST, preferred_element_type=F32
    )
    two = 2 * ROWS
    ext = jnp.concatenate(
        [
            jnp.concatenate([gram[i : i + ROWS], gram[i + ROWS : i + two]], axis=1)
            for i in range(0, rank, two)
        ]
        + [jnp.broadcast_to(peak, (ROWS, 128))],
        axis=0,
    )
    ext_ref[...] = ext
    out_ref[out_ref.shape[0] - ext.shape[0] :, :] = ext


def next_right_kernel(own, turns, pieces_ref, m_ref, after_ref, out_ref):
    del after_ref
    right_tiles(quarters_of(own, turns), pieces_ref[...], m_ref, out_ref)


def first_right(turns, parts, merged, rank, replicas):
    rows, columns = merged.shape
    size = rank * columns // 1024
    extra = rank * rank // 128 + ROWS
    return pl.pallas_call(
        functools.partial(first_right_kernel, replicas, rank, turns),
        out_shape=[
            jax.ShapeDtypeStruct((size + extra, 128), F32),
            pltpu.VMEM((extra, 128), F32),
            pltpu.VMEM((rank, rows), F32),
            pltpu.VMEM((3 * rank, rows), BF16),
        ],
        in_specs=[WHOLE] * 5,
        out_specs=[WHOLE] * 4,
        compiler_params=params(12),
        cost_estimate=cost(RIGHT, 1 << 20),
        name="first_right",
    )(*parts, merged)


def next_right(own, turns, pieces, merged, after):
    size = pieces.shape[0] // 3 * merged.shape[1] // 1024 * len(turns)
    return pl.pallas_call(
        functools.partial(next_right_kernel, own, turns),
        out_shape=jax.ShapeDtypeStruct((size, 128), F32),
        in_specs=[WHOLE, WHOLE, ANY],
        out_specs=WHOLE,
        compiler_params=params(12),
        cost_estimate=cost(RIGHT, 1 << 20),
        name="next_right",
    )(pieces, merged, after)


def first_pair_kernel(kept_ref, got_ref, ext_ref, out_ref, pair_ref, weight_ref):
    grams = ext_ref.shape[0] - ROWS
    size = kept_ref.shape[0]
    own, its = ext_ref[grams : grams + 1, :1], got_ref[size + grams : size + grams + 1, :1]
    top = jnp.maximum(own, its)
    pair_ref[:grams] = ext_ref[:grams] + got_ref[size : size + grams]
    pair_ref[grams:] = jnp.broadcast_to(top, (ROWS, 128))
    own, its = own / top, its / top
    weight_ref[:ROWS] = jnp.broadcast_to(own, (ROWS, 128))
    weight_ref[ROWS:] = jnp.broadcast_to(its, (ROWS, 128))
    out_ref[...] = kept_ref[...] * own + got_ref[:size] * its


def first_pair(kept, got, ext):
    return pl.pallas_call(
        first_pair_kernel,
        out_shape=[
            jax.ShapeDtypeStruct(kept.shape, F32),
            pltpu.VMEM(ext.shape, F32),
            pltpu.VMEM((2 * ROWS, 128), F32),
        ],
        in_specs=[WHOLE] * 3,
        out_specs=[WHOLE] * 3,
        compiler_params=params(8),
        name="first_pair",
    )(kept, got, ext)


def next_pair_kernel(kept_ref, got_ref, weight_ref, *out):
    own, its = weight_ref[:1, :1], weight_ref[ROWS : ROWS + 1, :1]
    size = out[0].shape[0]
    for n, ref in enumerate(out):
        at = slice(n * size, (n + 1) * size)
        ref[...] = kept_ref[at] * own + got_ref[at] * its


def next_pair(kept, got, weight):
    size = kept.shape[0] // 3
    return pl.pallas_call(
        next_pair_kernel,
        out_shape=[jax.ShapeDtypeStruct((size, 128), F32)] * 3,
        in_specs=[WHOLE] * 3,
        out_specs=[WHOLE] * 3,
        compiler_params=params(8),
        name="next_pair",
    )(kept, got, weight)


def add_quarters_kernel(a_ref, b_ref, c_ref, d_ref, ext_ref, *out):
    size = a_ref.shape[0] // QUARTERS
    for k, ref in zip((0,) + SHIFTS, out):
        at = pl.ds(pl.multiple_of((place()[2] + k) % QUARTERS * size, size), size)
        ref[:size] = (a_ref[at] + b_ref[at]) + (c_ref[at] + d_ref[at])
        ref[size:] = ext_ref[...]


def add_quarters(parts, ext):
    size = parts[0].shape[0] // QUARTERS
    return pl.pallas_call(
        add_quarters_kernel,
        out_shape=[jax.ShapeDtypeStruct((size + ext.shape[0], 128), F32)] * QUARTERS,
        in_specs=[WHOLE] * (QUARTERS + 1),
        out_specs=[WHOLE] * QUARTERS,
        compiler_params=params(8),
        name="add_quarters",
    )(*parts, ext)


def across_kernel(half_along_y, extra, a_ref, b_ref, c_ref, d_ref, out_ref, *ext_ref):
    grams = extra - ROWS
    size = a_ref.shape[0] - extra
    refs = (a_ref, b_ref, c_ref, d_ref)
    peaks = [r[size + grams : size + grams + 1, :1] for r in refs]
    top = jnp.maximum(jnp.maximum(peaks[0], peaks[1]), jnp.maximum(peaks[2], peaks[3]))
    a, b, c, d = (r[:size] * (k / top) for r, k in zip(refs, peaks))
    out_ref[:size] = (a + b) + (c + d)
    a, b, c, d = (r[size : size + grams] for r in refs)
    gram = jnp.where(place()[0] == half_along_y, (a + b) + (c + d), a)
    ext = out_ref.at[size:] if not ext_ref else ext_ref[0]
    ext[:grams] = gram
    ext[grams:] = jnp.broadcast_to(top, (ROWS, 128))


def across(half_along_y, parts, extra, keep):
    rows = parts[0].shape[0]
    out = [jax.ShapeDtypeStruct((rows, 128), F32)]
    if not keep:
        out = [jax.ShapeDtypeStruct((rows - extra, 128), F32), pltpu.VMEM((extra, 128), F32)]
    return pl.pallas_call(
        functools.partial(across_kernel, half_along_y, extra),
        out_shape=out,
        in_specs=[WHOLE] * 4,
        out_specs=[WHOLE] * len(out),
        compiler_params=params(8),
        name="across",
    )(*parts)


def assemble_kernel(a_ref, b_ref, c_ref, d_ref, after_ref, out_ref):
    del after_ref
    size = a_ref.shape[0]
    for k, ref in zip((0,) + SHIFTS, (a_ref, b_ref, c_ref, d_ref)):
        at = pl.multiple_of((place()[2] + QUARTERS - k) % QUARTERS * size, size)
        out_ref[pl.ds(at, size)] = ref[...]


def assemble(parts, after):
    return pl.pallas_call(
        assemble_kernel,
        out_shape=jax.ShapeDtypeStruct((parts[0].shape[0] * QUARTERS, 128), F32),
        in_specs=[WHOLE] * 4 + [ANY],
        out_specs=WHOLE,
        compiler_params=params(8),
        name="assemble",
    )(*parts, after)


def factor_kernel(replicas, ext_ref, p_ref, solve_ref, left_ref, hat_ref):
    rank = p_ref.shape[0]
    groups = rank // ROWS
    sub = lax.broadcasted_iota(jnp.int32, (ROWS, 2 * rank), 0)
    lane = lax.broadcasted_iota(jnp.int32, (ROWS, 2 * rank), 1)
    blocks = []
    for g in range(groups):
        tile = ext_ref[g // 2 * ROWS : (g // 2 + 1) * ROWS, (g % 2) * rank : (g % 2 + 1) * rank]
        unit = jnp.where(lane[:, :rank] == sub[:, :rank] + g * ROWS, 1.0, 0.0)
        blocks.append(jnp.concatenate([tile, unit], axis=1))
    for own in range(groups):
        spread = lambda g: [
            jnp.broadcast_to(blocks[g][:, own * ROWS + k : own * ROWS + k + 1], (ROWS, 2 * rank))
            for k in range(ROWS)
        ]
        columns = spread(own)
        rows, heads = [], []
        for k in range(ROWS):
            scale = 1.0 / columns[k][k : k + 1]
            row = blocks[own][k : k + 1] * scale
            head = {m: columns[m][k : k + 1] * scale for m in range(k + 1, ROWS)}
            factors = jnp.where(sub > k, columns[k], 0.0)
            blocks[own] = blocks[own] - factors * row
            for m, h in head.items():
                columns[m] = columns[m] - factors * h
            rows.append(row)
            heads.append(head)
        for g in range(own + 1, groups):
            columns = spread(g)
            for k in range(ROWS):
                blocks[g] = blocks[g] - columns[k] * rows[k]
                for m, h in heads[k].items():
                    columns[m] = columns[m] - columns[k] * h
    inverse = []
    for g in range(groups):
        diagonal = jnp.sum(
            jnp.where(lane == sub + g * ROWS, blocks[g], 0.0), axis=1, keepdims=True
        )
        inverse.append(blocks[g][:, rank:] / jnp.sqrt(diagonal))
    inverse = jnp.concatenate(inverse, axis=0)
    grams = ext_ref.shape[0] - ROWS
    s1, s2, s3 = split(inverse * (ext_ref[grams : grams + 1, :1] * (1.0 / replicas)))
    solve_ref[...] = jnp.concatenate([s1, s1, s2, s2, s1, s3], axis=1)
    hat = jnp.dot(inverse, p_ref[...], precision=HIGHEST, preferred_element_type=F32)
    hat_ref[...] = hat
    left_ref[...] = hat.T.astype(BF16)


def factor(ext, p_mean, replicas):
    rank, rows = p_mean.shape
    return pl.pallas_call(
        functools.partial(factor_kernel, replicas),
        out_shape=[
            jax.ShapeDtypeStruct((rank, 6 * rank), BF16),
            jax.ShapeDtypeStruct((rows, rank), BF16),
            jax.ShapeDtypeStruct((rank, rows), F32),
        ],
        in_specs=[WHOLE] * 2,
        out_specs=[WHOLE] * 3,
        compiler_params=params(8),
        cost_estimate=cost(1 << 32, 1 << 20),
        name="factor",
    )(ext, p_mean)


def result_kernel(sources, more, width, solve_ref, left_ref, m_ref, *refs):
    refs, (error_ref, q_ref, sems) = refs[:-3], refs[-3:]
    if more == "hat":
        hat = pltpu.make_async_copy(refs[len(sources)], refs[-1], sems.at[0, len(sources)])
        hat.start()
    if more == "token":
        refs[-1][...] = jnp.zeros_like(refs[-1])
    error_hbm, q_hbm = refs[-3:-1] if more else refs[-2:]
    rank = solve_ref.shape[0]
    columns = q_ref.shape[2]
    left = left_ref[...]
    solve = solve_ref[...]

    def copies(n, base, at, size):
        to, here = pl.ds(pl.multiple_of(base + at, 128), size), pl.ds(at, size)
        return (
            pltpu.make_async_copy(error_ref.at[n, :, here], error_hbm.at[:, to], sems.at[0, n]),
            pltpu.make_async_copy(q_ref.at[n, :, here], q_hbm.at[:, to], sems.at[1, n]),
        )

    bases = []
    for n, (own, k) in enumerate(sources):
        t_ref = refs[n]
        half, turn, _ = place() if own else other_place()
        quarter = (turn + QUARTERS - k) % QUARTERS
        base = (half * QUARTERS + quarter) * columns
        bases.append(base)
        for at in range(0, columns, width):
            t = jnp.concatenate(
                [
                    jnp.concatenate(
                        [
                            t_ref[(g * columns + i) // 128 * ROWS : (g * columns + i) // 128 * ROWS + ROWS, :]
                            for i in range(at, at + width, 128)
                        ],
                        axis=1,
                    )
                    for g in range(rank // ROWS)
                ],
                axis=0,
            )
            t1, t2, t3 = split(t)
            t = jnp.concatenate([t1, t2, t1, t2, t3, t1], axis=0)
            new = jnp.dot(solve, t, preferred_element_type=F32)
            q_ref[n, :, at : at + width] = new
            decoded = jnp.dot(left, new.astype(BF16), preferred_element_type=F32)
            m = m_ref[:, pl.ds(pl.multiple_of(base + at, 128), width)]
            error_ref[n, :, at : at + width] = (m.astype(F32) - decoded).astype(BF16)
            for c in copies(n, base, at, width):
                c.start()
    for n, base in enumerate(bases):
        for c in copies(n, base, 0, columns):
            c.wait()
    if more == "hat":
        hat.wait()


def result(sources, totals, merged, solve, left, before, p_hat=None, token=False):
    rank = solve.shape[0]
    rows, columns = merged.shape
    quarter = columns // 2 // QUARTERS
    n = len(sources)
    held = [] if before is None else list(before)
    last = [] if p_hat is None else [p_hat]
    more = "hat" if last else "token" if token else ""
    return pl.pallas_call(
        functools.partial(result_kernel, sources, more, quarter // 2),
        out_shape=[pltpu.HBM((rows, columns), BF16), pltpu.HBM((rank, columns), F32)]
        + [pltpu.HBM(a.shape, F32) for a in last]
        + [pltpu.VMEM((ROWS, 128), F32)] * token,
        in_specs=[WHOLE] * (3 + n + len(last)) + [ANY] * len(held),
        out_specs=[ANY, ANY] + [ANY] * len(last) + [WHOLE] * token,
        scratch_shapes=[
            pltpu.VMEM((n, rows, quarter), BF16),
            pltpu.VMEM((n, rank, quarter), F32),
            pltpu.SemaphoreType.DMA((2, n + 1)),
        ],
        input_output_aliases={3 + n + len(last) + i: i for i in range(len(held))},
        compiler_params=params(12),
        cost_estimate=cost(1 << 33, 1 << 20),
        name="result",
    )(solve, left, merged, *totals, *last, *held)


def tie_kernel(value_ref, after_ref, out_ref):
    del value_ref, after_ref, out_ref


def tie(value, after):
    return pl.pallas_call(
        tie_kernel,
        out_shape=jax.ShapeDtypeStruct(value.shape, value.dtype),
        in_specs=[ANY] * 2,
        out_specs=ANY,
        input_output_aliases={0: 0},
        compiler_params=params(4),
        name="tie",
    )(value, after)


def body(gradient, error, q_start):
    rank = q_start.shape[0]
    replicas = SIZES[0] * SIZES[1]
    merged, p = merge(gradient[0], error[0], q_start)
    a, b, c = ring([p] * 3, 0, orders=("xz", "zx"), group=core_of)
    p = (p + a) + (b + c)
    sent, ext, p_mean, pieces = first_right(
        (2,), (p, *ring([p] * 3, 1, orders=("xz", "zx"), group=core_of)), merged, rank, replicas
    )
    got = swap(sent)
    sent = next_right(False, (1, 3, 0), pieces, merged, ext)
    got_next = swap(sent)
    kept = next_right(True, (2,), pieces, merged, sent)
    two, ext, weight = first_pair(kept, got, ext)
    (two,) = ring((two,), 0, (2,))
    kept = next_right(True, (1, 3, 0), pieces, merged, weight)
    *near, own = next_pair(kept, got_next, weight)
    own, *sent = add_quarters((own, *ring(near, 0, (1, 3)), two), ext)
    extra = ext.shape[0]
    (part,) = across(1, (own, *ring(sent, 1)), extra, True)
    total, ext = across(0, (part, *ring([part] * 3, 2)), extra, False)
    solve, left, p_hat = factor(ext, p_mean, replicas)
    total = assemble((total, *ring([total] * 3, 1)), solve)
    two, one, three = ring([total] * 3, 0, (2, 1, 3))

    def write(sources, totals, *after, **more):
        return result(sources, totals, merged, solve, left, *after, **more)

    own, other = True, False
    out = write(((own, 0),), (total,), None)
    *out, token = write(((other, 0),), (swap(total),), out, token=True)
    two = tie(two, token)
    *out, token = write(((own, 2),), (two,), out, token=True)
    one, three = tie(one, token), tie(three, token)
    out = write(((own, 1), (own, 3), (other, 2)), (one, three, swap(two)), out)
    new_error, q_new, p_hat = write(
        ((other, 1), (other, 3)), (swap(one), swap(three)), out, p_hat
    )
    return (new_error[None], p_hat, q_new)


def solution(mesh):
    fine = Mesh(mesh.devices.reshape(SIZES), AXES)
    return jax.shard_map(
        body,
        mesh=fine,
        in_specs=(P(DP, ("y", "c"), None), P(DP, ("y", "c"), None), P()),
        out_specs=(P(DP, ("y", "c"), None), P(None, ("y", "c")), P()),
        check_vma=False,
    )
```

```python
import functools

import jax
import jax.numpy as jnp
from jax import lax
from jax.experimental import pallas as pl
from jax.experimental.pallas import tpu as pltpu
from jax.sharding import Mesh, PartitionSpec as P

DP = ("z", "x")
AXES = ("z", "x", "y", "c")
SIZES = (4, 4, 4, 2)
HIGHEST = lax.Precision.HIGHEST
F32 = jnp.float32
BF16 = jnp.bfloat16
MIB = 1 << 20
ROWS = 8
QUARTERS = 4
SHRINK = 2.0**-16
RIGHT = 1 << 33
SHIFTS = (1, 3, 2)
ANY = pl.BlockSpec(memory_space=pl.ANY)
WHOLE = pl.BlockSpec(memory_space=pltpu.VMEM)


def params(mib):
    return pltpu.CompilerParams(vmem_limit_bytes=mib * MIB)


def cost(flops, nbytes):
    return pl.CostEstimate(flops=flops, bytes_accessed=nbytes, transcendentals=0)


def half_of(x, y, z, c):
    return (x + y + z + c) % 2


def core_of(x, y, z, c):
    return c


def place():
    x, y, z, c = (lax.axis_index(a) for a in ("x", "y", "z", "c"))
    half = half_of(x, y, z, c)
    return half, jnp.where(half == 0, x, z), jnp.where(half == 0, z, y)


def other_place():
    x, y, z, c = (lax.axis_index(a) for a in ("x", "y", "z", "c"))
    half = 1 - half_of(x, y, z, c)
    return half, jnp.where(half == 0, x, z), jnp.where(half == 0, z, y)


def index(z, x, y, c):
    return ((z * SIZES[1] + x) * SIZES[2] + y) * SIZES[3] + c


def everyone():
    return [
        (z, x, y, c)
        for z in range(SIZES[0])
        for x in range(SIZES[1])
        for y in range(SIZES[2])
        for c in range(SIZES[3])
    ]


def ring(values, phase, shifts=SHIFTS, orders=("xzy", "zyx"), group=half_of):
    out = []
    for k, value in zip(shifts, values):
        pairs = []
        for z, x, y, c in everyone():
            to = {"z": z, "x": x, "y": y}
            axis = orders[group(x, y, z, c)][phase]
            to[axis] = (to[axis] + k) % SIZES[AXES.index(axis)]
            core = c if group is core_of else (c + k) % 2
            pairs.append((index(z, x, y, c), index(*to.values(), core)))
        out.append(lax.ppermute(value, AXES, pairs))
    return out


def swap(value):
    return lax.ppermute(value, "c", [(0, 1), (1, 0)])


def merge_kernel(cuts, g_hbm, e_hbm, q_hbm, m_ref, p_ref, g_ref, e_ref, q_ref, sems):
    rows = g_ref.shape[0]
    rank = q_ref.shape[0]

    def copies(i):
        at = pl.ds(cuts[i], cuts[i + 1] - cuts[i])
        return [
            pltpu.make_async_copy(src.at[:, at], dst.at[:, at], sems.at[n, i])
            for n, (src, dst) in enumerate(((g_hbm, g_ref), (e_hbm, e_ref), (q_hbm, q_ref)))
        ]

    for i in range(len(cuts) - 1):
        for c in copies(i):
            c.start()
    acc = jnp.zeros((rows, rank), F32)
    for i in range(len(cuts) - 1):
        for c in copies(i):
            c.wait()
        at = pl.ds(cuts[i], cuts[i + 1] - cuts[i])
        m = (g_ref[:, at].astype(F32) + e_ref[:, at].astype(F32)).astype(BF16)
        m_ref[:, at] = m
        acc = acc + lax.dot_general(
            m, q_ref[:, at], (((1,), (1,)), ((), ())), preferred_element_type=F32
        )
    p_ref[...] = pack(acc.T)


def pack(p):
    rank, rows = p.shape
    full = rows // 128
    half = rank // 2
    parts = [p[:, i * 128 : (i + 1) * 128] for i in range(full)]
    rest = p[:, full * 128 :]
    return jnp.concatenate(parts + [jnp.concatenate([rest[:half], rest[half:]], axis=1)], axis=0)


def unpack(packed, rank):
    full = packed.shape[0] // rank
    last = packed[full * rank :]
    rest = jnp.concatenate([last[:, :64], last[:, 64:]], axis=0)
    return jnp.concatenate(
        [packed[i * rank : (i + 1) * rank] for i in range(full)] + [rest], axis=1
    )


def merge(gradient, error, q_start):
    rows, columns = gradient.shape
    rank = q_start.shape[0]
    step = columns // 20
    cuts = [n * step for n in (0, 2, 4, 6, 8, 10, 12, 14, 16, 18, 19, 20)]
    gradient, error, q_start = (
        pltpu.with_memory_space_constraint(a, pltpu.HBM) for a in (gradient, error, q_start)
    )
    return pl.pallas_call(
        functools.partial(merge_kernel, cuts),
        out_shape=[pltpu.VMEM((rows, columns), BF16), pltpu.VMEM((rank * rows // 128, 128), F32)],
        in_specs=[ANY, ANY, ANY],
        out_specs=[WHOLE, WHOLE],
        scratch_shapes=[
            pltpu.VMEM((rows, columns), BF16),
            pltpu.VMEM((rows, columns), BF16),
            pltpu.VMEM((rank, columns), BF16),
            pltpu.SemaphoreType.DMA((3, len(cuts) - 1)),
        ],
        compiler_params=params(24),
        cost_estimate=cost(2 * rank * rows * columns, 4 * rows * columns),
        name="merge",
    )(gradient, error, q_start)


def right_tiles(quarters, pieces, m_ref, out_ref):
    rank = pieces.shape[0] // 3
    width = m_ref.shape[1] // 2 // QUARTERS
    to = 0
    for quarter in quarters:
        at = pl.multiple_of(quarter * width, width)
        t = jnp.dot(pieces, m_ref[:, pl.ds(at, width)], preferred_element_type=F32)
        t = t[:rank] + (t[rank : 2 * rank] + t[2 * rank :])
        for g in range(rank // ROWS):
            for n in range(width // 128):
                out_ref[to : to + ROWS, :] = t[g * ROWS : (g + 1) * ROWS, n * 128 : (n + 1) * 128]
                to += ROWS


def quarters_of(own, turns):
    half, turn, _ = place() if own else other_place()
    return [half * QUARTERS + (turn + k) % QUARTERS for k in turns]


def split(n):
    high = n.astype(BF16)
    n = n - high.astype(F32)
    middle = n.astype(BF16)
    return high, middle, (n - middle.astype(F32)).astype(BF16)


def first_right_kernel(replicas, rank, turns, a_ref, b_ref, c_ref, d_ref, m_ref, out_ref, ext_ref, p_ref, pieces_ref):
    p = (a_ref[...] + b_ref[...] + (c_ref[...] + d_ref[...])) * (1.0 / replicas)
    peak = jnp.max(jnp.abs(p), axis=(0, 1), keepdims=True)
    peak = jnp.where(peak > 0, peak, 1.0)
    p = unpack(p, rank)
    p_ref[...] = p
    pieces = jnp.concatenate(split(p / peak * SHRINK), axis=0)
    pieces_ref[...] = pieces
    right_tiles(quarters_of(False, turns), pieces, m_ref, out_ref)
    gram = lax.dot_general(
        p, p, (((1,), (1,)), ((), ())), precision=HIGHEST, preferred_element_type=F32
    )
    two = 2 * ROWS
    ext = jnp.concatenate(
        [
            jnp.concatenate([gram[i : i + ROWS], gram[i + ROWS : i + two]], axis=1)
            for i in range(0, rank, two)
        ]
        + [jnp.broadcast_to(peak, (ROWS, 128))],
        axis=0,
    )
    ext_ref[...] = ext
    out_ref[out_ref.shape[0] - ext.shape[0] :, :] = ext


def next_right_kernel(own, turns, pieces_ref, m_ref, after_ref, out_ref):
    del after_ref
    right_tiles(quarters_of(own, turns), pieces_ref[...], m_ref, out_ref)


def first_right(turns, parts, merged, rank, replicas):
    rows, columns = merged.shape
    size = rank * columns // 1024
    extra = rank * rank // 128 + ROWS
    return pl.pallas_call(
        functools.partial(first_right_kernel, replicas, rank, turns),
        out_shape=[
            jax.ShapeDtypeStruct((size + extra, 128), F32),
            pltpu.VMEM((extra, 128), F32),
            pltpu.VMEM((rank, rows), F32),
            pltpu.VMEM((3 * rank, rows), BF16),
        ],
        in_specs=[WHOLE] * 5,
        out_specs=[WHOLE] * 4,
        compiler_params=params(12),
        cost_estimate=cost(RIGHT, 1 << 20),
        name="first_right",
    )(*parts, merged)


def next_right(own, turns, pieces, merged, after):
    size = pieces.shape[0] // 3 * merged.shape[1] // 1024 * len(turns)
    return pl.pallas_call(
        functools.partial(next_right_kernel, own, turns),
        out_shape=jax.ShapeDtypeStruct((size, 128), F32),
        in_specs=[WHOLE, WHOLE, ANY],
        out_specs=WHOLE,
        compiler_params=params(12),
        cost_estimate=cost(RIGHT, 1 << 20),
        name="next_right",
    )(pieces, merged, after)


def first_pair_kernel(kept_ref, got_ref, ext_ref, out_ref, pair_ref, weight_ref):
    grams = ext_ref.shape[0] - ROWS
    size = kept_ref.shape[0]
    own, its = ext_ref[grams : grams + 1, :1], got_ref[size + grams : size + grams + 1, :1]
    top = jnp.maximum(own, its)
    pair_ref[:grams] = ext_ref[:grams] + got_ref[size : size + grams]
    pair_ref[grams:] = jnp.broadcast_to(top, (ROWS, 128))
    own, its = own / top, its / top
    weight_ref[:ROWS] = jnp.broadcast_to(own, (ROWS, 128))
    weight_ref[ROWS:] = jnp.broadcast_to(its, (ROWS, 128))
    out_ref[...] = kept_ref[...] * own + got_ref[:size] * its


def first_pair(kept, got, ext):
    return pl.pallas_call(
        first_pair_kernel,
        out_shape=[
            jax.ShapeDtypeStruct(kept.shape, F32),
            pltpu.VMEM(ext.shape, F32),
            pltpu.VMEM((2 * ROWS, 128), F32),
        ],
        in_specs=[WHOLE] * 3,
        out_specs=[WHOLE] * 3,
        compiler_params=params(8),
        name="first_pair",
    )(kept, got, ext)


def next_pair_kernel(kept_ref, got_ref, weight_ref, *out):
    own, its = weight_ref[:1, :1], weight_ref[ROWS : ROWS + 1, :1]
    size = out[0].shape[0]
    for n, ref in enumerate(out):
        at = slice(n * size, (n + 1) * size)
        ref[...] = kept_ref[at] * own + got_ref[at] * its


def next_pair(kept, got, weight):
    size = kept.shape[0] // 3
    return pl.pallas_call(
        next_pair_kernel,
        out_shape=[jax.ShapeDtypeStruct((size, 128), F32)] * 3,
        in_specs=[WHOLE] * 3,
        out_specs=[WHOLE] * 3,
        compiler_params=params(8),
        name="next_pair",
    )(kept, got, weight)


def add_quarters_kernel(a_ref, b_ref, c_ref, d_ref, ext_ref, *out):
    size = a_ref.shape[0] // QUARTERS
    for k, ref in zip((0,) + SHIFTS, out):
        at = pl.ds(pl.multiple_of((place()[2] + k) % QUARTERS * size, size), size)
        ref[:size] = (a_ref[at] + b_ref[at]) + (c_ref[at] + d_ref[at])
        ref[size:] = ext_ref[...]


def add_quarters(parts, ext):
    size = parts[0].shape[0] // QUARTERS
    return pl.pallas_call(
        add_quarters_kernel,
        out_shape=[jax.ShapeDtypeStruct((size + ext.shape[0], 128), F32)] * QUARTERS,
        in_specs=[WHOLE] * (QUARTERS + 1),
        out_specs=[WHOLE] * QUARTERS,
        compiler_params=params(8),
        name="add_quarters",
    )(*parts, ext)


def across_kernel(half_along_y, extra, a_ref, b_ref, c_ref, d_ref, out_ref, *ext_ref):
    grams = extra - ROWS
    size = a_ref.shape[0] - extra
    refs = (a_ref, b_ref, c_ref, d_ref)
    peaks = [r[size + grams : size + grams + 1, :1] for r in refs]
    top = jnp.maximum(jnp.maximum(peaks[0], peaks[1]), jnp.maximum(peaks[2], peaks[3]))
    a, b, c, d = (r[:size] * (k / top) for r, k in zip(refs, peaks))
    out_ref[:size] = (a + b) + (c + d)
    a, b, c, d = (r[size : size + grams] for r in refs)
    gram = jnp.where(place()[0] == half_along_y, (a + b) + (c + d), a)
    ext = out_ref.at[size:] if not ext_ref else ext_ref[0]
    ext[:grams] = gram
    ext[grams:] = jnp.broadcast_to(top, (ROWS, 128))


def across(half_along_y, parts, extra, keep):
    rows = parts[0].shape[0]
    out = [jax.ShapeDtypeStruct((rows, 128), F32)]
    if not keep:
        out = [jax.ShapeDtypeStruct((rows - extra, 128), F32), pltpu.VMEM((extra, 128), F32)]
    return pl.pallas_call(
        functools.partial(across_kernel, half_along_y, extra),
        out_shape=out,
        in_specs=[WHOLE] * 4,
        out_specs=[WHOLE] * len(out),
        compiler_params=params(8),
        name="across",
    )(*parts)


def assemble_kernel(a_ref, b_ref, c_ref, d_ref, after_ref, out_ref):
    del after_ref
    size = a_ref.shape[0]
    for k, ref in zip((0,) + SHIFTS, (a_ref, b_ref, c_ref, d_ref)):
        at = pl.multiple_of((place()[2] + QUARTERS - k) % QUARTERS * size, size)
        out_ref[pl.ds(at, size)] = ref[...]


def assemble(parts, after):
    return pl.pallas_call(
        assemble_kernel,
        out_shape=jax.ShapeDtypeStruct((parts[0].shape[0] * QUARTERS, 128), F32),
        in_specs=[WHOLE] * 4 + [ANY],
        out_specs=WHOLE,
        compiler_params=params(8),
        name="assemble",
    )(*parts, after)


def factor_kernel(replicas, ext_ref, p_ref, solve_ref, left_ref, hat_ref):
    rank = p_ref.shape[0]
    groups = rank // ROWS
    sub = lax.broadcasted_iota(jnp.int32, (ROWS, 2 * rank), 0)
    lane = lax.broadcasted_iota(jnp.int32, (ROWS, 2 * rank), 1)
    blocks = []
    for g in range(groups):
        tile = ext_ref[g // 2 * ROWS : (g // 2 + 1) * ROWS, (g % 2) * rank : (g % 2 + 1) * rank]
        unit = jnp.where(lane[:, :rank] == sub[:, :rank] + g * ROWS, 1.0, 0.0)
        blocks.append(jnp.concatenate([tile, unit], axis=1))
    for own in range(groups):
        spread = lambda g: [
            jnp.broadcast_to(blocks[g][:, own * ROWS + k : own * ROWS + k + 1], (ROWS, 2 * rank))
            for k in range(ROWS)
        ]
        columns = spread(own)
        rows, heads = [], []
        for k in range(ROWS):
            scale = 1.0 / columns[k][k : k + 1]
            row = blocks[own][k : k + 1] * scale
            head = {m: columns[m][k : k + 1] * scale for m in range(k + 1, ROWS)}
            factors = jnp.where(sub > k, columns[k], 0.0)
            blocks[own] = blocks[own] - factors * row
            for m, h in head.items():
                columns[m] = columns[m] - factors * h
            rows.append(row)
            heads.append(head)
        for g in range(own + 1, groups):
            columns = spread(g)
            for k in range(ROWS):
                blocks[g] = blocks[g] - columns[k] * rows[k]
                for m, h in heads[k].items():
                    columns[m] = columns[m] - columns[k] * h
    inverse = []
    for g in range(groups):
        diagonal = jnp.sum(
            jnp.where(lane == sub + g * ROWS, blocks[g], 0.0), axis=1, keepdims=True
        )
        inverse.append(blocks[g][:, rank:] / jnp.sqrt(diagonal))
    inverse = jnp.concatenate(inverse, axis=0)
    grams = ext_ref.shape[0] - ROWS
    solve = inverse * ext_ref[grams : grams + 1, :1] * (1.0 / (replicas * SHRINK))
    s1, s2, s3 = split(solve)
    solve_ref[...] = jnp.concatenate([s1, s1, s2, s2, s1, s3], axis=1)
    hat = jnp.dot(inverse, p_ref[...], precision=HIGHEST, preferred_element_type=F32)
    hat_ref[...] = hat
    left_ref[...] = hat.T.astype(BF16)


def factor(ext, p_mean, replicas):
    rank, rows = p_mean.shape
    return pl.pallas_call(
        functools.partial(factor_kernel, replicas),
        out_shape=[
            jax.ShapeDtypeStruct((rank, 6 * rank), BF16),
            jax.ShapeDtypeStruct((rows, rank), BF16),
            jax.ShapeDtypeStruct((rank, rows), F32),
        ],
        in_specs=[WHOLE] * 2,
        out_specs=[WHOLE] * 3,
        compiler_params=params(8),
        cost_estimate=cost(1 << 32, 1 << 20),
        name="factor",
    )(ext, p_mean)


def result_kernel(sources, more, width, solve_ref, left_ref, m_ref, *refs):
    refs, (error_ref, q_ref, sems) = refs[:-3], refs[-3:]
    if more == "hat":
        hat = pltpu.make_async_copy(refs[len(sources)], refs[-1], sems.at[0, len(sources)])
        hat.start()
    if more == "token":
        refs[-1][...] = jnp.zeros_like(refs[-1])
    error_hbm, q_hbm = refs[-3:-1] if more else refs[-2:]
    rank = solve_ref.shape[0]
    columns = q_ref.shape[2]
    left = left_ref[...]
    solve = solve_ref[...]

    def copies(n, base, at, size):
        to, here = pl.ds(pl.multiple_of(base + at, 128), size), pl.ds(at, size)
        return (
            pltpu.make_async_copy(error_ref.at[n, :, here], error_hbm.at[:, to], sems.at[0, n]),
            pltpu.make_async_copy(q_ref.at[n, :, here], q_hbm.at[:, to], sems.at[1, n]),
        )

    bases = []
    for n, (own, k) in enumerate(sources):
        t_ref = refs[n]
        half, turn, _ = place() if own else other_place()
        quarter = (turn + QUARTERS - k) % QUARTERS
        base = (half * QUARTERS + quarter) * columns
        bases.append(base)
        for at in range(0, columns, width):
            t = jnp.concatenate(
                [
                    jnp.concatenate(
                        [
                            t_ref[(g * columns + i) // 128 * ROWS : (g * columns + i) // 128 * ROWS + ROWS, :]
                            for i in range(at, at + width, 128)
                        ],
                        axis=1,
                    )
                    for g in range(rank // ROWS)
                ],
                axis=0,
            )
            t1, t2, t3 = split(t)
            t = jnp.concatenate([t1, t2, t1, t2, t3, t1], axis=0)
            new = jnp.dot(solve, t, preferred_element_type=F32)
            q_ref[n, :, at : at + width] = new
            decoded = jnp.dot(left, new.astype(BF16), preferred_element_type=F32)
            m = m_ref[:, pl.ds(pl.multiple_of(base + at, 128), width)]
            error_ref[n, :, at : at + width] = (m.astype(F32) - decoded).astype(BF16)
            for c in copies(n, base, at, width):
                c.start()
    for n, base in enumerate(bases):
        for c in copies(n, base, 0, columns):
            c.wait()
    if more == "hat":
        hat.wait()


def result(sources, totals, merged, solve, left, before, p_hat=None, token=False):
    rank = solve.shape[0]
    rows, columns = merged.shape
    quarter = columns // 2 // QUARTERS
    n = len(sources)
    held = [] if before is None else list(before)
    last = [] if p_hat is None else [p_hat]
    more = "hat" if last else "token" if token else ""
    return pl.pallas_call(
        functools.partial(result_kernel, sources, more, quarter // 2),
        out_shape=[pltpu.HBM((rows, columns), BF16), pltpu.HBM((rank, columns), F32)]
        + [pltpu.HBM(a.shape, F32) for a in last]
        + [pltpu.VMEM((ROWS, 128), F32)] * token,
        in_specs=[WHOLE] * (3 + n + len(last)) + [ANY] * len(held),
        out_specs=[ANY, ANY] + [ANY] * len(last) + [WHOLE] * token,
        scratch_shapes=[
            pltpu.VMEM((n, rows, quarter), BF16),
            pltpu.VMEM((n, rank, quarter), F32),
            pltpu.SemaphoreType.DMA((2, n + 1)),
        ],
        input_output_aliases={3 + n + len(last) + i: i for i in range(len(held))},
        compiler_params=params(12),
        cost_estimate=cost(1 << 33, 1 << 20),
        name="result",
    )(solve, left, merged, *totals, *last, *held)


def tie_kernel(value_ref, after_ref, out_ref):
    del value_ref, after_ref, out_ref


def tie(value, after):
    return pl.pallas_call(
        tie_kernel,
        out_shape=jax.ShapeDtypeStruct(value.shape, value.dtype),
        in_specs=[ANY] * 2,
        out_specs=ANY,
        input_output_aliases={0: 0},
        compiler_params=params(4),
        name="tie",
    )(value, after)


def body(gradient, error, q_start):
    rank = q_start.shape[0]
    replicas = SIZES[0] * SIZES[1]
    merged, p = merge(gradient[0], error[0], q_start)
    a, b, c = ring([p] * 3, 0, orders=("xz", "zx"), group=core_of)
    p = (p + a) + (b + c)
    sent, ext, p_mean, pieces = first_right(
        (2,), (p, *ring([p] * 3, 1, orders=("xz", "zx"), group=core_of)), merged, rank, replicas
    )
    got = swap(sent)
    sent = next_right(False, (1, 3, 0), pieces, merged, ext)
    got_next = swap(sent)
    kept = next_right(True, (2,), pieces, merged, sent)
    two, ext, weight = first_pair(kept, got, ext)
    (two,) = ring((two,), 0, (2,))
    kept = next_right(True, (1, 3, 0), pieces, merged, weight)
    *near, own = next_pair(kept, got_next, weight)
    own, *sent = add_quarters((own, *ring(near, 0, (1, 3)), two), ext)
    extra = ext.shape[0]
    (part,) = across(1, (own, *ring(sent, 1)), extra, True)
    total, ext = across(0, (part, *ring([part] * 3, 2)), extra, False)
    solve, left, p_hat = factor(ext, p_mean, replicas)
    total = assemble((total, *ring([total] * 3, 1)), solve)
    two, one, three = ring([total] * 3, 0, (2, 1, 3))

    def write(sources, totals, *after, **more):
        return result(sources, totals, merged, solve, left, *after, **more)

    own, other = True, False
    out = write(((own, 0),), (total,), None)
    *out, token = write(((other, 0),), (swap(total),), out, token=True)
    two = tie(two, token)
    *out, token = write(((own, 2),), (two,), out, token=True)
    one, three = tie(one, token), tie(three, token)
    out = write(((own, 1), (own, 3), (other, 2)), (one, three, swap(two)), out)
    new_error, q_new, p_hat = write(
        ((other, 1), (other, 3)), (swap(one), swap(three)), out, p_hat
    )
    return (new_error[None], p_hat, q_new)


def solution(mesh):
    fine = Mesh(mesh.devices.reshape(SIZES), AXES)
    return jax.shard_map(
        body,
        mesh=fine,
        in_specs=(P(DP, ("y", "c"), None), P(DP, ("y", "c"), None), P()),
        out_specs=(P(DP, ("y", "c"), None), P(None, ("y", "c")), P()),
        check_vma=False,
    )
```

```python
import functools

import jax
import jax.numpy as jnp
from jax import lax
from jax.experimental import pallas as pl
from jax.experimental.pallas import tpu as pltpu
from jax.sharding import Mesh, PartitionSpec as P

DP = ("z", "x")
AXES = ("z", "x", "y", "c")
SIZES = (4, 4, 4, 2)
HIGHEST = lax.Precision.HIGHEST
F32 = jnp.float32
BF16 = jnp.bfloat16
MIB = 1 << 20
ROWS = 8
QUARTERS = 4
SHRINK = 2.0**-16
RIGHT = 1 << 33
SHIFTS = (1, 3, 2)
ANY = pl.BlockSpec(memory_space=pl.ANY)
WHOLE = pl.BlockSpec(memory_space=pltpu.VMEM)


def params(mib):
    return pltpu.CompilerParams(vmem_limit_bytes=mib * MIB)


def cost(flops, nbytes):
    return pl.CostEstimate(flops=flops, bytes_accessed=nbytes, transcendentals=0)


def half_of(x, y, z, c):
    return (x + y + z + c) % 2


def core_of(x, y, z, c):
    return c


def place():
    x, y, z, c = (lax.axis_index(a) for a in ("x", "y", "z", "c"))
    half = half_of(x, y, z, c)
    return half, jnp.where(half == 0, x, z), jnp.where(half == 0, z, y)


def other_place():
    x, y, z, c = (lax.axis_index(a) for a in ("x", "y", "z", "c"))
    half = 1 - half_of(x, y, z, c)
    return half, jnp.where(half == 0, x, z), jnp.where(half == 0, z, y)


def index(z, x, y, c):
    return ((z * SIZES[1] + x) * SIZES[2] + y) * SIZES[3] + c


def everyone():
    return [
        (z, x, y, c)
        for z in range(SIZES[0])
        for x in range(SIZES[1])
        for y in range(SIZES[2])
        for c in range(SIZES[3])
    ]


def ring(values, phase, shifts=SHIFTS, orders=("xzy", "zyx"), group=half_of):
    out = []
    for k, value in zip(shifts, values):
        pairs = []
        for z, x, y, c in everyone():
            to = {"z": z, "x": x, "y": y}
            axis = orders[group(x, y, z, c)][phase]
            to[axis] = (to[axis] + k) % SIZES[AXES.index(axis)]
            core = c if group is core_of else (c + k) % 2
            pairs.append((index(z, x, y, c), index(*to.values(), core)))
        out.append(lax.ppermute(value, AXES, pairs))
    return out


def swap(value):
    return lax.ppermute(value, "c", [(0, 1), (1, 0)])


def merge_kernel(cuts, g_hbm, e_hbm, q_hbm, m_ref, p_ref, g_ref, e_ref, q_ref, sems):
    rows = g_ref.shape[0]
    rank = q_ref.shape[0]

    def copies(i):
        at = pl.ds(cuts[i], cuts[i + 1] - cuts[i])
        return [
            pltpu.make_async_copy(src.at[:, at], dst.at[:, at], sems.at[n, i])
            for n, (src, dst) in enumerate(((g_hbm, g_ref), (e_hbm, e_ref), (q_hbm, q_ref)))
        ]

    for i in range(len(cuts) - 1):
        for c in copies(i):
            c.start()
    acc = jnp.zeros((rows, rank), F32)
    for i in range(len(cuts) - 1):
        for c in copies(i):
            c.wait()
        at = pl.ds(cuts[i], cuts[i + 1] - cuts[i])
        m = (g_ref[:, at].astype(F32) + e_ref[:, at].astype(F32)).astype(BF16)
        m_ref[:, at] = m
        acc = acc + lax.dot_general(
            m, q_ref[:, at], (((1,), (1,)), ((), ())), preferred_element_type=F32
        )
    p_ref[...] = pack(acc.T)


def pack(p):
    rank, rows = p.shape
    full = rows // 128
    half = rank // 2
    parts = [p[:, i * 128 : (i + 1) * 128] for i in range(full)]
    rest = p[:, full * 128 :]
    return jnp.concatenate(parts + [jnp.concatenate([rest[:half], rest[half:]], axis=1)], axis=0)


def unpack(packed, rank):
    full = packed.shape[0] // rank
    last = packed[full * rank :]
    rest = jnp.concatenate([last[:, :64], last[:, 64:]], axis=0)
    return jnp.concatenate(
        [packed[i * rank : (i + 1) * rank] for i in range(full)] + [rest], axis=1
    )


def merge(gradient, error, q_start):
    rows, columns = gradient.shape
    rank = q_start.shape[0]
    step = columns // 20
    cuts = [n * step for n in (0, 2, 4, 6, 8, 10, 12, 14, 16, 18, 19, 20)]
    gradient, error, q_start = (
        pltpu.with_memory_space_constraint(a, pltpu.HBM) for a in (gradient, error, q_start)
    )
    return pl.pallas_call(
        functools.partial(merge_kernel, cuts),
        out_shape=[pltpu.VMEM((rows, columns), BF16), pltpu.VMEM((rank * rows // 128, 128), F32)],
        in_specs=[ANY, ANY, ANY],
        out_specs=[WHOLE, WHOLE],
        scratch_shapes=[
            pltpu.VMEM((rows, columns), BF16),
            pltpu.VMEM((rows, columns), BF16),
            pltpu.VMEM((rank, columns), BF16),
            pltpu.SemaphoreType.DMA((3, len(cuts) - 1)),
        ],
        compiler_params=params(24),
        cost_estimate=cost(2 * rank * rows * columns, 4 * rows * columns),
        name="merge",
    )(gradient, error, q_start)


def right_tiles(quarters, pieces, m_ref, out_ref):
    rank = pieces.shape[0] // 3
    width = m_ref.shape[1] // 2 // QUARTERS
    main = pieces.shape[1] // 256 * 256
    rest = jnp.concatenate(
        [pieces[i : i + rank, main:] for i in range(0, 3 * rank, rank)], axis=1
    )
    to = 0
    for quarter in quarters:
        at = pl.multiple_of(quarter * width, width)
        m = m_ref[:, pl.ds(at, width)]
        t = jnp.dot(pieces[:, :main], m[:main], preferred_element_type=F32)
        t = t[:rank] + (t[rank : 2 * rank] + t[2 * rank :])
        m = jnp.concatenate([m[main:]] * 3, axis=0)
        t = t + jnp.dot(rest, m, preferred_element_type=F32)
        for g in range(rank // ROWS):
            for n in range(width // 128):
                out_ref[to : to + ROWS, :] = t[g * ROWS : (g + 1) * ROWS, n * 128 : (n + 1) * 128]
                to += ROWS


def quarters_of(own, turns):
    half, turn, _ = place() if own else other_place()
    return [half * QUARTERS + (turn + k) % QUARTERS for k in turns]


def split(n):
    high = n.astype(BF16)
    n = n - high.astype(F32)
    middle = n.astype(BF16)
    return high, middle, (n - middle.astype(F32)).astype(BF16)


def first_right_kernel(replicas, rank, turns, a_ref, b_ref, c_ref, d_ref, m_ref, out_ref, ext_ref, p_ref, pieces_ref):
    p = (a_ref[...] + b_ref[...] + (c_ref[...] + d_ref[...])) * (1.0 / replicas)
    peak = jnp.max(jnp.abs(p), axis=(0, 1), keepdims=True)
    peak = jnp.where(peak > 0, peak, 1.0)
    p = unpack(p, rank)
    p_ref[...] = p
    pieces = jnp.concatenate(split(p / peak * SHRINK), axis=0)
    pieces_ref[...] = pieces
    right_tiles(quarters_of(False, turns), pieces, m_ref, out_ref)
    gram = lax.dot_general(
        p, p, (((1,), (1,)), ((), ())), precision=HIGHEST, preferred_element_type=F32
    )
    two = 2 * ROWS
    ext = jnp.concatenate(
        [
            jnp.concatenate([gram[i : i + ROWS], gram[i + ROWS : i + two]], axis=1)
            for i in range(0, rank, two)
        ]
        + [jnp.broadcast_to(peak, (ROWS, 128))],
        axis=0,
    )
    ext_ref[...] = ext
    out_ref[out_ref.shape[0] - ext.shape[0] :, :] = ext


def next_right_kernel(own, turns, pieces_ref, m_ref, after_ref, out_ref):
    del after_ref
    right_tiles(quarters_of(own, turns), pieces_ref[...], m_ref, out_ref)


def first_right(turns, parts, merged, rank, replicas):
    rows, columns = merged.shape
    size = rank * columns // 1024
    extra = rank * rank // 128 + ROWS
    return pl.pallas_call(
        functools.partial(first_right_kernel, replicas, rank, turns),
        out_shape=[
            jax.ShapeDtypeStruct((size + extra, 128), F32),
            pltpu.VMEM((extra, 128), F32),
            pltpu.VMEM((rank, rows), F32),
            pltpu.VMEM((3 * rank, rows), BF16),
        ],
        in_specs=[WHOLE] * 5,
        out_specs=[WHOLE] * 4,
        compiler_params=params(12),
        cost_estimate=cost(RIGHT, 1 << 20),
        name="first_right",
    )(*parts, merged)


def next_right(own, turns, pieces, merged, after):
    size = pieces.shape[0] // 3 * merged.shape[1] // 1024 * len(turns)
    return pl.pallas_call(
        functools.partial(next_right_kernel, own, turns),
        out_shape=jax.ShapeDtypeStruct((size, 128), F32),
        in_specs=[WHOLE, WHOLE, ANY],
        out_specs=WHOLE,
        compiler_params=params(12),
        cost_estimate=cost(RIGHT, 1 << 20),
        name="next_right",
    )(pieces, merged, after)


def first_pair_kernel(kept_ref, got_ref, ext_ref, out_ref, pair_ref, weight_ref):
    grams = ext_ref.shape[0] - ROWS
    size = kept_ref.shape[0]
    own, its = ext_ref[grams : grams + 1, :1], got_ref[size + grams : size + grams + 1, :1]
    top = jnp.maximum(own, its)
    pair_ref[:grams] = ext_ref[:grams] + got_ref[size : size + grams]
    pair_ref[grams:] = jnp.broadcast_to(top, (ROWS, 128))
    own, its = own / top, its / top
    weight_ref[:ROWS] = jnp.broadcast_to(own, (ROWS, 128))
    weight_ref[ROWS:] = jnp.broadcast_to(its, (ROWS, 128))
    out_ref[...] = kept_ref[...] * own + got_ref[:size] * its


def first_pair(kept, got, ext):
    return pl.pallas_call(
        first_pair_kernel,
        out_shape=[
            jax.ShapeDtypeStruct(kept.shape, F32),
            pltpu.VMEM(ext.shape, F32),
            pltpu.VMEM((2 * ROWS, 128), F32),
        ],
        in_specs=[WHOLE] * 3,
        out_specs=[WHOLE] * 3,
        compiler_params=params(8),
        name="first_pair",
    )(kept, got, ext)


def next_pair_kernel(kept_ref, got_ref, weight_ref, *out):
    own, its = weight_ref[:1, :1], weight_ref[ROWS : ROWS + 1, :1]
    size = out[0].shape[0]
    for n, ref in enumerate(out):
        at = slice(n * size, (n + 1) * size)
        ref[...] = kept_ref[at] * own + got_ref[at] * its


def next_pair(kept, got, weight):
    size = kept.shape[0] // 3
    return pl.pallas_call(
        next_pair_kernel,
        out_shape=[jax.ShapeDtypeStruct((size, 128), F32)] * 3,
        in_specs=[WHOLE] * 3,
        out_specs=[WHOLE] * 3,
        compiler_params=params(8),
        name="next_pair",
    )(kept, got, weight)


def add_quarters_kernel(a_ref, b_ref, c_ref, d_ref, ext_ref, *out):
    size = a_ref.shape[0] // QUARTERS
    for k, ref in zip((0,) + SHIFTS, out):
        at = pl.ds(pl.multiple_of((place()[2] + k) % QUARTERS * size, size), size)
        ref[:size] = (a_ref[at] + b_ref[at]) + (c_ref[at] + d_ref[at])
        ref[size:] = ext_ref[...]


def add_quarters(parts, ext):
    size = parts[0].shape[0] // QUARTERS
    return pl.pallas_call(
        add_quarters_kernel,
        out_shape=[jax.ShapeDtypeStruct((size + ext.shape[0], 128), F32)] * QUARTERS,
        in_specs=[WHOLE] * (QUARTERS + 1),
        out_specs=[WHOLE] * QUARTERS,
        compiler_params=params(8),
        name="add_quarters",
    )(*parts, ext)


def across_kernel(half_along_y, extra, a_ref, b_ref, c_ref, d_ref, out_ref, *ext_ref):
    grams = extra - ROWS
    size = a_ref.shape[0] - extra
    refs = (a_ref, b_ref, c_ref, d_ref)
    peaks = [r[size + grams : size + grams + 1, :1] for r in refs]
    top = jnp.maximum(jnp.maximum(peaks[0], peaks[1]), jnp.maximum(peaks[2], peaks[3]))
    a, b, c, d = (r[:size] * (k / top) for r, k in zip(refs, peaks))
    out_ref[:size] = (a + b) + (c + d)
    a, b, c, d = (r[size : size + grams] for r in refs)
    gram = jnp.where(place()[0] == half_along_y, (a + b) + (c + d), a)
    ext = out_ref.at[size:] if not ext_ref else ext_ref[0]
    ext[:grams] = gram
    ext[grams:] = jnp.broadcast_to(top, (ROWS, 128))


def across(half_along_y, parts, extra, keep):
    rows = parts[0].shape[0]
    out = [jax.ShapeDtypeStruct((rows, 128), F32)]
    if not keep:
        out = [jax.ShapeDtypeStruct((rows - extra, 128), F32), pltpu.VMEM((extra, 128), F32)]
    return pl.pallas_call(
        functools.partial(across_kernel, half_along_y, extra),
        out_shape=out,
        in_specs=[WHOLE] * 4,
        out_specs=[WHOLE] * len(out),
        compiler_params=params(8),
        name="across",
    )(*parts)


def assemble_kernel(a_ref, b_ref, c_ref, d_ref, after_ref, out_ref):
    del after_ref
    size = a_ref.shape[0]
    for k, ref in zip((0,) + SHIFTS, (a_ref, b_ref, c_ref, d_ref)):
        at = pl.multiple_of((place()[2] + QUARTERS - k) % QUARTERS * size, size)
        out_ref[pl.ds(at, size)] = ref[...]


def assemble(parts, after):
    return pl.pallas_call(
        assemble_kernel,
        out_shape=jax.ShapeDtypeStruct((parts[0].shape[0] * QUARTERS, 128), F32),
        in_specs=[WHOLE] * 4 + [ANY],
        out_specs=WHOLE,
        compiler_params=params(8),
        name="assemble",
    )(*parts, after)


def factor_kernel(replicas, ext_ref, p_ref, solve_ref, left_ref, hat_ref):
    rank = p_ref.shape[0]
    groups = rank // ROWS
    sub = lax.broadcasted_iota(jnp.int32, (ROWS, 2 * rank), 0)
    lane = lax.broadcasted_iota(jnp.int32, (ROWS, 2 * rank), 1)
    blocks = []
    for g in range(groups):
        tile = ext_ref[g // 2 * ROWS : (g // 2 + 1) * ROWS, (g % 2) * rank : (g % 2 + 1) * rank]
        unit = jnp.where(lane[:, :rank] == sub[:, :rank] + g * ROWS, 1.0, 0.0)
        blocks.append(jnp.concatenate([tile, unit], axis=1))
    for own in range(groups):
        spread = lambda g: [
            jnp.broadcast_to(blocks[g][:, own * ROWS + k : own * ROWS + k + 1], (ROWS, 2 * rank))
            for k in range(ROWS)
        ]
        columns = spread(own)
        rows, heads = [], []
        for k in range(ROWS):
            scale = 1.0 / columns[k][k : k + 1]
            row = blocks[own][k : k + 1] * scale
            head = {m: columns[m][k : k + 1] * scale for m in range(k + 1, ROWS)}
            factors = jnp.where(sub > k, columns[k], 0.0)
            blocks[own] = blocks[own] - factors * row
            for m, h in head.items():
                columns[m] = columns[m] - factors * h
            rows.append(row)
            heads.append(head)
        for g in range(own + 1, groups):
            columns = spread(g)
            for k in range(ROWS):
                blocks[g] = blocks[g] - columns[k] * rows[k]
                for m, h in heads[k].items():
                    columns[m] = columns[m] - columns[k] * h
    inverse = []
    for g in range(groups):
        diagonal = jnp.sum(
            jnp.where(lane == sub + g * ROWS, blocks[g], 0.0), axis=1, keepdims=True
        )
        inverse.append(blocks[g][:, rank:] / jnp.sqrt(diagonal))
    inverse = jnp.concatenate(inverse, axis=0)
    grams = ext_ref.shape[0] - ROWS
    solve = inverse * ext_ref[grams : grams + 1, :1] * (1.0 / (replicas * SHRINK))
    s1, s2, s3 = split(solve)
    solve_ref[...] = jnp.concatenate([s1, s1, s2, s2, s1, s3], axis=1)
    hat = jnp.dot(inverse, p_ref[...], precision=HIGHEST, preferred_element_type=F32)
    hat_ref[...] = hat
    left_ref[...] = hat.T.astype(BF16)


def factor(ext, p_mean, replicas):
    rank, rows = p_mean.shape
    return pl.pallas_call(
        functools.partial(factor_kernel, replicas),
        out_shape=[
            jax.ShapeDtypeStruct((rank, 6 * rank), BF16),
            jax.ShapeDtypeStruct((rows, rank), BF16),
            jax.ShapeDtypeStruct((rank, rows), F32),
        ],
        in_specs=[WHOLE] * 2,
        out_specs=[WHOLE] * 3,
        compiler_params=params(8),
        cost_estimate=cost(1 << 32, 1 << 20),
        name="factor",
    )(ext, p_mean)


def result_kernel(sources, more, width, solve_ref, left_ref, m_ref, *refs):
    refs, (error_ref, q_ref, sems) = refs[:-3], refs[-3:]
    if more == "hat":
        hat = pltpu.make_async_copy(refs[len(sources)], refs[-1], sems.at[0, len(sources)])
        hat.start()
    if more == "token":
        refs[-1][...] = jnp.zeros_like(refs[-1])
    error_hbm, q_hbm = refs[-3:-1] if more else refs[-2:]
    rank = solve_ref.shape[0]
    columns = q_ref.shape[2]
    left = left_ref[...]
    solve = solve_ref[...]

    def copies(n, base, at, size):
        to, here = pl.ds(pl.multiple_of(base + at, 128), size), pl.ds(at, size)
        return (
            pltpu.make_async_copy(error_ref.at[n, :, here], error_hbm.at[:, to], sems.at[0, n]),
            pltpu.make_async_copy(q_ref.at[n, :, here], q_hbm.at[:, to], sems.at[1, n]),
        )

    bases = []
    for n, (own, k) in enumerate(sources):
        t_ref = refs[n]
        half, turn, _ = place() if own else other_place()
        quarter = (turn + QUARTERS - k) % QUARTERS
        base = (half * QUARTERS + quarter) * columns
        bases.append(base)
        for at in range(0, columns, width):
            t = jnp.concatenate(
                [
                    jnp.concatenate(
                        [
                            t_ref[(g * columns + i) // 128 * ROWS : (g * columns + i) // 128 * ROWS + ROWS, :]
                            for i in range(at, at + width, 128)
                        ],
                        axis=1,
                    )
                    for g in range(rank // ROWS)
                ],
                axis=0,
            )
            t1, t2, t3 = split(t)
            t = jnp.concatenate([t1, t2, t1, t2, t3, t1], axis=0)
            new = jnp.dot(solve, t, preferred_element_type=F32)
            q_ref[n, :, at : at + width] = new
            decoded = jnp.dot(left, new.astype(BF16), preferred_element_type=F32)
            m = m_ref[:, pl.ds(pl.multiple_of(base + at, 128), width)]
            error_ref[n, :, at : at + width] = (m.astype(F32) - decoded).astype(BF16)
            for c in copies(n, base, at, width):
                c.start()
    for n, base in enumerate(bases):
        for c in copies(n, base, 0, columns):
            c.wait()
    if more == "hat":
        hat.wait()


def result(sources, totals, merged, solve, left, before, p_hat=None, token=False):
    rank = solve.shape[0]
    rows, columns = merged.shape
    quarter = columns // 2 // QUARTERS
    n = len(sources)
    held = [] if before is None else list(before)
    last = [] if p_hat is None else [p_hat]
    more = "hat" if last else "token" if token else ""
    return pl.pallas_call(
        functools.partial(result_kernel, sources, more, quarter // 2),
        out_shape=[pltpu.HBM((rows, columns), BF16), pltpu.HBM((rank, columns), F32)]
        + [pltpu.HBM(a.shape, F32) for a in last]
        + [pltpu.VMEM((ROWS, 128), F32)] * token,
        in_specs=[WHOLE] * (3 + n + len(last)) + [ANY] * len(held),
        out_specs=[ANY, ANY] + [ANY] * len(last) + [WHOLE] * token,
        scratch_shapes=[
            pltpu.VMEM((n, rows, quarter), BF16),
            pltpu.VMEM((n, rank, quarter), F32),
            pltpu.SemaphoreType.DMA((2, n + 1)),
        ],
        input_output_aliases={3 + n + len(last) + i: i for i in range(len(held))},
        compiler_params=params(12),
        cost_estimate=cost(1 << 33, 1 << 20),
        name="result",
    )(solve, left, merged, *totals, *last, *held)


def again_kernel(value_ref, out_ref):
    out_ref[...] = value_ref[...]


def again(value):
    return pl.pallas_call(
        again_kernel,
        out_shape=jax.ShapeDtypeStruct(value.shape, value.dtype),
        in_specs=[WHOLE],
        out_specs=WHOLE,
        compiler_params=params(4),
        cost_estimate=cost(RIGHT, 1 << 20),
        name="again",
    )(value)


def tie_kernel(value_ref, after_ref, out_ref):
    del value_ref, after_ref, out_ref


def tie(value, after):
    return pl.pallas_call(
        tie_kernel,
        out_shape=jax.ShapeDtypeStruct(value.shape, value.dtype),
        in_specs=[ANY] * 2,
        out_specs=ANY,
        input_output_aliases={0: 0},
        compiler_params=params(4),
        name="tie",
    )(value, after)


def body(gradient, error, q_start):
    rank = q_start.shape[0]
    replicas = SIZES[0] * SIZES[1]
    merged, p = merge(gradient[0], error[0], q_start)
    a, b, c = ring([p] * 3, 0, orders=("xz", "zx"), group=core_of)
    p = (p + a) + (b + c)
    sent, ext, p_mean, pieces = first_right(
        (2,), (p, *ring([p] * 3, 1, orders=("xz", "zx"), group=core_of)), merged, rank, replicas
    )
    got = swap(sent)
    sent = next_right(False, (1, 3, 0), pieces, merged, ext)
    got_next = swap(sent)
    kept = next_right(True, (2,), pieces, merged, sent)
    two, ext, weight = first_pair(kept, got, ext)
    (two,) = ring((two,), 0, (2,))
    kept = next_right(True, (1, 3, 0), pieces, merged, weight)
    *near, own = next_pair(kept, got_next, weight)
    own, *sent = add_quarters((own, *ring(near, 0, (1, 3)), two), ext)
    extra = ext.shape[0]
    (part,) = across(1, (own, *ring(sent, 1)), extra, True)
    total, ext = across(0, (part, *ring([part] * 3, 2)), extra, False)
    solve, left, p_hat = factor(ext, p_mean, replicas)
    total = assemble((total, *ring([total] * 3, 1)), solve)
    two, one, three = ring([total] * 3, 0, (2, 1, 3))

    def write(sources, totals, *after, **more):
        return result(sources, totals, merged, solve, left, *after, **more)

    own, other = True, False
    total = again(total)
    out = write(((own, 0),), (total,), None)
    *out, token = write(((other, 0),), (swap(total),), out, token=True)
    two = tie(two, token)
    *out, token = write(((own, 2),), (two,), out, token=True)
    one, three = tie(one, token), tie(three, token)
    out = write(((own, 1), (own, 3), (other, 2)), (one, three, swap(two)), out)
    new_error, q_new, p_hat = write(
        ((other, 1), (other, 3)), (swap(one), swap(three)), out, p_hat
    )
    return (new_error[None], p_hat, q_new)


def solution(mesh):
    fine = Mesh(mesh.devices.reshape(SIZES), AXES)
    return jax.shard_map(
        body,
        mesh=fine,
        in_specs=(P(DP, ("y", "c"), None), P(DP, ("y", "c"), None), P()),
        out_specs=(P(DP, ("y", "c"), None), P(None, ("y", "c")), P()),
        check_vma=False,
    )
```

```python
import functools

import jax
import jax.numpy as jnp
from jax import lax
from jax.experimental import pallas as pl
from jax.experimental.pallas import tpu as pltpu
from jax.sharding import Mesh, PartitionSpec as P

DP = ("z", "x")
AXES = ("z", "x", "y", "c")
SIZES = (4, 4, 4, 2)
HIGHEST = lax.Precision.HIGHEST
F32 = jnp.float32
BF16 = jnp.bfloat16
MIB = 1 << 20
ROWS = 8
QUARTERS = 4
SHRINK = 2.0**-16
RIGHT = 1 << 33
TURNS = (1, 2, 3)
ANY = pl.BlockSpec(memory_space=pl.ANY)
WHOLE = pl.BlockSpec(memory_space=pltpu.VMEM)


def params(mib):
    return pltpu.CompilerParams(vmem_limit_bytes=mib * MIB)


def cost(flops, nbytes):
    return pl.CostEstimate(flops=flops, bytes_accessed=nbytes, transcendentals=0)


def half_of(x, y, z, c):
    return (x + y + z + c) % 2


def core_of(x, y, z, c):
    return c


def half_of(x, y, z, c):
    return (x + y + z + c) % 2


MASKS = (1, 3)


def corner(kind, x, z):
    if kind == 0:
        return ((x ^ (x >> 1)) & 1) + 2 * ((z ^ (z >> 1)) & 1)
    return (x >> 1) + 2 * (z >> 1)


def place():
    x, y, z, c = (lax.axis_index(a) for a in ("x", "y", "z", "c"))
    half = half_of(x, y, z, c)
    zero, one = corner(0, x, z), corner(1, x, z)
    return half, jnp.where(half == 0, zero, one), jnp.where(half == 0, one, zero)


def other_place():
    half, first, second = place()
    return 1 - half, second, first


def index(z, x, y, c):
    return ((z * SIZES[1] + x) * SIZES[2] + y) * SIZES[3] + c


def everyone():
    return [
        (z, x, y, c)
        for z in range(SIZES[0])
        for x in range(SIZES[1])
        for y in range(SIZES[2])
        for c in range(SIZES[3])
    ]


def square(values, phase, turns, group=half_of):
    out = []
    for k, value in zip(turns, values):
        pairs = []
        for z, x, y, c in everyone():
            mask = MASKS[(group(x, y, z, c) + phase) % 2]
            to_x, to_z = x ^ (mask if k & 1 else 0), z ^ (mask if k & 2 else 0)
            core = c if group is core_of else (c + x + to_x + z + to_z) % 2
            pairs.append((index(z, x, y, c), index(to_z, to_x, y, core)))
        out.append(lax.ppermute(value, AXES, pairs))
    return out


def ring_y(value):
    out = []
    for k in (1, 3, 2):
        pairs = [
            (index(z, x, y, c), index(z, x, (y + k) % SIZES[2], (c + k) % 2))
            for z, x, y, c in everyone()
        ]
        out.append(lax.ppermute(value, AXES, pairs))
    return out


def swap(value):
    return lax.ppermute(value, "c", [(0, 1), (1, 0)])


def merge_kernel(cuts, g_hbm, e_hbm, q_hbm, m_ref, p_ref, g_ref, e_ref, q_ref, sems):
    rows = g_ref.shape[0]
    rank = q_ref.shape[0]

    def copies(i):
        at = pl.ds(cuts[i], cuts[i + 1] - cuts[i])
        return [
            pltpu.make_async_copy(src.at[:, at], dst.at[:, at], sems.at[n, i])
            for n, (src, dst) in enumerate(((g_hbm, g_ref), (e_hbm, e_ref), (q_hbm, q_ref)))
        ]

    for i in range(len(cuts) - 1):
        for c in copies(i):
            c.start()
    acc = jnp.zeros((rows, rank), F32)
    for i in range(len(cuts) - 1):
        for c in copies(i):
            c.wait()
        at = pl.ds(cuts[i], cuts[i + 1] - cuts[i])
        m = (g_ref[:, at].astype(F32) + e_ref[:, at].astype(F32)).astype(BF16)
        m_ref[:, at] = m
        acc = acc + lax.dot_general(
            m, q_ref[:, at], (((1,), (1,)), ((), ())), preferred_element_type=F32
        )
    p_ref[...] = pack(acc.T)


def pack(p):
    rank, rows = p.shape
    full = rows // 128
    half = rank // 2
    parts = [p[:, i * 128 : (i + 1) * 128] for i in range(full)]
    rest = p[:, full * 128 :]
    return jnp.concatenate(parts + [jnp.concatenate([rest[:half], rest[half:]], axis=1)], axis=0)


def unpack(packed, rank):
    full = packed.shape[0] // rank
    last = packed[full * rank :]
    rest = jnp.concatenate([last[:, :64], last[:, 64:]], axis=0)
    return jnp.concatenate(
        [packed[i * rank : (i + 1) * rank] for i in range(full)] + [rest], axis=1
    )


def merge(gradient, error, q_start):
    rows, columns = gradient.shape
    rank = q_start.shape[0]
    step = columns // 20
    cuts = [n * step for n in (0, 2, 4, 6, 8, 10, 12, 14, 16, 18, 19, 20)]
    gradient, error, q_start = (
        pltpu.with_memory_space_constraint(a, pltpu.HBM) for a in (gradient, error, q_start)
    )
    return pl.pallas_call(
        functools.partial(merge_kernel, cuts),
        out_shape=[pltpu.VMEM((rows, columns), BF16), pltpu.VMEM((rank * rows // 128, 128), F32)],
        in_specs=[ANY, ANY, ANY],
        out_specs=[WHOLE, WHOLE],
        scratch_shapes=[
            pltpu.VMEM((rows, columns), BF16),
            pltpu.VMEM((rows, columns), BF16),
            pltpu.VMEM((rank, columns), BF16),
            pltpu.SemaphoreType.DMA((3, len(cuts) - 1)),
        ],
        compiler_params=params(24),
        cost_estimate=cost(2 * rank * rows * columns, 4 * rows * columns),
        name="merge",
    )(gradient, error, q_start)


def right_tiles(quarters, pieces, m_ref, out_ref):
    rank = pieces.shape[0] // 3
    width = m_ref.shape[1] // 2 // QUARTERS
    main = pieces.shape[1] // 256 * 256
    rest = jnp.concatenate(
        [pieces[i : i + rank, main:] for i in range(0, 3 * rank, rank)], axis=1
    )
    to = 0
    for quarter in quarters:
        at = pl.multiple_of(quarter * width, width)
        m = m_ref[:, pl.ds(at, width)]
        t = jnp.dot(pieces[:, :main], m[:main], preferred_element_type=F32)
        t = t[:rank] + (t[rank : 2 * rank] + t[2 * rank :])
        m = jnp.concatenate([m[main:]] * 3, axis=0)
        t = t + jnp.dot(rest, m, preferred_element_type=F32)
        for g in range(rank // ROWS):
            for n in range(width // 128):
                out_ref[to : to + ROWS, :] = t[g * ROWS : (g + 1) * ROWS, n * 128 : (n + 1) * 128]
                to += ROWS


def quarters_of(own, turns):
    half, turn, _ = place() if own else other_place()
    return [half * QUARTERS + (turn ^ k) for k in turns]


def split(n):
    high = n.astype(BF16)
    n = n - high.astype(F32)
    middle = n.astype(BF16)
    return high, middle, (n - middle.astype(F32)).astype(BF16)


def first_right_kernel(replicas, rank, turns, a_ref, b_ref, c_ref, d_ref, m_ref, out_ref, ext_ref, p_ref, pieces_ref):
    p = (a_ref[...] + b_ref[...] + (c_ref[...] + d_ref[...])) * (1.0 / replicas)
    peak = jnp.max(jnp.abs(p), axis=(0, 1), keepdims=True)
    peak = jnp.where(peak > 0, peak, 1.0)
    p = unpack(p, rank)
    p_ref[...] = p
    pieces = jnp.concatenate(split(p / peak * SHRINK), axis=0)
    pieces_ref[...] = pieces
    right_tiles(quarters_of(False, turns), pieces, m_ref, out_ref)
    gram = lax.dot_general(
        p, p, (((1,), (1,)), ((), ())), precision=HIGHEST, preferred_element_type=F32
    )
    two = 2 * ROWS
    ext = jnp.concatenate(
        [
            jnp.concatenate([gram[i : i + ROWS], gram[i + ROWS : i + two]], axis=1)
            for i in range(0, rank, two)
        ]
        + [jnp.broadcast_to(peak, (ROWS, 128))],
        axis=0,
    )
    ext_ref[...] = ext
    out_ref[out_ref.shape[0] - ext.shape[0] :, :] = ext


def next_right_kernel(own, turns, pieces_ref, m_ref, after_ref, out_ref):
    del after_ref
    right_tiles(quarters_of(own, turns), pieces_ref[...], m_ref, out_ref)


def first_right(turns, parts, merged, rank, replicas):
    rows, columns = merged.shape
    size = rank * columns // 1024
    extra = rank * rank // 128 + ROWS
    return pl.pallas_call(
        functools.partial(first_right_kernel, replicas, rank, turns),
        out_shape=[
            jax.ShapeDtypeStruct((size + extra, 128), F32),
            pltpu.VMEM((extra, 128), F32),
            pltpu.VMEM((rank, rows), F32),
            pltpu.VMEM((3 * rank, rows), BF16),
        ],
        in_specs=[WHOLE] * 5,
        out_specs=[WHOLE] * 4,
        compiler_params=params(12),
        cost_estimate=cost(RIGHT, 1 << 20),
        name="first_right",
    )(*parts, merged)


def next_right(own, turns, pieces, merged, after):
    size = pieces.shape[0] // 3 * merged.shape[1] // 1024 * len(turns)
    return pl.pallas_call(
        functools.partial(next_right_kernel, own, turns),
        out_shape=jax.ShapeDtypeStruct((size, 128), F32),
        in_specs=[WHOLE, WHOLE, ANY],
        out_specs=WHOLE,
        compiler_params=params(12),
        cost_estimate=cost(RIGHT, 1 << 20),
        name="next_right",
    )(pieces, merged, after)


def first_pair_kernel(kept_ref, got_ref, ext_ref, out_ref, pair_ref, weight_ref):
    grams = ext_ref.shape[0] - ROWS
    size = kept_ref.shape[0]
    own, its = ext_ref[grams : grams + 1, :1], got_ref[size + grams : size + grams + 1, :1]
    top = jnp.maximum(own, its)
    pair_ref[:grams] = ext_ref[:grams] + got_ref[size : size + grams]
    pair_ref[grams:] = jnp.broadcast_to(top, (ROWS, 128))
    own, its = own / top, its / top
    weight_ref[:ROWS] = jnp.broadcast_to(own, (ROWS, 128))
    weight_ref[ROWS:] = jnp.broadcast_to(its, (ROWS, 128))
    out_ref[...] = kept_ref[...] * own + got_ref[:size] * its


def first_pair(kept, got, ext):
    return pl.pallas_call(
        first_pair_kernel,
        out_shape=[
            jax.ShapeDtypeStruct(kept.shape, F32),
            pltpu.VMEM(ext.shape, F32),
            pltpu.VMEM((2 * ROWS, 128), F32),
        ],
        in_specs=[WHOLE] * 3,
        out_specs=[WHOLE] * 3,
        compiler_params=params(8),
        name="first_pair",
    )(kept, got, ext)


def next_pair_kernel(kept_ref, got_ref, weight_ref, *out):
    own, its = weight_ref[:1, :1], weight_ref[ROWS : ROWS + 1, :1]
    size = out[0].shape[0]
    for n, ref in enumerate(out):
        at = slice(n * size, (n + 1) * size)
        ref[...] = kept_ref[at] * own + got_ref[at] * its


def next_pair(kept, got, weight):
    size = kept.shape[0] // 3
    return pl.pallas_call(
        next_pair_kernel,
        out_shape=[jax.ShapeDtypeStruct((size, 128), F32)] * 3,
        in_specs=[WHOLE] * 3,
        out_specs=[WHOLE] * 3,
        compiler_params=params(8),
        name="next_pair",
    )(kept, got, weight)


def add_quarters_kernel(a_ref, b_ref, c_ref, d_ref, *out):
    size = a_ref.shape[0] // QUARTERS
    for k, ref in zip((0,) + TURNS, out):
        at = pl.ds(pl.multiple_of((place()[2] ^ k) * size, size), size)
        ref[...] = (a_ref[at] + b_ref[at]) + (c_ref[at] + d_ref[at])


def add_quarters(parts):
    size = parts[0].shape[0] // QUARTERS
    return pl.pallas_call(
        add_quarters_kernel,
        out_shape=[jax.ShapeDtypeStruct((size, 128), F32)] * QUARTERS,
        in_specs=[WHOLE] * QUARTERS,
        out_specs=[WHOLE] * QUARTERS,
        compiler_params=params(8),
        name="add_quarters",
    )(*parts)


def add_parts_kernel(a_ref, b_ref, c_ref, d_ref, ext_ref, out_ref):
    size = a_ref.shape[0]
    out_ref[:size] = (a_ref[...] + b_ref[...]) + (c_ref[...] + d_ref[...])
    out_ref[size:] = ext_ref[...]


def add_parts(parts, ext):
    return pl.pallas_call(
        add_parts_kernel,
        out_shape=jax.ShapeDtypeStruct((parts[0].shape[0] + ext.shape[0], 128), F32),
        in_specs=[WHOLE] * 5,
        out_specs=WHOLE,
        compiler_params=params(8),
        name="add_parts",
    )(*parts, ext)


def across_kernel(a_ref, b_ref, c_ref, d_ref, out_ref, ext_ref):
    size = out_ref.shape[0]
    grams = ext_ref.shape[0] - ROWS
    refs = (a_ref, b_ref, c_ref, d_ref)
    peaks = [r[size + grams : size + grams + 1, :1] for r in refs]
    top = jnp.maximum(jnp.maximum(peaks[0], peaks[1]), jnp.maximum(peaks[2], peaks[3]))
    a, b, c, d = (r[:size] * (k / top) for r, k in zip(refs, peaks))
    out_ref[...] = (a + b) + (c + d)
    a, b, c, d = (r[size : size + grams] for r in refs)
    ext_ref[:grams] = (a + b) + (c + d)
    ext_ref[grams:] = jnp.broadcast_to(top, (ROWS, 128))


def across(parts, extra):
    return pl.pallas_call(
        across_kernel,
        out_shape=[
            jax.ShapeDtypeStruct((parts[0].shape[0] - extra, 128), F32),
            pltpu.VMEM((extra, 128), F32),
        ],
        in_specs=[WHOLE] * 4,
        out_specs=[WHOLE] * 2,
        compiler_params=params(8),
        name="across",
    )(*parts)


def assemble_kernel(a_ref, b_ref, c_ref, d_ref, after_ref, out_ref):
    del after_ref
    size = a_ref.shape[0]
    for k, ref in zip((0,) + TURNS, (a_ref, b_ref, c_ref, d_ref)):
        at = pl.multiple_of((place()[2] ^ k) * size, size)
        out_ref[pl.ds(at, size)] = ref[...]


def assemble(parts, after):
    return pl.pallas_call(
        assemble_kernel,
        out_shape=jax.ShapeDtypeStruct((parts[0].shape[0] * QUARTERS, 128), F32),
        in_specs=[WHOLE] * 4 + [ANY],
        out_specs=WHOLE,
        compiler_params=params(8),
        name="assemble",
    )(*parts, after)


def factor_kernel(replicas, ext_ref, p_ref, solve_ref, left_ref, hat_ref):
    rank = p_ref.shape[0]
    groups = rank // ROWS
    sub = lax.broadcasted_iota(jnp.int32, (ROWS, 2 * rank), 0)
    lane = lax.broadcasted_iota(jnp.int32, (ROWS, 2 * rank), 1)
    blocks = []
    for g in range(groups):
        tile = ext_ref[g // 2 * ROWS : (g // 2 + 1) * ROWS, (g % 2) * rank : (g % 2 + 1) * rank]
        unit = jnp.where(lane[:, :rank] == sub[:, :rank] + g * ROWS, 1.0, 0.0)
        blocks.append(jnp.concatenate([tile, unit], axis=1))
    for own in range(groups):
        spread = lambda g: [
            jnp.broadcast_to(blocks[g][:, own * ROWS + k : own * ROWS + k + 1], (ROWS, 2 * rank))
            for k in range(ROWS)
        ]
        columns = spread(own)
        rows, heads = [], []
        for k in range(ROWS):
            scale = 1.0 / columns[k][k : k + 1]
            row = blocks[own][k : k + 1] * scale
            head = {m: columns[m][k : k + 1] * scale for m in range(k + 1, ROWS)}
            factors = jnp.where(sub > k, columns[k], 0.0)
            blocks[own] = blocks[own] - factors * row
            for m, h in head.items():
                columns[m] = columns[m] - factors * h
            rows.append(row)
            heads.append(head)
        for g in range(own + 1, groups):
            columns = spread(g)
            for k in range(ROWS):
                blocks[g] = blocks[g] - columns[k] * rows[k]
                for m, h in heads[k].items():
                    columns[m] = columns[m] - columns[k] * h
    inverse = []
    for g in range(groups):
        diagonal = jnp.sum(
            jnp.where(lane == sub + g * ROWS, blocks[g], 0.0), axis=1, keepdims=True
        )
        inverse.append(blocks[g][:, rank:] / jnp.sqrt(diagonal))
    inverse = jnp.concatenate(inverse, axis=0)
    grams = ext_ref.shape[0] - ROWS
    solve = inverse * ext_ref[grams : grams + 1, :1] * (1.0 / (replicas * SHRINK))
    s1, s2, s3 = split(solve)
    solve_ref[...] = jnp.concatenate([s1, s1, s2, s2, s1, s3], axis=1)
    hat = jnp.dot(inverse, p_ref[...], precision=HIGHEST, preferred_element_type=F32)
    hat_ref[...] = hat
    left_ref[...] = hat.T.astype(BF16)


def factor(ext, p_mean, replicas):
    rank, rows = p_mean.shape
    return pl.pallas_call(
        functools.partial(factor_kernel, replicas),
        out_shape=[
            jax.ShapeDtypeStruct((rank, 6 * rank), BF16),
            jax.ShapeDtypeStruct((rows, rank), BF16),
            jax.ShapeDtypeStruct((rank, rows), F32),
        ],
        in_specs=[WHOLE] * 2,
        out_specs=[WHOLE] * 3,
        compiler_params=params(8),
        cost_estimate=cost(1 << 32, 1 << 20),
        name="factor",
    )(ext, p_mean)


def result_kernel(sources, more, width, solve_ref, left_ref, m_ref, *refs):
    refs, (error_ref, q_ref, sems) = refs[:-3], refs[-3:]
    if more == "hat":
        hat = pltpu.make_async_copy(refs[len(sources)], refs[-1], sems.at[0, len(sources)])
        hat.start()
    if more == "token":
        refs[-1][...] = jnp.zeros_like(refs[-1])
    error_hbm, q_hbm = refs[-3:-1] if more else refs[-2:]
    rank = solve_ref.shape[0]
    columns = q_ref.shape[2]
    left = left_ref[...]
    solve = solve_ref[...]

    def copies(n, base, at, size):
        to, here = pl.ds(pl.multiple_of(base + at, 128), size), pl.ds(at, size)
        return (
            pltpu.make_async_copy(error_ref.at[n, :, here], error_hbm.at[:, to], sems.at[0, n]),
            pltpu.make_async_copy(q_ref.at[n, :, here], q_hbm.at[:, to], sems.at[1, n]),
        )

    bases = []
    for n, (own, k) in enumerate(sources):
        t_ref = refs[n]
        half, turn, _ = place() if own else other_place()
        base = (half * QUARTERS + (turn ^ k)) * columns
        bases.append(base)
        for at in range(0, columns, width):
            t = jnp.concatenate(
                [
                    jnp.concatenate(
                        [
                            t_ref[(g * columns + i) // 128 * ROWS : (g * columns + i) // 128 * ROWS + ROWS, :]
                            for i in range(at, at + width, 128)
                        ],
                        axis=1,
                    )
                    for g in range(rank // ROWS)
                ],
                axis=0,
            )
            t1, t2, t3 = split(t)
            t = jnp.concatenate([t1, t2, t1, t2, t3, t1], axis=0)
            new = jnp.dot(solve, t, preferred_element_type=F32)
            q_ref[n, :, at : at + width] = new
            decoded = jnp.dot(left, new.astype(BF16), preferred_element_type=F32)
            m = m_ref[:, pl.ds(pl.multiple_of(base + at, 128), width)]
            error_ref[n, :, at : at + width] = (m.astype(F32) - decoded).astype(BF16)
            for c in copies(n, base, at, width):
                c.start()
    for n, base in enumerate(bases):
        for c in copies(n, base, 0, columns):
            c.wait()
    if more == "hat":
        hat.wait()


def result(sources, totals, merged, solve, left, before, p_hat=None, token=False):
    rank = solve.shape[0]
    rows, columns = merged.shape
    quarter = columns // 2 // QUARTERS
    n = len(sources)
    held = [] if before is None else list(before)
    last = [] if p_hat is None else [p_hat]
    more = "hat" if last else "token" if token else ""
    return pl.pallas_call(
        functools.partial(result_kernel, sources, more, quarter // 2),
        out_shape=[pltpu.HBM((rows, columns), BF16), pltpu.HBM((rank, columns), F32)]
        + [pltpu.HBM(a.shape, F32) for a in last]
        + [pltpu.VMEM((ROWS, 128), F32)] * token,
        in_specs=[WHOLE] * (3 + n + len(last)) + [ANY] * len(held),
        out_specs=[ANY, ANY] + [ANY] * len(last) + [WHOLE] * token,
        scratch_shapes=[
            pltpu.VMEM((n, rows, quarter), BF16),
            pltpu.VMEM((n, rank, quarter), F32),
            pltpu.SemaphoreType.DMA((2, n + 1)),
        ],
        input_output_aliases={3 + n + len(last) + i: i for i in range(len(held))},
        compiler_params=params(12),
        cost_estimate=cost(1 << 33, 1 << 20),
        name="result",
    )(solve, left, merged, *totals, *last, *held)


def again_kernel(value_ref, out_ref):
    out_ref[...] = value_ref[...]


def again(value):
    return pl.pallas_call(
        again_kernel,
        out_shape=jax.ShapeDtypeStruct(value.shape, value.dtype),
        in_specs=[WHOLE],
        out_specs=WHOLE,
        compiler_params=params(4),
        cost_estimate=cost(RIGHT, 1 << 20),
        name="again",
    )(value)


def tie_kernel(value_ref, after_ref, out_ref):
    del value_ref, after_ref, out_ref


def tie(value, after):
    return pl.pallas_call(
        tie_kernel,
        out_shape=jax.ShapeDtypeStruct(value.shape, value.dtype),
        in_specs=[ANY] * 2,
        out_specs=ANY,
        input_output_aliases={0: 0},
        compiler_params=params(4),
        name="tie",
    )(value, after)


def body(gradient, error, q_start):
    rank = q_start.shape[0]
    replicas = SIZES[0] * SIZES[1]
    merged, p = merge(gradient[0], error[0], q_start)
    a, b, c = square([p] * 3, 0, TURNS, core_of)
    p = (p + a) + (b + c)
    sent, ext, p_mean, pieces = first_right(
        (3,), (p, *square([p] * 3, 1, TURNS, core_of)), merged, rank, replicas
    )
    got = swap(sent)
    sent = next_right(False, (1, 2, 0), pieces, merged, ext)
    got_next = swap(sent)
    kept = next_right(True, (3,), pieces, merged, sent)
    far, ext, weight = first_pair(kept, got, ext)
    (far,) = square((far,), 0, (3,))
    kept = next_right(True, (1, 2, 0), pieces, merged, weight)
    *near, own = next_pair(kept, got_next, weight)
    own, *sent = add_quarters((own, *square(near, 0, (1, 2)), far))
    part = add_parts((own, *square(sent, 1, TURNS)), ext)
    total, ext = across((part, *ring_y(part)), ext.shape[0])
    solve, left, p_hat = factor(ext, p_mean, replicas)
    total = assemble((total, *square([total] * 3, 1, TURNS)), solve)
    three, one, two = square([total] * 3, 0, (3, 1, 2))

    def write(sources, totals, *after, **more):
        return result(sources, totals, merged, solve, left, *after, **more)

    own, other = True, False
    total = again(total)
    out = write(((own, 0),), (total,), None)
    *out, token = write(((other, 0),), (swap(total),), out, token=True)
    three = tie(three, token)
    *out, token = write(((own, 3),), (three,), out, token=True)
    one, two = tie(one, token), tie(two, token)
    out = write(((own, 1), (own, 2), (other, 3)), (one, two, swap(three)), out)
    new_error, q_new, p_hat = write(
        ((other, 1), (other, 2)), (swap(one), swap(two)), out, p_hat
    )
    return (new_error[None], p_hat, q_new)


def solution(mesh):
    fine = Mesh(mesh.devices.reshape(SIZES), AXES)
    return jax.shard_map(
        body,
        mesh=fine,
        in_specs=(P(DP, ("y", "c"), None), P(DP, ("y", "c"), None), P()),
        out_specs=(P(DP, ("y", "c"), None), P(None, ("y", "c")), P()),
        check_vma=False,
    )
```

```python
import functools

import jax
import jax.numpy as jnp
from jax import lax
from jax.experimental import pallas as pl
from jax.experimental.pallas import tpu as pltpu
from jax.sharding import Mesh, PartitionSpec as P

DP = ("z", "x")
AXES = ("z", "x", "y", "c")
SIZES = (4, 4, 4, 2)
HIGHEST = lax.Precision.HIGHEST
F32 = jnp.float32
BF16 = jnp.bfloat16
MIB = 1 << 20
ROWS = 8
QUARTERS = 4
SHRINK = 2.0**-16
RIGHT = 1 << 33
SHIFTS = (1, 3, 2)
ANY = pl.BlockSpec(memory_space=pl.ANY)
WHOLE = pl.BlockSpec(memory_space=pltpu.VMEM)


def params(mib):
    return pltpu.CompilerParams(vmem_limit_bytes=mib * MIB)


def cost(flops, nbytes):
    return pl.CostEstimate(flops=flops, bytes_accessed=nbytes, transcendentals=0)


def half_of(x, y, z, c):
    return (x + y + z + c) % 2


def core_of(x, y, z, c):
    return c


def place():
    x, y, z, c = (lax.axis_index(a) for a in ("x", "y", "z", "c"))
    half = half_of(x, y, z, c)
    return half, jnp.where(half == 0, x, z), jnp.where(half == 0, z, y)


def other_place():
    x, y, z, c = (lax.axis_index(a) for a in ("x", "y", "z", "c"))
    half = 1 - half_of(x, y, z, c)
    return half, jnp.where(half == 0, x, z), jnp.where(half == 0, z, y)


def index(z, x, y, c):
    return ((z * SIZES[1] + x) * SIZES[2] + y) * SIZES[3] + c


def everyone():
    return [
        (z, x, y, c)
        for z in range(SIZES[0])
        for x in range(SIZES[1])
        for y in range(SIZES[2])
        for c in range(SIZES[3])
    ]


def ring(values, phase, shifts=SHIFTS, orders=("xzy", "zyx"), group=half_of):
    out = []
    for k, value in zip(shifts, values):
        pairs = []
        for z, x, y, c in everyone():
            to = {"z": z, "x": x, "y": y}
            axis = orders[group(x, y, z, c)][phase]
            to[axis] = (to[axis] + k) % SIZES[AXES.index(axis)]
            core = c if group is core_of else (c + k) % 2
            pairs.append((index(z, x, y, c), index(*to.values(), core)))
        out.append(lax.ppermute(value, AXES, pairs))
    return out


def swap(value):
    return lax.ppermute(value, "c", [(0, 1), (1, 0)])


def merge_kernel(cuts, g_hbm, e_hbm, q_hbm, m_ref, p_ref, g_ref, e_ref, q_ref, sems):
    rows = g_ref.shape[0]
    rank = q_ref.shape[0]

    def copies(i):
        at = pl.ds(cuts[i], cuts[i + 1] - cuts[i])
        return [
            pltpu.make_async_copy(src.at[:, at], dst.at[:, at], sems.at[n, i])
            for n, (src, dst) in enumerate(((g_hbm, g_ref), (e_hbm, e_ref), (q_hbm, q_ref)))
        ]

    for i in range(len(cuts) - 1):
        for c in copies(i):
            c.start()
    acc = jnp.zeros((rows, rank), F32)
    for i in range(len(cuts) - 1):
        for c in copies(i):
            c.wait()
        at = pl.ds(cuts[i], cuts[i + 1] - cuts[i])
        m = (g_ref[:, at].astype(F32) + e_ref[:, at].astype(F32)).astype(BF16)
        m_ref[:, at] = m
        acc = acc + lax.dot_general(
            m, q_ref[:, at], (((1,), (1,)), ((), ())), preferred_element_type=F32
        )
    p_ref[...] = pack(acc.T)


def pack(p):
    rank, rows = p.shape
    full = rows // 128
    half = rank // 2
    parts = [p[:, i * 128 : (i + 1) * 128] for i in range(full)]
    rest = p[:, full * 128 :]
    return jnp.concatenate(parts + [jnp.concatenate([rest[:half], rest[half:]], axis=1)], axis=0)


def unpack(packed, rank):
    full = packed.shape[0] // rank
    last = packed[full * rank :]
    rest = jnp.concatenate([last[:, :64], last[:, 64:]], axis=0)
    return jnp.concatenate(
        [packed[i * rank : (i + 1) * rank] for i in range(full)] + [rest], axis=1
    )


def merge(gradient, error, q_start):
    rows, columns = gradient.shape
    rank = q_start.shape[0]
    step = columns // 20
    cuts = [n * step for n in (0, 2, 4, 6, 8, 10, 12, 14, 16, 18, 19, 20)]
    gradient, error, q_start = (
        pltpu.with_memory_space_constraint(a, pltpu.HBM) for a in (gradient, error, q_start)
    )
    return pl.pallas_call(
        functools.partial(merge_kernel, cuts),
        out_shape=[pltpu.VMEM((rows, columns), BF16), pltpu.VMEM((rank * rows // 128, 128), F32)],
        in_specs=[ANY, ANY, ANY],
        out_specs=[WHOLE, WHOLE],
        scratch_shapes=[
            pltpu.VMEM((rows, columns), BF16),
            pltpu.VMEM((rows, columns), BF16),
            pltpu.VMEM((rank, columns), BF16),
            pltpu.SemaphoreType.DMA((3, len(cuts) - 1)),
        ],
        compiler_params=params(24),
        cost_estimate=cost(2 * rank * rows * columns, 4 * rows * columns),
        name="merge",
    )(gradient, error, q_start)


def right_tiles(quarters, pieces, m_ref, out_ref):
    rank = pieces.shape[0] // 3
    width = m_ref.shape[1] // 2 // QUARTERS
    main = pieces.shape[1] // 256 * 256
    rest = jnp.concatenate(
        [pieces[i : i + rank, main:] for i in range(0, 3 * rank, rank)], axis=1
    )
    to = 0
    for quarter in quarters:
        at = pl.multiple_of(quarter * width, width)
        m = m_ref[:, pl.ds(at, width)]
        t = jnp.dot(pieces[:, :main], m[:main], preferred_element_type=F32)
        t = t[:rank] + (t[rank : 2 * rank] + t[2 * rank :])
        m = jnp.concatenate([m[main:]] * 3, axis=0)
        t = t + jnp.dot(rest, m, preferred_element_type=F32)
        for g in range(rank // ROWS):
            for n in range(width // 128):
                out_ref[to : to + ROWS, :] = t[g * ROWS : (g + 1) * ROWS, n * 128 : (n + 1) * 128]
                to += ROWS


def quarters_of(own, turns):
    half, turn, _ = place() if own else other_place()
    return [half * QUARTERS + (turn + k) % QUARTERS for k in turns]


def split(n):
    high = n.astype(BF16)
    n = n - high.astype(F32)
    middle = n.astype(BF16)
    return high, middle, (n - middle.astype(F32)).astype(BF16)


def first_right_kernel(replicas, rank, turns, a_ref, b_ref, c_ref, d_ref, m_ref, out_ref, ext_ref, p_ref, pieces_ref):
    p = (a_ref[...] + b_ref[...] + (c_ref[...] + d_ref[...])) * (1.0 / replicas)
    peak = jnp.max(jnp.abs(p), axis=(0, 1), keepdims=True)
    peak = jnp.where(peak > 0, peak, 1.0)
    p = unpack(p, rank)
    p_ref[...] = p
    pieces = jnp.concatenate(split(p / peak * SHRINK), axis=0)
    pieces_ref[...] = pieces
    right_tiles(quarters_of(False, turns), pieces, m_ref, out_ref)
    gram = lax.dot_general(
        p, p, (((1,), (1,)), ((), ())), precision=HIGHEST, preferred_element_type=F32
    )
    two = 2 * ROWS
    ext = jnp.concatenate(
        [
            jnp.concatenate([gram[i : i + ROWS], gram[i + ROWS : i + two]], axis=1)
            for i in range(0, rank, two)
        ]
        + [jnp.broadcast_to(peak, (ROWS, 128))],
        axis=0,
    )
    ext_ref[...] = ext
    out_ref[out_ref.shape[0] - ext.shape[0] :, :] = ext


def next_right_kernel(own, turns, pieces_ref, m_ref, after_ref, out_ref):
    del after_ref
    right_tiles(quarters_of(own, turns), pieces_ref[...], m_ref, out_ref)


def first_right(turns, parts, merged, rank, replicas):
    rows, columns = merged.shape
    size = rank * columns // 1024
    extra = rank * rank // 128 + ROWS
    return pl.pallas_call(
        functools.partial(first_right_kernel, replicas, rank, turns),
        out_shape=[
            jax.ShapeDtypeStruct((size + extra, 128), F32),
            pltpu.VMEM((extra, 128), F32),
            pltpu.VMEM((rank, rows), F32),
            pltpu.VMEM((3 * rank, rows), BF16),
        ],
        in_specs=[WHOLE] * 5,
        out_specs=[WHOLE] * 4,
        compiler_params=params(12),
        cost_estimate=cost(RIGHT, 1 << 20),
        name="first_right",
    )(*parts, merged)


def next_right(own, turns, pieces, merged, after):
    size = pieces.shape[0] // 3 * merged.shape[1] // 1024 * len(turns)
    return pl.pallas_call(
        functools.partial(next_right_kernel, own, turns),
        out_shape=jax.ShapeDtypeStruct((size, 128), F32),
        in_specs=[WHOLE, WHOLE, ANY],
        out_specs=WHOLE,
        compiler_params=params(12),
        cost_estimate=cost(RIGHT, 1 << 20),
        name="next_right",
    )(pieces, merged, after)


def first_pair_kernel(kept_ref, got_ref, ext_ref, out_ref, pair_ref, weight_ref):
    grams = ext_ref.shape[0] - ROWS
    size = kept_ref.shape[0]
    own, its = ext_ref[grams : grams + 1, :1], got_ref[size + grams : size + grams + 1, :1]
    top = jnp.maximum(own, its)
    pair_ref[:grams] = ext_ref[:grams] + got_ref[size : size + grams]
    pair_ref[grams:] = jnp.broadcast_to(top, (ROWS, 128))
    own, its = own / top, its / top
    weight_ref[:ROWS] = jnp.broadcast_to(own, (ROWS, 128))
    weight_ref[ROWS:] = jnp.broadcast_to(its, (ROWS, 128))
    out_ref[...] = kept_ref[...] * own + got_ref[:size] * its


def first_pair(kept, got, ext):
    return pl.pallas_call(
        first_pair_kernel,
        out_shape=[
            jax.ShapeDtypeStruct(kept.shape, F32),
            pltpu.VMEM(ext.shape, F32),
            pltpu.VMEM((2 * ROWS, 128), F32),
        ],
        in_specs=[WHOLE] * 3,
        out_specs=[WHOLE] * 3,
        compiler_params=params(8),
        name="first_pair",
    )(kept, got, ext)


def next_pair_kernel(kept_ref, got_ref, weight_ref, *out):
    own, its = weight_ref[:1, :1], weight_ref[ROWS : ROWS + 1, :1]
    size = out[0].shape[0]
    for n, ref in enumerate(out):
        at = slice(n * size, (n + 1) * size)
        ref[...] = kept_ref[at] * own + got_ref[at] * its


def next_pair(kept, got, weight):
    size = kept.shape[0] // 3
    return pl.pallas_call(
        next_pair_kernel,
        out_shape=[jax.ShapeDtypeStruct((size, 128), F32)] * 3,
        in_specs=[WHOLE] * 3,
        out_specs=[WHOLE] * 3,
        compiler_params=params(8),
        name="next_pair",
    )(kept, got, weight)


def add_quarters_kernel(a_ref, b_ref, c_ref, d_ref, ext_ref, *out):
    size = a_ref.shape[0] // QUARTERS
    for k, ref in zip((0,) + SHIFTS, out):
        at = pl.ds(pl.multiple_of((place()[2] + k) % QUARTERS * size, size), size)
        ref[:size] = (a_ref[at] + b_ref[at]) + (c_ref[at] + d_ref[at])
        ref[size:] = ext_ref[...]


def add_quarters(parts, ext):
    size = parts[0].shape[0] // QUARTERS
    return pl.pallas_call(
        add_quarters_kernel,
        out_shape=[jax.ShapeDtypeStruct((size + ext.shape[0], 128), F32)] * QUARTERS,
        in_specs=[WHOLE] * (QUARTERS + 1),
        out_specs=[WHOLE] * QUARTERS,
        compiler_params=params(8),
        name="add_quarters",
    )(*parts, ext)


def across_kernel(half_along_y, extra, a_ref, b_ref, c_ref, d_ref, out_ref, *ext_ref):
    grams = extra - ROWS
    size = a_ref.shape[0] - extra
    refs = (a_ref, b_ref, c_ref, d_ref)
    peaks = [r[size + grams : size + grams + 1, :1] for r in refs]
    top = jnp.maximum(jnp.maximum(peaks[0], peaks[1]), jnp.maximum(peaks[2], peaks[3]))
    a, b, c, d = (r[:size] * (k / top) for r, k in zip(refs, peaks))
    out_ref[:size] = (a + b) + (c + d)
    a, b, c, d = (r[size : size + grams] for r in refs)
    gram = jnp.where(place()[0] == half_along_y, (a + b) + (c + d), a)
    ext = out_ref.at[size:] if not ext_ref else ext_ref[0]
    ext[:grams] = gram
    ext[grams:] = jnp.broadcast_to(top, (ROWS, 128))


def across(half_along_y, parts, extra, keep):
    rows = parts[0].shape[0]
    out = [jax.ShapeDtypeStruct((rows, 128), F32)]
    if not keep:
        out = [jax.ShapeDtypeStruct((rows - extra, 128), F32), pltpu.VMEM((extra, 128), F32)]
    return pl.pallas_call(
        functools.partial(across_kernel, half_along_y, extra),
        out_shape=out,
        in_specs=[WHOLE] * 4,
        out_specs=[WHOLE] * len(out),
        compiler_params=params(8),
        name="across",
    )(*parts)


def assemble_kernel(a_ref, b_ref, c_ref, d_ref, after_ref, out_ref):
    del after_ref
    size = a_ref.shape[0]
    for k, ref in zip((0,) + SHIFTS, (a_ref, b_ref, c_ref, d_ref)):
        at = pl.multiple_of((place()[2] + QUARTERS - k) % QUARTERS * size, size)
        out_ref[pl.ds(at, size)] = ref[...]


def assemble(parts, after):
    return pl.pallas_call(
        assemble_kernel,
        out_shape=jax.ShapeDtypeStruct((parts[0].shape[0] * QUARTERS, 128), F32),
        in_specs=[WHOLE] * 4 + [ANY],
        out_specs=WHOLE,
        compiler_params=params(8),
        name="assemble",
    )(*parts, after)


def factor_kernel(replicas, ext_ref, p_ref, solve_ref, left_ref, hat_ref):
    rank = p_ref.shape[0]
    groups = rank // ROWS
    sub = lax.broadcasted_iota(jnp.int32, (ROWS, 2 * rank), 0)
    lane = lax.broadcasted_iota(jnp.int32, (ROWS, 2 * rank), 1)
    blocks = []
    for g in range(groups):
        tile = ext_ref[g // 2 * ROWS : (g // 2 + 1) * ROWS, (g % 2) * rank : (g % 2 + 1) * rank]
        unit = jnp.where(lane[:, :rank] == sub[:, :rank] + g * ROWS, 1.0, 0.0)
        blocks.append(jnp.concatenate([tile, unit], axis=1))
    for own in range(groups):
        spread = lambda g: [
            jnp.broadcast_to(blocks[g][:, own * ROWS + k : own * ROWS + k + 1], (ROWS, 2 * rank))
            for k in range(ROWS)
        ]
        columns = spread(own)
        rows, heads = [], []
        for k in range(ROWS):
            scale = 1.0 / columns[k][k : k + 1]
            row = blocks[own][k : k + 1] * scale
            head = {m: columns[m][k : k + 1] * scale for m in range(k + 1, ROWS)}
            factors = jnp.where(sub > k, columns[k], 0.0)
            blocks[own] = blocks[own] - factors * row
            for m, h in head.items():
                columns[m] = columns[m] - factors * h
            rows.append(row)
            heads.append(head)
        for g in range(own + 1, groups):
            columns = spread(g)
            for k in range(ROWS):
                blocks[g] = blocks[g] - columns[k] * rows[k]
                for m, h in heads[k].items():
                    columns[m] = columns[m] - columns[k] * h
    inverse = []
    for g in range(groups):
        diagonal = jnp.sum(
            jnp.where(lane == sub + g * ROWS, blocks[g], 0.0), axis=1, keepdims=True
        )
        inverse.append(blocks[g][:, rank:] / jnp.sqrt(diagonal))
    inverse = jnp.concatenate(inverse, axis=0)
    grams = ext_ref.shape[0] - ROWS
    solve = inverse * ext_ref[grams : grams + 1, :1] * (1.0 / (replicas * SHRINK))
    s1, s2, s3 = split(solve)
    solve_ref[...] = jnp.concatenate([s1, s1, s2, s2, s1, s3], axis=1)
    hat = jnp.dot(inverse, p_ref[...], precision=HIGHEST, preferred_element_type=F32)
    hat_ref[...] = hat
    left_ref[...] = hat.T.astype(BF16)


def factor(ext, p_mean, replicas):
    rank, rows = p_mean.shape
    return pl.pallas_call(
        functools.partial(factor_kernel, replicas),
        out_shape=[
            jax.ShapeDtypeStruct((rank, 6 * rank), BF16),
            jax.ShapeDtypeStruct((rows, rank), BF16),
            jax.ShapeDtypeStruct((rank, rows), F32),
        ],
        in_specs=[WHOLE] * 2,
        out_specs=[WHOLE] * 3,
        compiler_params=params(8),
        cost_estimate=cost(1 << 32, 1 << 20),
        name="factor",
    )(ext, p_mean)


def result_kernel(sources, more, width, solve_ref, left_ref, m_ref, *refs):
    refs, (error_ref, q_ref, sems) = refs[:-3], refs[-3:]
    if more == "hat":
        hat = pltpu.make_async_copy(refs[len(sources)], refs[-1], sems.at[0, len(sources)])
        hat.start()
    if more == "token":
        refs[-1][...] = jnp.zeros_like(refs[-1])
    error_hbm, q_hbm = refs[-3:-1] if more else refs[-2:]
    rank = solve_ref.shape[0]
    columns = q_ref.shape[2]
    left = left_ref[...]
    solve = solve_ref[...]

    def copies(n, base, at, size):
        to, here = pl.ds(pl.multiple_of(base + at, 128), size), pl.ds(at, size)
        return (
            pltpu.make_async_copy(error_ref.at[n, :, here], error_hbm.at[:, to], sems.at[0, n]),
            pltpu.make_async_copy(q_ref.at[n, :, here], q_hbm.at[:, to], sems.at[1, n]),
        )

    bases = []
    for n, (own, k) in enumerate(sources):
        t_ref = refs[n]
        half, turn, _ = place() if own else other_place()
        quarter = (turn + QUARTERS - k) % QUARTERS
        base = (half * QUARTERS + quarter) * columns
        bases.append(base)
        for at in range(0, columns, width):
            t = jnp.concatenate(
                [
                    jnp.concatenate(
                        [
                            t_ref[(g * columns + i) // 128 * ROWS : (g * columns + i) // 128 * ROWS + ROWS, :]
                            for i in range(at, at + width, 128)
                        ],
                        axis=1,
                    )
                    for g in range(rank // ROWS)
                ],
                axis=0,
            )
            t1, t2, t3 = split(t)
            t = jnp.concatenate([t1, t2, t1, t2, t3, t1], axis=0)
            new = jnp.dot(solve, t, preferred_element_type=F32)
            q_ref[n, :, at : at + width] = new
            decoded = jnp.dot(left, new.astype(BF16), preferred_element_type=F32)
            m = m_ref[:, pl.ds(pl.multiple_of(base + at, 128), width)]
            error_ref[n, :, at : at + width] = (m.astype(F32) - decoded).astype(BF16)
            for c in copies(n, base, at, width):
                c.start()
    for n, base in enumerate(bases):
        for c in copies(n, base, 0, columns):
            c.wait()
    if more == "hat":
        hat.wait()


def result(sources, totals, merged, solve, left, before, p_hat=None, token=False):
    rank = solve.shape[0]
    rows, columns = merged.shape
    quarter = columns // 2 // QUARTERS
    n = len(sources)
    held = [] if before is None else list(before)
    last = [] if p_hat is None else [p_hat]
    more = "hat" if last else "token" if token else ""
    return pl.pallas_call(
        functools.partial(result_kernel, sources, more, quarter // 2),
        out_shape=[pltpu.HBM((rows, columns), BF16), pltpu.HBM((rank, columns), F32)]
        + [pltpu.HBM(a.shape, F32) for a in last]
        + [pltpu.VMEM((ROWS, 128), F32)] * token,
        in_specs=[WHOLE] * (3 + n + len(last)) + [ANY] * len(held),
        out_specs=[ANY, ANY] + [ANY] * len(last) + [WHOLE] * token,
        scratch_shapes=[
            pltpu.VMEM((n, rows, quarter), BF16),
            pltpu.VMEM((n, rank, quarter), F32),
            pltpu.SemaphoreType.DMA((2, n + 1)),
        ],
        input_output_aliases={3 + n + len(last) + i: i for i in range(len(held))},
        compiler_params=params(12),
        cost_estimate=cost(1 << 33, 1 << 20),
        name="result",
    )(solve, left, merged, *totals, *last, *held)


def again_kernel(value_ref, out_ref):
    out_ref[...] = value_ref[...]


def again(value):
    return pl.pallas_call(
        again_kernel,
        out_shape=jax.ShapeDtypeStruct(value.shape, value.dtype),
        in_specs=[WHOLE],
        out_specs=WHOLE,
        compiler_params=params(4),
        cost_estimate=cost(RIGHT, 1 << 20),
        name="again",
    )(value)


def tie_kernel(value_ref, after_ref, out_ref):
    del value_ref, after_ref, out_ref


def tie(value, after):
    return pl.pallas_call(
        tie_kernel,
        out_shape=jax.ShapeDtypeStruct(value.shape, value.dtype),
        in_specs=[ANY] * 2,
        out_specs=ANY,
        input_output_aliases={0: 0},
        compiler_params=params(4),
        name="tie",
    )(value, after)


def body(gradient, error, q_start):
    rank = q_start.shape[0]
    replicas = SIZES[0] * SIZES[1]
    merged, p = merge(gradient[0], error[0], q_start)
    a, b, c = ring([p] * 3, 0, orders=("xz", "zx"), group=core_of)
    p = (p + a) + (b + c)
    sent, ext, p_mean, pieces = first_right(
        (2,), (p, *ring([p] * 3, 1, orders=("xz", "zx"), group=core_of)), merged, rank, replicas
    )
    got = swap(sent)
    sent = next_right(False, (1, 3, 0), pieces, merged, ext)
    got_next = swap(sent)
    kept = next_right(True, (2,), pieces, merged, sent)
    two, ext, weight = first_pair(kept, got, ext)
    (two,) = ring((two,), 0, (2,))
    kept = next_right(True, (1, 3, 0), pieces, merged, weight)
    *near, own = next_pair(kept, got_next, weight)
    own, *sent = add_quarters((own, *ring(near, 0, (1, 3)), two), ext)
    extra = ext.shape[0]
    (part,) = across(1, (own, *ring(sent, 1)), extra, True)
    total, ext = across(0, (part, *ring([part] * 3, 2)), extra, False)
    solve, left, p_hat = factor(ext, p_mean, replicas)
    total = assemble((total, *ring([total] * 3, 1)), solve)
    two, one, three = ring([total] * 3, 0, (2, 1, 3))

    def write(sources, totals, *after, **more):
        return result(sources, totals, merged, solve, left, *after, **more)

    own, other = True, False
    total = again(total)
    out = write(((own, 0),), (total,), None)
    *out, token = write(((other, 0),), (swap(total),), out, token=True)
    two = tie(two, token)
    out = write(((own, 2),), (two,), out)
    *out, token = write(((other, 2),), (swap(two),), out, token=True)
    one, three = tie(one, token), tie(three, token)
    out = write(((own, 1), (own, 3)), (one, three), out)
    new_error, q_new, p_hat = write(
        ((other, 1), (other, 3)), (swap(one), swap(three)), out, p_hat
    )
    return (new_error[None], p_hat, q_new)


def solution(mesh):
    fine = Mesh(mesh.devices.reshape(SIZES), AXES)
    return jax.shard_map(
        body,
        mesh=fine,
        in_specs=(P(DP, ("y", "c"), None), P(DP, ("y", "c"), None), P()),
        out_specs=(P(DP, ("y", "c"), None), P(None, ("y", "c")), P()),
        check_vma=False,
    )
```

```python
import functools

import jax
import jax.numpy as jnp
from jax import lax
from jax.experimental import pallas as pl
from jax.experimental.pallas import tpu as pltpu
from jax.sharding import Mesh, PartitionSpec as P

DP = ("z", "x")
AXES = ("z", "x", "y", "c")
SIZES = (4, 4, 4, 2)
HIGHEST = lax.Precision.HIGHEST
F32 = jnp.float32
BF16 = jnp.bfloat16
MIB = 1 << 20
ROWS = 8
QUARTERS = 4
SHRINK = 2.0**-16
RIGHT = 1 << 33
SHIFTS = (1, 3, 2)
ANY = pl.BlockSpec(memory_space=pl.ANY)
WHOLE = pl.BlockSpec(memory_space=pltpu.VMEM)


def params(mib):
    return pltpu.CompilerParams(vmem_limit_bytes=mib * MIB)


def cost(flops, nbytes):
    return pl.CostEstimate(flops=flops, bytes_accessed=nbytes, transcendentals=0)


def half_of(x, y, z, c):
    return c


def core_of(x, y, z, c):
    return c


def place():
    x, y, z, c = (lax.axis_index(a) for a in ("x", "y", "z", "c"))
    half = half_of(x, y, z, c)
    return half, jnp.where(half == 0, x, z), jnp.where(half == 0, z, y)


def other_place():
    x, y, z, c = (lax.axis_index(a) for a in ("x", "y", "z", "c"))
    half = 1 - half_of(x, y, z, c)
    return half, jnp.where(half == 0, x, z), jnp.where(half == 0, z, y)


def index(z, x, y, c):
    return ((z * SIZES[1] + x) * SIZES[2] + y) * SIZES[3] + c


def everyone():
    return [
        (z, x, y, c)
        for z in range(SIZES[0])
        for x in range(SIZES[1])
        for y in range(SIZES[2])
        for c in range(SIZES[3])
    ]


def ring(values, phase, shifts=SHIFTS, orders=("xzy", "zyx"), group=half_of):
    out = []
    for k, value in zip(shifts, values):
        pairs = []
        for z, x, y, c in everyone():
            to = {"z": z, "x": x, "y": y}
            axis = orders[group(x, y, z, c)][phase]
            to[axis] = (to[axis] + k) % SIZES[AXES.index(axis)]
            core = c
            pairs.append((index(z, x, y, c), index(*to.values(), core)))
        out.append(lax.ppermute(value, AXES, pairs))
    return out


def swap(value):
    return lax.ppermute(value, "c", [(0, 1), (1, 0)])


def merge_kernel(cuts, g_hbm, e_hbm, q_hbm, m_ref, p_ref, g_ref, e_ref, q_ref, sems):
    rows = g_ref.shape[0]
    rank = q_ref.shape[0]

    def copies(i):
        at = pl.ds(cuts[i], cuts[i + 1] - cuts[i])
        return [
            pltpu.make_async_copy(src.at[:, at], dst.at[:, at], sems.at[n, i])
            for n, (src, dst) in enumerate(((g_hbm, g_ref), (e_hbm, e_ref), (q_hbm, q_ref)))
        ]

    for i in range(len(cuts) - 1):
        for c in copies(i):
            c.start()
    acc = jnp.zeros((rows, rank), F32)
    for i in range(len(cuts) - 1):
        for c in copies(i):
            c.wait()
        at = pl.ds(cuts[i], cuts[i + 1] - cuts[i])
        m = (g_ref[:, at].astype(F32) + e_ref[:, at].astype(F32)).astype(BF16)
        m_ref[:, at] = m
        acc = acc + lax.dot_general(
            m, q_ref[:, at], (((1,), (1,)), ((), ())), preferred_element_type=F32
        )
    p_ref[...] = pack(acc.T)


def pack(p):
    rank, rows = p.shape
    full = rows // 128
    half = rank // 2
    parts = [p[:, i * 128 : (i + 1) * 128] for i in range(full)]
    rest = p[:, full * 128 :]
    return jnp.concatenate(parts + [jnp.concatenate([rest[:half], rest[half:]], axis=1)], axis=0)


def unpack(packed, rank):
    full = packed.shape[0] // rank
    last = packed[full * rank :]
    rest = jnp.concatenate([last[:, :64], last[:, 64:]], axis=0)
    return jnp.concatenate(
        [packed[i * rank : (i + 1) * rank] for i in range(full)] + [rest], axis=1
    )


def merge(gradient, error, q_start):
    rows, columns = gradient.shape
    rank = q_start.shape[0]
    step = columns // 20
    cuts = [n * step for n in (0, 2, 4, 6, 8, 10, 12, 14, 16, 18, 19, 20)]
    gradient, error, q_start = (
        pltpu.with_memory_space_constraint(a, pltpu.HBM) for a in (gradient, error, q_start)
    )
    return pl.pallas_call(
        functools.partial(merge_kernel, cuts),
        out_shape=[pltpu.VMEM((rows, columns), BF16), pltpu.VMEM((rank * rows // 128, 128), F32)],
        in_specs=[ANY, ANY, ANY],
        out_specs=[WHOLE, WHOLE],
        scratch_shapes=[
            pltpu.VMEM((rows, columns), BF16),
            pltpu.VMEM((rows, columns), BF16),
            pltpu.VMEM((rank, columns), BF16),
            pltpu.SemaphoreType.DMA((3, len(cuts) - 1)),
        ],
        compiler_params=params(24),
        cost_estimate=cost(2 * rank * rows * columns, 4 * rows * columns),
        name="merge",
    )(gradient, error, q_start)


def right_tiles(quarters, pieces, m_ref, out_ref):
    rank = pieces.shape[0] // 3
    width = m_ref.shape[1] // 2 // QUARTERS
    main = pieces.shape[1] // 256 * 256
    rest = jnp.concatenate(
        [pieces[i : i + rank, main:] for i in range(0, 3 * rank, rank)], axis=1
    )
    to = 0
    for quarter in quarters:
        at = pl.multiple_of(quarter * width, width)
        m = m_ref[:, pl.ds(at, width)]
        t = jnp.dot(pieces[:, :main], m[:main], preferred_element_type=F32)
        t = t[:rank] + (t[rank : 2 * rank] + t[2 * rank :])
        m = jnp.concatenate([m[main:]] * 3, axis=0)
        t = t + jnp.dot(rest, m, preferred_element_type=F32)
        for g in range(rank // ROWS):
            for n in range(width // 128):
                out_ref[to : to + ROWS, :] = t[g * ROWS : (g + 1) * ROWS, n * 128 : (n + 1) * 128]
                to += ROWS


def quarters_of(own, turns):
    half, turn, _ = place() if own else other_place()
    return [half * QUARTERS + (turn + k) % QUARTERS for k in turns]


def split(n):
    high = n.astype(BF16)
    n = n - high.astype(F32)
    middle = n.astype(BF16)
    return high, middle, (n - middle.astype(F32)).astype(BF16)


def first_right_kernel(replicas, rank, turns, a_ref, b_ref, c_ref, d_ref, m_ref, out_ref, ext_ref, p_ref, pieces_ref):
    p = (a_ref[...] + b_ref[...] + (c_ref[...] + d_ref[...])) * (1.0 / replicas)
    peak = jnp.max(jnp.abs(p), axis=(0, 1), keepdims=True)
    peak = jnp.where(peak > 0, peak, 1.0)
    p = unpack(p, rank)
    p_ref[...] = p
    pieces = jnp.concatenate(split(p / peak * SHRINK), axis=0)
    pieces_ref[...] = pieces
    right_tiles(quarters_of(False, turns), pieces, m_ref, out_ref)
    gram = lax.dot_general(
        p, p, (((1,), (1,)), ((), ())), precision=HIGHEST, preferred_element_type=F32
    )
    two = 2 * ROWS
    ext = jnp.concatenate(
        [
            jnp.concatenate([gram[i : i + ROWS], gram[i + ROWS : i + two]], axis=1)
            for i in range(0, rank, two)
        ]
        + [jnp.broadcast_to(peak, (ROWS, 128))],
        axis=0,
    )
    ext_ref[...] = ext
    out_ref[out_ref.shape[0] - ext.shape[0] :, :] = ext


def next_right_kernel(own, turns, pieces_ref, m_ref, after_ref, out_ref):
    del after_ref
    right_tiles(quarters_of(own, turns), pieces_ref[...], m_ref, out_ref)


def first_right(turns, parts, merged, rank, replicas):
    rows, columns = merged.shape
    size = rank * columns // 1024
    extra = rank * rank // 128 + ROWS
    return pl.pallas_call(
        functools.partial(first_right_kernel, replicas, rank, turns),
        out_shape=[
            jax.ShapeDtypeStruct((size + extra, 128), F32),
            pltpu.VMEM((extra, 128), F32),
            pltpu.VMEM((rank, rows), F32),
            pltpu.VMEM((3 * rank, rows), BF16),
        ],
        in_specs=[WHOLE] * 5,
        out_specs=[WHOLE] * 4,
        compiler_params=params(12),
        cost_estimate=cost(RIGHT, 1 << 20),
        name="first_right",
    )(*parts, merged)


def next_right(own, turns, pieces, merged, after):
    size = pieces.shape[0] // 3 * merged.shape[1] // 1024 * len(turns)
    return pl.pallas_call(
        functools.partial(next_right_kernel, own, turns),
        out_shape=jax.ShapeDtypeStruct((size, 128), F32),
        in_specs=[WHOLE, WHOLE, ANY],
        out_specs=WHOLE,
        compiler_params=params(12),
        cost_estimate=cost(RIGHT, 1 << 20),
        name="next_right",
    )(pieces, merged, after)


def first_pair_kernel(kept_ref, got_ref, ext_ref, out_ref, pair_ref, weight_ref):
    grams = ext_ref.shape[0] - ROWS
    size = kept_ref.shape[0]
    own, its = ext_ref[grams : grams + 1, :1], got_ref[size + grams : size + grams + 1, :1]
    top = jnp.maximum(own, its)
    pair_ref[:grams] = ext_ref[:grams] + got_ref[size : size + grams]
    pair_ref[grams:] = jnp.broadcast_to(top, (ROWS, 128))
    own, its = own / top, its / top
    weight_ref[:ROWS] = jnp.broadcast_to(own, (ROWS, 128))
    weight_ref[ROWS:] = jnp.broadcast_to(its, (ROWS, 128))
    out_ref[...] = kept_ref[...] * own + got_ref[:size] * its


def first_pair(kept, got, ext):
    return pl.pallas_call(
        first_pair_kernel,
        out_shape=[
            jax.ShapeDtypeStruct(kept.shape, F32),
            pltpu.VMEM(ext.shape, F32),
            pltpu.VMEM((2 * ROWS, 128), F32),
        ],
        in_specs=[WHOLE] * 3,
        out_specs=[WHOLE] * 3,
        compiler_params=params(8),
        name="first_pair",
    )(kept, got, ext)


def next_pair_kernel(kept_ref, got_ref, weight_ref, *out):
    own, its = weight_ref[:1, :1], weight_ref[ROWS : ROWS + 1, :1]
    size = out[0].shape[0]
    for n, ref in enumerate(out):
        at = slice(n * size, (n + 1) * size)
        ref[...] = kept_ref[at] * own + got_ref[at] * its


def next_pair(kept, got, weight):
    size = kept.shape[0] // 3
    return pl.pallas_call(
        next_pair_kernel,
        out_shape=[jax.ShapeDtypeStruct((size, 128), F32)] * 3,
        in_specs=[WHOLE] * 3,
        out_specs=[WHOLE] * 3,
        compiler_params=params(8),
        name="next_pair",
    )(kept, got, weight)


def add_quarters_kernel(a_ref, b_ref, c_ref, d_ref, ext_ref, *out):
    size = a_ref.shape[0] // QUARTERS
    for k, ref in zip((0,) + SHIFTS, out):
        at = pl.ds(pl.multiple_of((place()[2] + k) % QUARTERS * size, size), size)
        ref[:size] = (a_ref[at] + b_ref[at]) + (c_ref[at] + d_ref[at])
        ref[size:] = ext_ref[...]


def add_quarters(parts, ext):
    size = parts[0].shape[0] // QUARTERS
    return pl.pallas_call(
        add_quarters_kernel,
        out_shape=[jax.ShapeDtypeStruct((size + ext.shape[0], 128), F32)] * QUARTERS,
        in_specs=[WHOLE] * (QUARTERS + 1),
        out_specs=[WHOLE] * QUARTERS,
        compiler_params=params(8),
        name="add_quarters",
    )(*parts, ext)


def across_kernel(half_along_y, extra, a_ref, b_ref, c_ref, d_ref, out_ref, *ext_ref):
    grams = extra - ROWS
    size = a_ref.shape[0] - extra
    refs = (a_ref, b_ref, c_ref, d_ref)
    peaks = [r[size + grams : size + grams + 1, :1] for r in refs]
    top = jnp.maximum(jnp.maximum(peaks[0], peaks[1]), jnp.maximum(peaks[2], peaks[3]))
    a, b, c, d = (r[:size] * (k / top) for r, k in zip(refs, peaks))
    out_ref[:size] = (a + b) + (c + d)
    a, b, c, d = (r[size : size + grams] for r in refs)
    gram = jnp.where(place()[0] == half_along_y, (a + b) + (c + d), a)
    ext = out_ref.at[size:] if not ext_ref else ext_ref[0]
    ext[:grams] = gram
    ext[grams:] = jnp.broadcast_to(top, (ROWS, 128))


def across(half_along_y, parts, extra, keep):
    rows = parts[0].shape[0]
    out = [jax.ShapeDtypeStruct((rows, 128), F32)]
    if not keep:
        out = [jax.ShapeDtypeStruct((rows - extra, 128), F32), pltpu.VMEM((extra, 128), F32)]
    return pl.pallas_call(
        functools.partial(across_kernel, half_along_y, extra),
        out_shape=out,
        in_specs=[WHOLE] * 4,
        out_specs=[WHOLE] * len(out),
        compiler_params=params(8),
        name="across",
    )(*parts)


def assemble_kernel(a_ref, b_ref, c_ref, d_ref, after_ref, out_ref):
    del after_ref
    size = a_ref.shape[0]
    for k, ref in zip((0,) + SHIFTS, (a_ref, b_ref, c_ref, d_ref)):
        at = pl.multiple_of((place()[2] + QUARTERS - k) % QUARTERS * size, size)
        out_ref[pl.ds(at, size)] = ref[...]


def assemble(parts, after):
    return pl.pallas_call(
        assemble_kernel,
        out_shape=jax.ShapeDtypeStruct((parts[0].shape[0] * QUARTERS, 128), F32),
        in_specs=[WHOLE] * 4 + [ANY],
        out_specs=WHOLE,
        compiler_params=params(8),
        name="assemble",
    )(*parts, after)


def factor_kernel(replicas, ext_ref, p_ref, solve_ref, left_ref, hat_ref):
    rank = p_ref.shape[0]
    groups = rank // ROWS
    sub = lax.broadcasted_iota(jnp.int32, (ROWS, 2 * rank), 0)
    lane = lax.broadcasted_iota(jnp.int32, (ROWS, 2 * rank), 1)
    blocks = []
    for g in range(groups):
        tile = ext_ref[g // 2 * ROWS : (g // 2 + 1) * ROWS, (g % 2) * rank : (g % 2 + 1) * rank]
        unit = jnp.where(lane[:, :rank] == sub[:, :rank] + g * ROWS, 1.0, 0.0)
        blocks.append(jnp.concatenate([tile, unit], axis=1))
    for own in range(groups):
        spread = lambda g: [
            jnp.broadcast_to(blocks[g][:, own * ROWS + k : own * ROWS + k + 1], (ROWS, 2 * rank))
            for k in range(ROWS)
        ]
        columns = spread(own)
        rows, heads = [], []
        for k in range(ROWS):
            scale = 1.0 / columns[k][k : k + 1]
            row = blocks[own][k : k + 1] * scale
            head = {m: columns[m][k : k + 1] * scale for m in range(k + 1, ROWS)}
            factors = jnp.where(sub > k, columns[k], 0.0)
            blocks[own] = blocks[own] - factors * row
            for m, h in head.items():
                columns[m] = columns[m] - factors * h
            rows.append(row)
            heads.append(head)
        for g in range(own + 1, groups):
            columns = spread(g)
            for k in range(ROWS):
                blocks[g] = blocks[g] - columns[k] * rows[k]
                for m, h in heads[k].items():
                    columns[m] = columns[m] - columns[k] * h
    inverse = []
    for g in range(groups):
        diagonal = jnp.sum(
            jnp.where(lane == sub + g * ROWS, blocks[g], 0.0), axis=1, keepdims=True
        )
        inverse.append(blocks[g][:, rank:] / jnp.sqrt(diagonal))
    inverse = jnp.concatenate(inverse, axis=0)
    grams = ext_ref.shape[0] - ROWS
    solve = inverse * ext_ref[grams : grams + 1, :1] * (1.0 / (replicas * SHRINK))
    s1, s2, s3 = split(solve)
    solve_ref[...] = jnp.concatenate([s1, s1, s2, s2, s1, s3], axis=1)
    hat = jnp.dot(inverse, p_ref[...], precision=HIGHEST, preferred_element_type=F32)
    hat_ref[...] = hat
    left_ref[...] = hat.T.astype(BF16)


def factor(ext, p_mean, replicas):
    rank, rows = p_mean.shape
    return pl.pallas_call(
        functools.partial(factor_kernel, replicas),
        out_shape=[
            jax.ShapeDtypeStruct((rank, 6 * rank), BF16),
            jax.ShapeDtypeStruct((rows, rank), BF16),
            jax.ShapeDtypeStruct((rank, rows), F32),
        ],
        in_specs=[WHOLE] * 2,
        out_specs=[WHOLE] * 3,
        compiler_params=params(8),
        cost_estimate=cost(1 << 32, 1 << 20),
        name="factor",
    )(ext, p_mean)


def result_kernel(sources, more, width, solve_ref, left_ref, m_ref, *refs):
    refs, (error_ref, q_ref, sems) = refs[:-3], refs[-3:]
    if more == "hat":
        hat = pltpu.make_async_copy(refs[len(sources)], refs[-1], sems.at[0, len(sources)])
        hat.start()
    if more == "token":
        refs[-1][...] = jnp.zeros_like(refs[-1])
    error_hbm, q_hbm = refs[-3:-1] if more else refs[-2:]
    rank = solve_ref.shape[0]
    columns = q_ref.shape[2]
    left = left_ref[...]
    solve = solve_ref[...]

    def copies(n, base, at, size):
        to, here = pl.ds(pl.multiple_of(base + at, 128), size), pl.ds(at, size)
        return (
            pltpu.make_async_copy(error_ref.at[n, :, here], error_hbm.at[:, to], sems.at[0, n]),
            pltpu.make_async_copy(q_ref.at[n, :, here], q_hbm.at[:, to], sems.at[1, n]),
        )

    bases = []
    for n, (own, k) in enumerate(sources):
        t_ref = refs[n]
        half, turn, _ = place() if own else other_place()
        quarter = (turn + QUARTERS - k) % QUARTERS
        base = (half * QUARTERS + quarter) * columns
        bases.append(base)
        for at in range(0, columns, width):
            t = jnp.concatenate(
                [
                    jnp.concatenate(
                        [
                            t_ref[(g * columns + i) // 128 * ROWS : (g * columns + i) // 128 * ROWS + ROWS, :]
                            for i in range(at, at + width, 128)
                        ],
                        axis=1,
                    )
                    for g in range(rank // ROWS)
                ],
                axis=0,
            )
            t1, t2, t3 = split(t)
            t = jnp.concatenate([t1, t2, t1, t2, t3, t1], axis=0)
            new = jnp.dot(solve, t, preferred_element_type=F32)
            q_ref[n, :, at : at + width] = new
            decoded = jnp.dot(left, new.astype(BF16), preferred_element_type=F32)
            m = m_ref[:, pl.ds(pl.multiple_of(base + at, 128), width)]
            error_ref[n, :, at : at + width] = (m.astype(F32) - decoded).astype(BF16)
            for c in copies(n, base, at, width):
                c.start()
    for n, base in enumerate(bases):
        for c in copies(n, base, 0, columns):
            c.wait()
    if more == "hat":
        hat.wait()


def result(sources, totals, merged, solve, left, before, p_hat=None, token=False):
    rank = solve.shape[0]
    rows, columns = merged.shape
    quarter = columns // 2 // QUARTERS
    n = len(sources)
    held = [] if before is None else list(before)
    last = [] if p_hat is None else [p_hat]
    more = "hat" if last else "token" if token else ""
    return pl.pallas_call(
        functools.partial(result_kernel, sources, more, quarter // 2),
        out_shape=[pltpu.HBM((rows, columns), BF16), pltpu.HBM((rank, columns), F32)]
        + [pltpu.HBM(a.shape, F32) for a in last]
        + [pltpu.VMEM((ROWS, 128), F32)] * token,
        in_specs=[WHOLE] * (3 + n + len(last)) + [ANY] * len(held),
        out_specs=[ANY, ANY] + [ANY] * len(last) + [WHOLE] * token,
        scratch_shapes=[
            pltpu.VMEM((n, rows, quarter), BF16),
            pltpu.VMEM((n, rank, quarter), F32),
            pltpu.SemaphoreType.DMA((2, n + 1)),
        ],
        input_output_aliases={3 + n + len(last) + i: i for i in range(len(held))},
        compiler_params=params(12),
        cost_estimate=cost(1 << 33, 1 << 20),
        name="result",
    )(solve, left, merged, *totals, *last, *held)


def again_kernel(value_ref, out_ref):
    out_ref[...] = value_ref[...]


def again(value):
    return pl.pallas_call(
        again_kernel,
        out_shape=jax.ShapeDtypeStruct(value.shape, value.dtype),
        in_specs=[WHOLE],
        out_specs=WHOLE,
        compiler_params=params(4),
        cost_estimate=cost(RIGHT, 1 << 20),
        name="again",
    )(value)


def tie_kernel(value_ref, after_ref, out_ref):
    del value_ref, after_ref, out_ref


def tie(value, after):
    return pl.pallas_call(
        tie_kernel,
        out_shape=jax.ShapeDtypeStruct(value.shape, value.dtype),
        in_specs=[ANY] * 2,
        out_specs=ANY,
        input_output_aliases={0: 0},
        compiler_params=params(4),
        name="tie",
    )(value, after)


def body(gradient, error, q_start):
    rank = q_start.shape[0]
    replicas = SIZES[0] * SIZES[1]
    merged, p = merge(gradient[0], error[0], q_start)
    a, b, c = ring([p] * 3, 0, orders=("xz", "zx"), group=core_of)
    p = (p + a) + (b + c)
    sent, ext, p_mean, pieces = first_right(
        (2,), (p, *ring([p] * 3, 1, orders=("xz", "zx"), group=core_of)), merged, rank, replicas
    )
    got = swap(sent)
    sent = next_right(False, (1, 3, 0), pieces, merged, ext)
    got_next = swap(sent)
    kept = next_right(True, (2,), pieces, merged, sent)
    two, ext, weight = first_pair(kept, got, ext)
    (two,) = ring((two,), 0, (2,))
    kept = next_right(True, (1, 3, 0), pieces, merged, weight)
    *near, own = next_pair(kept, got_next, weight)
    own, *sent = add_quarters((own, *ring(near, 0, (1, 3)), two), ext)
    extra = ext.shape[0]
    (part,) = across(1, (own, *ring(sent, 1)), extra, True)
    total, ext = across(0, (part, *ring([part] * 3, 2)), extra, False)
    solve, left, p_hat = factor(ext, p_mean, replicas)
    total = assemble((total, *ring([total] * 3, 1)), solve)
    two, one, three = ring([total] * 3, 0, (2, 1, 3))

    def write(sources, totals, *after, **more):
        return result(sources, totals, merged, solve, left, *after, **more)

    own, other = True, False
    total = again(total)
    out = write(((own, 0),), (total,), None)
    *out, token = write(((other, 0),), (swap(total),), out, token=True)
    two = tie(two, token)
    out = write(((own, 2),), (two,), out)
    *out, token = write(((other, 2),), (swap(two),), out, token=True)
    one, three = tie(one, token), tie(three, token)
    out = write(((own, 1), (own, 3)), (one, three), out)
    new_error, q_new, p_hat = write(
        ((other, 1), (other, 3)), (swap(one), swap(three)), out, p_hat
    )
    return (new_error[None], p_hat, q_new)


def solution(mesh):
    fine = Mesh(mesh.devices.reshape(SIZES), AXES)
    return jax.shard_map(
        body,
        mesh=fine,
        in_specs=(P(DP, ("y", "c"), None), P(DP, ("y", "c"), None), P()),
        out_specs=(P(DP, ("y", "c"), None), P(None, ("y", "c")), P()),
        check_vma=False,
    )
```
